32 devices in a mesh: shard: 4 (over y, x), rep: 8 (over z, core).
Axes of the slice: x: 2, y: 2, z: 4, core: 2. Of those that a mesh axis runs over, the one named last changes fastest.
Arguments:
- tokens: bfloat16 [8192, 2560], P(('shard', 'rep')), may hold values from -6 to 6
- segments: int32 [32, 256], P(('shard', 'rep')), may hold values from 0 to 3, never falling along the last dimension, each value on 1 to 128 neighbouring positions
- cotangent: bfloat16 [8192, 2560], P(('shard', 'rep')), may hold values from -6 to 6
- latent_proj: bfloat16 [2560, 1056], P('shard'), may hold values from -0.125 to 0.125
- query_up: bfloat16 [768, 3840], P('shard'), may hold values from -0.21875 to 0.21875
- keyval_up: bfloat16 [256, 5120], P('shard'), may hold values from -0.375 to 0.375
- out_proj: bfloat16 [2560, 2560], P('shard'), may hold values from -2.5 to 2.5
- gate_up: bfloat16 [2560, 12800], P('shard'), may hold values from -0.125 to 0.125
- down_proj: bfloat16 [6400, 2560], P('shard'), may hold values from -0.4375 to 0.4375
- norm_gains: bfloat16 [6144], P('shard'), may hold values from 0.5 to 1.5
- latent_mean: bfloat16 [2560, 1056], P(('shard', 'rep')), may hold values from -128 to 128
- query_mean: bfloat16 [768, 3840], P(('shard', 'rep')), may hold values from -32 to 32
- keyval_mean: bfloat16 [256, 5120], P(('shard', 'rep')), may hold values from -64 to 64
- outproj_mean: bfloat16 [2560, 2560], P(('shard', 'rep')), may hold values from -3.5 to 3.5
- gateup_mean: bfloat16 [2560, 12800], P(('shard', 'rep')), may hold values from -20 to 20
- down_mean: bfloat16 [6400, 2560], P(('shard', 'rep')), may hold values from -5 to 5
- gains_mean: bfloat16 [6144], P(('shard', 'rep')), may hold values from -96 to 96
- latent_square: bfloat16 [2560, 1056], P(('shard', 'rep')), may hold values from 1144 to 17920
- query_square: bfloat16 [768, 3840], P(('shard', 'rep')), may hold values from 77 to 1224
- keyval_square: bfloat16 [256, 5120], P(('shard', 'rep')), may hold values from 212 to 3440
- outproj_square: bfloat16 [2560, 2560], P(('shard', 'rep')), may hold values from 0.81640625 to 12.25
- gateup_square: bfloat16 [2560, 12800], P(('shard', 'rep')), may hold values from 27 to 408
- down_square: bfloat16 [6400, 2560], P(('shard', 'rep')), may hold values from 1.6328125 to 27.75
- gains_square: bfloat16 [6144], P(('shard', 'rep')), may hold values from 474 to 7776
Outputs:
- block_out: bfloat16 [8192, 2560], P(('shard', 'rep'))
- input_grad: float32 [8192, 2560], P(('shard', 'rep'))
- latent_updated: float32 [2560, 1056], P(('shard', 'rep'))
- latent_mean_next: float32 [2560, 1056], P(('shard', 'rep'))
- latent_square_next: float32 [2560, 1056], P(('shard', 'rep'))
- query_updated: float32 [768, 3840], P(('shard', 'rep'))
- query_mean_next: float32 [768, 3840], P(('shard', 'rep'))
- query_square_next: float32 [768, 3840], P(('shard', 'rep'))
- keyval_updated: float32 [256, 5120], P(('shard', 'rep'))
- keyval_mean_next: float32 [256, 5120], P(('shard', 'rep'))
- keyval_square_next: float32 [256, 5120], P(('shard', 'rep'))
- outproj_updated: float32 [2560, 2560], P(('shard', 'rep'))
- outproj_mean_next: float32 [2560, 2560], P(('shard', 'rep'))
- outproj_square_next: float32 [2560, 2560], P(('shard', 'rep'))
- gateup_updated: float32 [2560, 12800], P(('shard', 'rep'))
- gateup_mean_next: float32 [2560, 12800], P(('shard', 'rep'))
- gateup_square_next: float32 [2560, 12800], P(('shard', 'rep'))
- down_updated: float32 [6400, 2560], P(('shard', 'rep'))
- down_mean_next: float32 [6400, 2560], P(('shard', 'rep'))
- down_square_next: float32 [6400, 2560], P(('shard', 'rep'))
- gains_updated: float32 [6144], P(('shard', 'rep'))
- gains_mean_next: float32 [6144], P(('shard', 'rep'))
- gains_square_next: float32 [6144], P(('shard', 'rep'))
The draws below stay inside these ranges and needn't reach their ends.
Inputs may be any that keep to these rules, and one draw needn't show every extreme that they name: `segments`: never falling along a sequence.
All inputs are finite; a program needn't handle non-finite values.
Results may differ from the reference program's by a relative error of at most 0.033.
Values may be sent and summed in bfloat16 or wider, within the bound.
A program may use at most 512 MiB of HBM per device.

```python
import math
import jax
import jax.numpy as jnp
import numpy as np
from jax import lax

D = 2560
H = 40
HD = 64
RD = 32
QR = 768
KR = 256
FF = 6400
SEQ = 256
DOCS = 4
STEP = 10
SEQS = 32
TOKENS = 8192


def block_scale(rng, shape, cuts, smallest, largest):
    loudness = 1.0
    for dim, blocks in cuts:
        heights = jax.random.uniform(jax.random.fold_in(jax.random.fold_in(rng, 6), dim), (blocks,), jnp.float32, smallest / len(cuts), largest / len(cuts))
        loudness = loudness * jnp.repeat(jnp.exp(heights), shape[dim] // blocks).reshape((-1,) + (1,) * (len(shape) - 1 - dim))
    return loudness


def split_up(number_of, total, most, slope):
    weights = [(1 << 20) // math.isqrt(standing ** slope) + 1 for standing in range(2, number_of + 1)]
    surplus, counts = total - most - (number_of - 1), [1] * (number_of - 1)
    while surplus > 0:
        movable = [i for i in range(number_of - 1) if counts[i] < most]
        pool, remaining = sum([weights[i] for i in movable]), surplus
        for i in movable:
            extra = min(most - counts[i], max(1, remaining * weights[i] // pool), surplus)
            counts[i] = counts[i] + extra
            surplus = surplus - extra
    return np.array([most] + counts)


def ragged_sizes(rng, count, total, bound, lean):
    if count == 2:
        one = jax.random.randint(rng, (), max(1, total - bound), min(bound, total - 1) + 1)
        return jnp.stack([one, total - one])
    lengths = jnp.asarray(split_up(count, total, bound, lean), jnp.int32)
    couples = (count - 1) // 2
    source_of, sink = lengths[1:1 + 2 * couples:2], lengths[2:2 + 2 * couples:2]
    slack = jnp.minimum(source_of - 1, bound - sink)
    passed = jax.random.randint(jax.random.fold_in(rng, 1), (couples,), 0, 1 << 20) % (slack + 1)
    lengths = lengths.at[1:1 + 2 * couples:2].set(source_of - passed).at[2:2 + 2 * couples:2].set(sink + passed)
    return lengths[jax.random.permutation(jax.random.fold_in(rng, 2), count)]


def gaussian(own_key, extent, width, most, cuts=(), held_as=jnp.bfloat16):
    result = width * jax.random.normal(own_key, extent, jnp.float32)
    if cuts:
        result = result * block_scale(own_key, extent, cuts, -0.22, 0.18)
    return jnp.clip(result, -most, most).astype(held_as)


def setup_inputs(seed: int = 0) -> dict:
    key_of = jax.random.split(jax.random.key(seed), 25)
    return {
        "tokens": gaussian(key_of[0], (TOKENS, D), 1.0, 6.0, ((0, 32),)),
        "segments": jax.vmap(lambda own: jnp.searchsorted(jnp.cumsum(ragged_sizes(own, DOCS, SEQ, SEQ // 2, 1)), jnp.arange(SEQ), side="right"))(jax.random.split(key_of[1], SEQS)).reshape((SEQS, SEQ)).astype(jnp.int32),
        "cotangent": gaussian(key_of[2], (TOKENS, D), 1.0, 6.0, ((0, 32),)),
        "latent_proj": gaussian(key_of[3], (D, QR + KR + RD), D ** -0.5, 0.125, ((0, 4),)),
        "query_up": gaussian(key_of[4], (QR, H * (HD + RD)), QR ** -0.5, 0.21875, ((0, 4),)),
        "keyval_up": gaussian(key_of[5], (KR, 2 * H * HD), KR ** -0.5, 0.375, ((0, 4),)),
        "out_proj": gaussian(key_of[6], (H * HD, D), (max(H * HD // 512, 1)) ** -0.5, 2.5, ((0, 4),)),
        "gate_up": gaussian(key_of[7], (D, 2 * FF), D ** -0.5, 0.125, ((0, 4),)),
        "down_proj": gaussian(key_of[8], (FF, D), (max(FF // 32, 1)) ** -0.5, 0.4375, ((0, 4),)),
        "norm_gains": jnp.clip(1.0 + 0.1 * jax.random.normal(key_of[9], (2 * D + QR + KR,), jnp.float32), 0.5, 1.5).astype(jnp.bfloat16),
        "latent_mean": gaussian(key_of[10], (D, QR + KR + RD), (0.25 * TOKENS ** 0.5), 128.0, ((0, 32),)),
        "query_mean": gaussian(key_of[11], (QR, H * (HD + RD)), (0.066 * TOKENS ** 0.5), 32.0, ((0, 32),)),
        "keyval_mean": gaussian(key_of[12], (KR, 2 * H * HD), (0.11 * TOKENS ** 0.5), 64.0, ((0, 32),)),
        "outproj_mean": gaussian(key_of[13], (H * HD, D), (0.0066 * TOKENS ** 0.5), 3.5, ((0, 32),)),
        "gateup_mean": gaussian(key_of[14], (D, 2 * FF), (0.039 * TOKENS ** 0.5), 20.0, ((0, 32),)),
        "down_mean": gaussian(key_of[15], (FF, D), (0.01 * TOKENS ** 0.5), 5.0, ((0, 32),)),
        "gains_mean": gaussian(key_of[16], (2 * D + QR + KR,), (0.17 * TOKENS ** 0.5), 96.0, ((0, 32),)),
        "latent_square": jnp.clip(jnp.exp(math.log(17920.0) - 2.7513865 * jax.random.uniform(key_of[17], (D, QR + KR + RD), jnp.float32) ** block_scale(key_of[17], (D, QR + KR + RD), ((0, 32),), -0.2, 0.2)), 1144.0, 17920.0).astype(jnp.bfloat16),
        "query_square": jnp.clip(jnp.exp(math.log(1224.0) - 2.766074 * jax.random.uniform(key_of[18], (QR, H * (HD + RD)), jnp.float32) ** block_scale(key_of[18], (QR, H * (HD + RD)), ((0, 32),), -0.2, 0.2)), 77.0, 1224.0).astype(jnp.bfloat16),
        "keyval_square": jnp.clip(jnp.exp(math.log(3440.0) - 2.7866405 * jax.random.uniform(key_of[19], (KR, 2 * H * HD), jnp.float32) ** block_scale(key_of[19], (KR, 2 * H * HD), ((0, 32),), -0.2, 0.2)), 212.0, 3440.0).astype(jnp.bfloat16),
        "outproj_square": jnp.clip(jnp.exp(math.log(12.25) - 2.708369 * jax.random.uniform(key_of[20], (H * HD, D), jnp.float32) ** block_scale(key_of[20], (H * HD, D), ((0, 32),), -0.2, 0.2)), 0.81640625, 12.25).astype(jnp.bfloat16),
        "gateup_square": jnp.clip(jnp.exp(math.log(408.0) - 2.7154303 * jax.random.uniform(key_of[21], (D, 2 * FF), jnp.float32) ** block_scale(key_of[21], (D, 2 * FF), ((0, 32),), -0.2, 0.2)), 27.0, 408.0).astype(jnp.bfloat16),
        "down_square": jnp.clip(jnp.exp(math.log(27.75) - 2.83293185 * jax.random.uniform(key_of[22], (FF, D), jnp.float32) ** block_scale(key_of[22], (FF, D), ((0, 32),), -0.2, 0.2)), 1.6328125, 27.75).astype(jnp.bfloat16),
        "gains_square": jnp.clip(jnp.exp(math.log(7776.0) - 2.79759 * jax.random.uniform(key_of[23], (2 * D + QR + KR,), jnp.float32) ** block_scale(key_of[23], (2 * D + QR + KR,), ((0, 32),), -0.2, 0.2)), 474.0, 7776.0).astype(jnp.bfloat16),
    }


@jax.custom_vjp
def low(v):
    return lax.optimization_barrier(v.astype(jnp.bfloat16)).astype(jnp.float32)

@jax.custom_vjp
def low_back(v):
    return v

def low_keep(v):
    return (low(v), None)

def low_pass(kept, grad):
    return (grad,)

def back_keep(v):
    return (v, None)

def back_low(kept, grad):
    return (low(grad),)
low.defvjp(low_keep, low_pass)
low_back.defvjp(back_keep, back_low)
norm_eps = 1e-05
residual_scale = 1.4 / math.sqrt(62.0)
beta_one = 0.9
beta_two = 0.95
adam_eps = 1e-08
decay_rate = 0.1
gain_rate = 0.8

def inverse_rms(values):
    return lax.rsqrt(lax.optimization_barrier(jnp.mean(values * values, axis=-1, keepdims=True)) + norm_eps)

def rotate(values, cos_table, sin_table):
    half_width = values.shape[-1] // 2
    first_half = values[..., :half_width]
    second_half = values[..., half_width:]
    return jnp.concatenate([first_half * cos_table - second_half * sin_table, second_half * cos_table + first_half * sin_table], axis=-1)

def position_tables(segment_row):
    position_index = jnp.arange(segment_row.shape[0])
    same_doc = segment_row[None, :] == segment_row[:, None]
    earlier = position_index[None, :] < position_index[:, None]
    position = lax.optimization_barrier(jnp.sum(jnp.where(same_doc & earlier, 1.0, 0.0), axis=1)).astype(jnp.float32)
    frequency = 10000.0 ** (-jnp.arange(RD // 2).astype(jnp.float32) * 2.0 / RD)
    angles = position[:, None] * frequency[None, :]
    allowed = same_doc & (position_index[None, :] <= position_index[:, None])
    return (jnp.cos(angles), jnp.sin(angles), allowed)

def layer_one(rows_in, segment_row, params):
    latent_w, query_w, keyval_w, out_w, gateup_w, down_w, gains_all = params
    gain_in = gains_all[:D]
    gain_query = gains_all[D:D + QR]
    gain_keyval = gains_all[D + QR:D + QR + KR]
    gain_mlp = gains_all[D + QR + KR:]
    cos_table, sin_table, allowed = position_tables(segment_row)
    highest = lax.Precision.HIGHEST
    seq_len = rows_in.shape[0]
    normed_in = low(rows_in * inverse_rms(rows_in) * gain_in)
    latent_all = low_back(jnp.dot(normed_in, latent_w, precision=highest))
    query_lat = latent_all[:, :QR]
    keyval_lat = latent_all[:, QR:QR + KR]
    normed_query = low(query_lat * inverse_rms(query_lat) * gain_query)
    normed_keyval = low(keyval_lat * inverse_rms(keyval_lat) * gain_keyval)
    query = low_back(jnp.dot(normed_query, query_w, precision=highest)).reshape(seq_len, H, HD + RD)
    keyval = low_back(jnp.dot(normed_keyval, keyval_w, precision=highest)).reshape(seq_len, H, 2 * HD)
    key_rope = rotate(latent_all[:, QR + KR:], cos_table, sin_table)
    query_heads = low(jnp.concatenate([query[:, :, :HD], rotate(query[:, :, HD:], cos_table[:, None, :], sin_table[:, None, :])], axis=2))
    key_heads = low(jnp.concatenate([keyval[:, :, :HD], jnp.broadcast_to(key_rope[:, None, :], (seq_len, H, RD))], axis=2))
    value_heads = low(keyval[:, :, HD:])
    scores = low_back(jnp.einsum('qhd,khd->hqk', query_heads, key_heads, precision=highest) * (HD + RD) ** (-0.5))
    masked = jnp.where(allowed[None], scores, -1e+30)
    row_max = lax.optimization_barrier(jnp.max(masked, axis=2, keepdims=True))
    exponent = jnp.exp(masked - row_max)
    attn_probs = low(exponent / lax.optimization_barrier(jnp.sum(exponent, axis=2, keepdims=True)))
    mixed_heads = low(low_back(jnp.einsum('hqk,khd->qhd', attn_probs, value_heads, precision=highest))).reshape(seq_len, H * HD)
    hidden = rows_in + residual_scale * low_back(jnp.dot(mixed_heads, out_w, precision=highest))
    normed_mlp = low(hidden * inverse_rms(hidden) * gain_mlp)
    gate_up_rows = low_back(jnp.dot(normed_mlp, gateup_w, precision=highest))
    activation = low(jax.nn.silu(gate_up_rows[:, :FF]) * gate_up_rows[:, FF:])
    return hidden + residual_scale * low_back(jnp.dot(activation, down_w, precision=highest))

def add_pair(total_one, total_two):
    return total_one + total_two

def adam_step(weight, gradient, mean_old, square_old, step_rate, decay_factor):
    mean_new = beta_one * mean_old.astype(jnp.float32) + (1.0 - beta_one) * gradient
    square_new = beta_two * square_old.astype(jnp.float32) + (1.0 - beta_two) * gradient * gradient
    ratio = mean_new / (1.0 - beta_one ** STEP) / (jnp.sqrt(square_new / (1.0 - beta_two ** STEP)) + adam_eps)
    updated = weight - step_rate * (ratio + decay_factor * weight)
    return (updated, mean_new, square_new)

def reference(tokens, segments, cotangent, latent_proj, query_up, keyval_up, out_proj, gate_up, down_proj, norm_gains, latent_mean, query_mean, keyval_mean, outproj_mean, gateup_mean, down_mean, gains_mean, latent_square, query_square, keyval_square, outproj_square, gateup_square, down_square, gains_square):
    weights = tuple((array_in.astype(jnp.float32) for array_in in (latent_proj, query_up, keyval_up, out_proj, gate_up, down_proj, norm_gains)))
    group_size = math.gcd(SEQS, max(1, 2048 // SEQ))
    count_groups = SEQS // group_size
    rows_all = tokens.astype(jnp.float32).reshape(count_groups, group_size, SEQ, D)
    segs_all = segments.reshape(count_groups, group_size, SEQ)
    cot_all = cotangent.astype(jnp.float32).reshape(count_groups, group_size, SEQ, D)

    def scan_step(totals, inputs):
        rows_group, seg_group, cot_group = inputs

        def run_group(rows_in, params):
            return jax.vmap(layer_one, in_axes=(0, 0, None))(rows_in, seg_group, params)
        out_rows, pull_back = jax.vjp(run_group, rows_group, weights)
        grad_rows, grad_weights = pull_back(cot_group)
        return (jax.tree.map(add_pair, totals, grad_weights), (out_rows.astype(jnp.bfloat16), grad_rows))
    zero_grads = tuple((jnp.zeros_like(array_in) for array_in in weights))
    summed, (out_blocks, grad_blocks) = lax.scan(scan_step, zero_grads, (rows_all, segs_all, cot_all))
    new_latent = adam_step(weights[0], summed[0], latent_mean, latent_square, D ** (-0.5), decay_rate)
    new_query = adam_step(weights[1], summed[1], query_mean, query_square, QR ** (-0.5), decay_rate)
    new_keyval = adam_step(weights[2], summed[2], keyval_mean, keyval_square, KR ** (-0.5), decay_rate)
    new_outproj = adam_step(weights[3], summed[3], outproj_mean, outproj_square, max(H * HD // 512, 1) ** (-0.5), decay_rate)
    new_gateup = adam_step(weights[4], summed[4], gateup_mean, gateup_square, D ** (-0.5), decay_rate)
    new_down = adam_step(weights[5], summed[5], down_mean, down_square, max(FF // 32, 1) ** (-0.5), decay_rate)
    new_gains = adam_step(weights[6], summed[6], gains_mean, gains_square, gain_rate, 0.0)
    return (out_blocks.reshape(TOKENS, D), grad_blocks.reshape(TOKENS, D), new_latent[0], new_latent[1], new_latent[2], new_query[0], new_query[1], new_query[2], new_keyval[0], new_keyval[1], new_keyval[2], new_outproj[0], new_outproj[1], new_outproj[2], new_gateup[0], new_gateup[1], new_gateup[2], new_down[0], new_down[1], new_down[2], new_gains[0], new_gains[1], new_gains[2])
```

```python
import functools
import math

import jax
import jax.numpy as jnp
from jax import lax
from jax.experimental import pallas as pl
from jax.experimental.pallas import tpu as pltpu
from jax.sharding import PartitionSpec as P

D = 2560
H = 40
HD = 64
RD = 32
QR = 768
KR = 256
FF = 6400
STEP = 10


norm_eps = 1e-05
residual_scale = 1.4 / math.sqrt(62.0)
beta_one = 0.9
beta_two = 0.95
adam_eps = 1e-08
decay_rate = 0.1
gain_rate = 0.8


def inverse_rms(values):
    return lax.rsqrt(jnp.mean(values * values, axis=-1, keepdims=True) + norm_eps)


def norm_back(incoming, operand, inv_scale):
    return inv_scale * (
        incoming
        - operand * inv_scale * inv_scale * jnp.mean(incoming * operand, axis=-1, keepdims=True)
    )


def rotation_rates():
    rates = [0.0] * LANES
    for i in range(RD // 2):
        rates[HD + i] = rates[HD + RD // 2 + i] = 10000.0 ** (-2.0 * i / RD)
    return jnp.array([rates], jnp.float32)


def own_rows(weight, gradient):
    count = gradient.shape[0]
    start = lax.axis_index("rep") * count
    return lax.dynamic_slice_in_dim(weight, start, count, 0)


def adam_step(weight, gradient, mean_old, square_old, step_rate, decay_factor):
    weight_f = own_rows(weight, gradient).astype(jnp.float32)
    gradient = gradient.astype(jnp.float32)
    mean_new = beta_one * mean_old.astype(jnp.float32) + (1.0 - beta_one) * gradient
    square_new = beta_two * square_old.astype(jnp.float32) + (1.0 - beta_two) * gradient * gradient
    ratio = (
        mean_new
        / (1.0 - beta_one**STEP)
        / (jnp.sqrt(square_new / (1.0 - beta_two**STEP)) + adam_eps)
    )
    updated = weight_f - step_rate * (ratio + decay_factor * weight_f)
    return (updated, mean_new, square_new)


TILE = 256
TAIL = 128
LANES = 128
LATENT = QR + KR + LANES
score_scale = (HD + RD) ** (-0.5)
VMEM_BYTES = 48 * 1024 * 1024


def across(a, b):
    return lax.dot_general(a, b, (((1,), (1,)), ((), ())), preferred_element_type=jnp.float32)


def along(a, b):
    return lax.dot_general(a, b, (((1,), (0,)), ((), ())), preferred_element_type=jnp.float32)


def mlp_kernel(group, tiles, tail, rows_d, order_ref, normed_ref, branch_ref, *refs):
    blocks = refs[:group]
    tails = refs[group : 2 * group]
    down_ref, down_tail_ref = refs[2 * group : 2 * group + 2]
    out_refs = refs[-9:]
    act_ref, grad_ref, sum_ref, back_ref, whole, whole_tail, down_wide, sum_acc, back_acc = out_refs
    step = pl.program_id(0)
    bf16 = jnp.bfloat16

    for j in range(group):
        start = pl.multiple_of(order_ref[j] * rows_d, 16)
        whole[pl.ds(start, rows_d), :] = blocks[j][...]

    def part(weights, down, width):
        both = along(normed_ref[...], weights)
        gate = both[:, :width]
        up = both[:, width:]
        sigmoid = 1.0 / (1.0 + jnp.exp(-gate))
        silu = gate * sigmoid
        act = (silu * up).astype(bf16)
        grad_act = across(branch_ref[...], down)
        grad_gate = grad_act * up * sigmoid * (1.0 + gate * (1.0 - sigmoid))
        grad_up = grad_act * silu
        grad = jnp.concatenate([grad_gate.astype(bf16), grad_up.astype(bf16)], axis=1)
        return act, grad, along(act, down), across(grad, weights)

    act, grad, term, back = part(whole[...], down_ref[...], TILE)
    first = pl.multiple_of(step * TILE, TILE)
    act_ref[:, pl.ds(first, TILE)] = act
    grad_ref[:, pl.ds(pl.multiple_of(2 * first, 2 * TILE), 2 * TILE)] = grad

    @pl.when(step == 0)
    def _():
        sum_acc[...] = term
        back_acc[...] = back

    @pl.when(step > 0)
    def _():
        sum_acc[...] += term
        back_acc[...] += back

    @pl.when(step == tiles - 1)
    def _():
        for j in range(group):
            start = pl.multiple_of(order_ref[j] * rows_d, 16)
            whole_tail[pl.ds(start, rows_d), :] = tails[j][...]
        down_wide[...] = jnp.zeros_like(down_wide)
        down_wide[:tail, :] = down_tail_ref[...]
        act, grad, term, back = part(whole_tail[...], down_wide[...], TAIL)
        act_ref[:, tiles * TILE :] = act
        grad_ref[:, 2 * tiles * TILE :] = grad
        sum_ref[...] = (sum_acc[...] + term).astype(bf16)
        back_ref[...] = (back_acc[...] + back).astype(bf16)


def mlp_part(order, normed, branch, own, gathered, down, earlier, index, group):
    tokens, width = normed.shape
    hidden = down.shape[0]
    tiles = hidden // TILE
    tail = hidden - tiles * TILE
    rows_d = width // group
    bf16 = jnp.bfloat16
    f32 = jnp.float32
    fixed = lambda t: (0, 0)
    weights = [own] + [gathered] * (group - 1)
    return pl.pallas_call(
        functools.partial(mlp_kernel, group, tiles, tail, rows_d),
        grid=(tiles,),
        in_specs=[
            pl.BlockSpec(memory_space=pltpu.SMEM),
            pl.BlockSpec((tokens, width), fixed),
            pl.BlockSpec((tokens, width), fixed),
        ]
        + [pl.BlockSpec((rows_d, 2 * TILE), lambda t: (0, t))]
        + [
            pl.BlockSpec((rows_d, 2 * TILE), lambda t, j=j: (0, j * tiles + t))
            for j in range(group - 1)
        ]
        + [pl.BlockSpec((rows_d, 2 * TAIL), lambda t: (0, tiles * TILE // TAIL))]
        + [
            pl.BlockSpec(
                (rows_d, 2 * TAIL), lambda t, j=j: (0, (group - 1) * tiles * TILE // TAIL + j)
            )
            for j in range(group - 1)
        ]
        + [
            pl.BlockSpec((TILE, width), lambda t: (t, 0)),
            pl.BlockSpec((tail, width), lambda t: (tiles * TILE // tail, 0)),
        ]
        + [pl.BlockSpec(memory_space=pl.ANY)] * len(earlier),
        out_specs=[
            pl.BlockSpec((tokens, tiles * TILE + TAIL), lambda t: (index, 0)),
            pl.BlockSpec((tokens, 2 * (tiles * TILE + TAIL)), lambda t: (index, 0)),
            pl.BlockSpec((tokens, width), fixed),
            pl.BlockSpec((tokens, width), fixed),
        ],
        out_shape=[
            jax.ShapeDtypeStruct((group * tokens, tiles * TILE + TAIL), bf16),
            jax.ShapeDtypeStruct((group * tokens, 2 * (tiles * TILE + TAIL)), bf16),
            jax.ShapeDtypeStruct((tokens, width), bf16),
            jax.ShapeDtypeStruct((tokens, width), bf16),
        ],
        scratch_shapes=[
            pltpu.VMEM((width, 2 * TILE), bf16),
            pltpu.VMEM((width, 2 * TAIL), bf16),
            pltpu.VMEM((TAIL, width), bf16),
            pltpu.VMEM((tokens, width), f32),
            pltpu.VMEM((tokens, width), f32),
        ],
        input_output_aliases={5 + 2 * group + i: i for i in range(len(earlier))},
        compiler_params=pltpu.CompilerParams(vmem_limit_bytes=VMEM_BYTES),
        cost_estimate=pl.CostEstimate(
            flops=12 * tokens * width * hidden,
            bytes_accessed=6 * width * hidden + 8 * tokens * width,
            transcendentals=tokens * hidden,
        ),
        name="mlp_part",
    )(order, normed, branch, *weights, *weights, down, down, *earlier)


def layer_kernel(group, base, tiles, tail, rows_d, shares, last, order_ref, *refs):
    normed_in = refs[:group]
    top_in = refs[group : 2 * group]
    at = 2 * group
    blocks = refs[at : at + group]
    at += group
    if last:
        tails = refs[at : at + group]
        at += group
        down_ref, down_tail_ref, act_old, acc_in = refs[at : at + 4]
        at += 4
    else:
        down_ref = refs[at]
        at += 1
    act_out, grad_out, back_out = refs[at : at + 3]
    normed, turned, branch, whole, acc, stage, act_stage, in_sems, out_sems, back_sem = refs[
        at + 3 : at + 13
    ]
    if last:
        whole_tail, down_wide, tail_stage, tail_act, tail_sems = refs[at + 13 :]
    bf16 = jnp.bfloat16
    f32 = jnp.float32
    step = pl.program_id(0)
    slot = lax.rem(step, 2)
    tokens = normed_in[0].shape[0]
    width = normed.shape[1]
    rows = rows_d // shares

    def arrivals():
        copies = []
        for j in range(group):
            copies.append(
                pltpu.make_async_copy(
                    normed_in[j], normed.at[pl.ds(j * tokens, tokens), :], in_sems.at[j]
                )
            )
            copies.append(
                pltpu.make_async_copy(
                    top_in[j], branch.at[pl.ds(j * tokens, tokens), :], in_sems.at[group + j]
                )
            )
        return copies

    @pl.when(step == 0)
    def _():
        copies = arrivals()
        for copy in copies:
            copy.start()
        if last:
            pltpu.make_async_copy(acc_in, acc, back_sem).start()
        else:
            acc[...] = jnp.zeros_like(acc)
        for j in range(group):
            at = pl.ds(j * tokens, tokens)
            copies[2 * j].wait()
            turned[:, j * tokens : (j + 1) * tokens] = normed[at, :].T
            copies[2 * j + 1].wait()
            branch[at, :] = (residual_scale * branch[at, :].astype(f32)).astype(bf16)
        if last:
            pltpu.make_async_copy(acc_in, acc, back_sem).wait()

    for j in range(group):
        start = pl.multiple_of(order_ref[j] * rows_d, 16)
        whole[pl.ds(start, rows_d), :] = blocks[j][...]

    def part(weights_ref, down, wide, act_to, grad_to):
        both = along(normed[...], weights_ref[...])
        gate = both[:, :wide]
        up = both[:, wide:]
        sigmoid = 1.0 / (1.0 + jnp.exp(-gate))
        silu = gate * sigmoid
        act_to[...] = (silu * up).astype(bf16)
        grad_act = across(branch[...], down)
        grad_gate = grad_act * up * sigmoid * (1.0 + gate * (1.0 - sigmoid))
        grad_up = grad_act * silu
        grad = jnp.concatenate([grad_gate.astype(bf16), grad_up.astype(bf16)], axis=1)
        cut = 512
        for c in range(width // cut):
            here = slice(c * cut, (c + 1) * cut)
            acc[:, here] += across(grad, weights_ref[here, :])
        for g in range(group):
            result = along(turned[g * rows_d : (g + 1) * rows_d, :], grad).astype(bf16)
            for r in range(shares):
                grad_to[r, g] = result[r * rows : (r + 1) * rows, :]

    def leaving(index, slot_index):
        first = pl.multiple_of((base + index) * TILE, TILE)
        return (
            pltpu.make_async_copy(
                act_stage.at[slot_index],
                act_out.at[:, pl.ds(first, TILE)],
                out_sems.at[0, slot_index],
            ),
            pltpu.make_async_copy(
                stage.at[slot_index],
                grad_out.at[:, :, :, pl.ds(pl.multiple_of(index * 2 * TILE, 2 * TILE), 2 * TILE)],
                out_sems.at[1, slot_index],
            ),
        )

    @pl.when(step >= 2)
    def _():
        for copy in leaving(step - 2, slot):
            copy.wait()

    part(whole, down_ref[...], TILE, act_stage.at[slot], stage.at[slot])
    for copy in leaving(step, slot):
        copy.start()

    @pl.when(step == tiles - 1)
    def _():
        if last:
            for j in range(group):
                start = pl.multiple_of(order_ref[j] * rows_d, 16)
                whole_tail[pl.ds(start, rows_d), :] = tails[j][...]
            down_wide[...] = jnp.zeros_like(down_wide)
            down_wide[:tail, :] = down_tail_ref[...]
            part(whole_tail, down_wide[...], TAIL, tail_act, tail_stage)
            final = [
                pltpu.make_async_copy(
                    tail_act, act_out.at[:, pl.ds((base + tiles) * TILE, TAIL)], tail_sems.at[0]
                ),
                pltpu.make_async_copy(
                    tail_stage,
                    grad_out.at[:, :, :, pl.ds(2 * tiles * TILE, 2 * TAIL)],
                    tail_sems.at[1],
                ),
            ]
            normed[...] = acc[...].astype(bf16)
            final.append(pltpu.make_async_copy(normed, back_out, back_sem))
        else:
            final = [pltpu.make_async_copy(acc, back_out, back_sem)]
        for copy in final:
            copy.start()
        for k in range(max(tiles - 2, 0), tiles):
            for copy in leaving(k, k % 2):
                copy.wait()
        for copy in final:
            copy.wait()


def layer_part(order, normed, top, own, gathered, down, earlier, tiles_from, tiles, group, shares):
    tokens, width = normed[0].shape
    hidden = down.shape[0]
    all_tiles = hidden // TILE
    tail = hidden - all_tiles * TILE
    rows_d = width // group
    rows = rows_d // shares
    bf16 = jnp.bfloat16
    f32 = jnp.float32
    last = earlier is not None
    total = group * tokens
    once = pl.Buffered(1)
    any_spec = pl.BlockSpec(memory_space=pl.ANY)
    weights = [own] + [gathered] * (group - 1)
    in_specs = [pl.BlockSpec(memory_space=pltpu.SMEM)] + [any_spec] * (2 * group)
    in_specs += [pl.BlockSpec((rows_d, 2 * TILE), lambda t: (0, tiles_from + t))]
    in_specs += [
        pl.BlockSpec((rows_d, 2 * TILE), lambda t, j=j: (0, j * all_tiles + tiles_from + t))
        for j in range(group - 1)
    ]
    inputs = [order] + normed + top + weights
    scratch = [
        pltpu.VMEM((total, width), bf16),
        pltpu.VMEM((width, total), bf16),
        pltpu.VMEM((total, width), bf16),
        pltpu.VMEM((width, 2 * TILE), bf16),
        pltpu.VMEM((total, width), f32),
        pltpu.VMEM((2, shares, group, rows, 2 * TILE), bf16),
        pltpu.VMEM((2, total, TILE), bf16),
        pltpu.SemaphoreType.DMA((2 * group,)),
        pltpu.SemaphoreType.DMA((2, 2)),
        pltpu.SemaphoreType.DMA,
    ]
    cols = 2 * tiles * TILE
    aliases = {}
    if last:
        first_tail = all_tiles * TILE // TAIL
        in_specs += [
            pl.BlockSpec((rows_d, 2 * TAIL), lambda t: (0, first_tail), pipeline_mode=once)
        ]
        in_specs += [
            pl.BlockSpec(
                (rows_d, 2 * TAIL),
                lambda t, j=j: (0, (group - 1) * first_tail + j),
                pipeline_mode=once,
            )
            for j in range(group - 1)
        ]
        inputs += weights
        cols += 2 * TAIL
    in_specs.append(pl.BlockSpec((TILE, width), lambda t: (tiles_from + t, 0)))
    inputs.append(down)
    if last:
        in_specs.append(
            pl.BlockSpec(
                (tail, width), lambda t: (all_tiles * TILE // tail, 0), pipeline_mode=once
            )
        )
        inputs.append(down)
        in_specs += [any_spec, any_spec]
        aliases = {len(inputs): 0}
        inputs += [earlier[0], earlier[2]]
        scratch += [
            pltpu.VMEM((width, 2 * TAIL), bf16),
            pltpu.VMEM((TAIL, width), bf16),
            pltpu.VMEM((shares, group, rows, 2 * TAIL), bf16),
            pltpu.VMEM((total, TAIL), bf16),
            pltpu.SemaphoreType.DMA((2,)),
        ]
    part_hidden = tiles * TILE + (tail if last else 0)
    return pl.pallas_call(
        functools.partial(
            layer_kernel, group, tiles_from, tiles, tail, rows_d, shares, last
        ),
        grid=(tiles,),
        in_specs=in_specs,
        out_specs=[any_spec] * 3,
        out_shape=[
            jax.ShapeDtypeStruct((total, all_tiles * TILE + TAIL), bf16),
            jax.ShapeDtypeStruct((shares, group, rows, cols), bf16),
            jax.ShapeDtypeStruct((total, width), bf16 if last else f32),
        ],
        scratch_shapes=scratch,
        input_output_aliases=aliases,
        compiler_params=pltpu.CompilerParams(vmem_limit_bytes=61 * 1024 * 1024),
        cost_estimate=pl.CostEstimate(
            flops=14 * total * width * part_hidden,
            bytes_accessed=12 * width * part_hidden + 16 * total * width,
            transcendentals=total * part_hidden,
        ),
        name="layer_part",
    )(*inputs)


def down_grad_kernel(group, tokens, act_ref, *refs):
    top = refs[:group]
    out_ref, whole = refs[group:]

    @pl.when(pl.program_id(0) == 0)
    def _():
        for j in range(group):
            whole[j * tokens : (j + 1) * tokens, :] = (
                residual_scale * top[j][...].astype(jnp.float32)
            ).astype(jnp.bfloat16)

    out_ref[...] = along(act_ref[...].T, whole[...]).astype(jnp.bfloat16)


def down_grad(act_all, top_parts, hidden, group):
    tokens, width = top_parts[0].shape
    tiles = (hidden + TILE - 1) // TILE
    return pl.pallas_call(
        functools.partial(down_grad_kernel, group, tokens),
        grid=(tiles,),
        in_specs=[pl.BlockSpec((group * tokens, TILE), lambda t: (0, t))]
        + [pl.BlockSpec((tokens, width), lambda t: (0, 0))] * group,
        out_specs=pl.BlockSpec((TILE, width), lambda t: (t, 0)),
        out_shape=jax.ShapeDtypeStruct((hidden, width), jnp.bfloat16),
        scratch_shapes=[pltpu.VMEM((group * tokens, width), jnp.bfloat16)],
        compiler_params=pltpu.CompilerParams(vmem_limit_bytes=VMEM_BYTES),
        cost_estimate=pl.CostEstimate(
            flops=2 * group * tokens * width * hidden,
            bytes_accessed=2 * width * hidden + 2 * group * tokens * (width + hidden),
            transcendentals=0,
        ),
        name="down_grad",
    )(act_all, *top_parts)


def lane_index(rows):
    return lax.broadcasted_iota(jnp.int32, (rows, LANES), 1)


def turn(values, table_ref, sign):
    ahead = pltpu.roll(values, LANES - RD // 2, 1)
    behind = pltpu.roll(values, RD // 2, 1)
    return values * table_ref[0] + sign * (ahead * table_ref[1] + behind * table_ref[2])


def seg_column(seg_ref):
    return seg_ref[...].T[:, :1]


def causal_mask(seg_ref):
    tokens = seg_ref.shape[1]
    row = lax.broadcasted_iota(jnp.int32, (tokens, tokens), 0)
    col = lax.broadcasted_iota(jnp.int32, (tokens, tokens), 1)
    return (seg_column(seg_ref) == seg_ref[:1, :]) & (col <= row)


def softmax_rows(query, key, allowed):
    scores = across(query, key) * score_scale
    masked = jnp.where(allowed, scores, -1e30)
    exponent = jnp.exp(masked - jnp.max(masked, axis=1, keepdims=True))
    return exponent * (1.0 / jnp.sum(exponent, axis=1, keepdims=True))


def key_lanes(keyval, latent_ref, lane):
    return jnp.where(lane < HD, keyval, latent_ref[:, QR + KR :])


def attend_kernel(
    heads,
    latent_ref,
    table_ref,
    seg_ref,
    query_w_ref,
    keyval_w_ref,
    out_w_ref,
    term_ref,
    query_ref,
    keyval_ref,
    mixed_ref,
):
    bf16 = jnp.bfloat16
    tokens = latent_ref.shape[0]
    lane = lane_index(tokens)
    allowed = causal_mask(seg_ref)
    query = along(latent_ref[:, :QR], query_w_ref[...])
    keyval_ref[...] = along(latent_ref[:, QR : QR + KR], keyval_w_ref[...]).astype(bf16)
    even = None
    for h in range(heads):
        at = slice(h * LANES, (h + 1) * LANES)
        query_h = turn(query[:, at], table_ref, 1.0).astype(bf16)
        query_ref[:, at] = query_h
        keyval_h = keyval_ref[:, at]
        probs = softmax_rows(query_h, key_lanes(keyval_h, latent_ref, lane), allowed).astype(bf16)
        mixed = along(probs, keyval_h)
        if h % 2 == 0:
            even = pltpu.roll(mixed, HD, 1)
            if h == heads - 1:
                mixed_ref[:, h * HD :] = even[:, :HD].astype(bf16)
        else:
            mixed_ref[:, (h - 1) * HD : (h + 1) * HD] = jnp.where(lane < HD, even, mixed).astype(
                bf16
            )
    term_ref[...] = along(mixed_ref[...], out_w_ref[...]).astype(bf16)


def nth(array, index):
    return pl.BlockSpec((None,) + array.shape[1:], lambda i: (index,) + (0,) * (array.ndim - 1))


def entire(array):
    return pl.BlockSpec(array.shape, lambda i: (0,) * array.ndim)


def attend(index, latent, table, seg, query_w, keyval_w, out_w):
    tokens = latent.shape[1]
    heads = query_w.shape[1] // LANES
    width = out_w.shape[1]
    bf16 = jnp.bfloat16
    return pl.pallas_call(
        functools.partial(attend_kernel, heads),
        grid=(1,),
        out_specs=[
            pl.BlockSpec((tokens, cols), lambda i: (0, 0))
            for cols in (width, heads * LANES, heads * LANES, heads * HD)
        ],
        in_specs=[nth(array, index) for array in (latent, table, seg)]
        + [entire(array) for array in (query_w, keyval_w, out_w)],
        out_shape=[
            jax.ShapeDtypeStruct((tokens, width), bf16),
            jax.ShapeDtypeStruct((tokens, heads * LANES), bf16),
            jax.ShapeDtypeStruct((tokens, heads * LANES), bf16),
            jax.ShapeDtypeStruct((tokens, heads * HD), bf16),
        ],
        compiler_params=pltpu.CompilerParams(vmem_limit_bytes=VMEM_BYTES),
        cost_estimate=pl.CostEstimate(
            flops=2 * tokens * (heads * LANES * (QR + KR + 2 * tokens) + heads * HD * width),
            bytes_accessed=2 * (heads * LANES * (QR + KR) + heads * HD * width + tokens * width),
            transcendentals=heads * tokens * tokens,
        ),
        name="attend",
    )(latent, table, seg, query_w, keyval_w, out_w)


def attend_back_kernel(
    heads,
    grad_ref,
    query_ref,
    keyval_ref,
    latent_ref,
    table_ref,
    seg_ref,
    query_w_ref,
    keyval_w_ref,
    out_w_ref,
    term_ref,
    grad_query_ref,
    grad_keyval_ref,
):
    bf16 = jnp.bfloat16
    f32 = jnp.float32
    tokens = latent_ref.shape[0]
    lane = lane_index(tokens)
    allowed = causal_mask(seg_ref)
    grad_mixed = across(grad_ref[...], out_w_ref[...])
    grad_rope = jnp.zeros((tokens, LANES), f32)
    for h in range(heads):
        at = slice(h * LANES, (h + 1) * LANES)
        query_h = query_ref[:, at]
        keyval_h = keyval_ref[:, at]
        key_h = key_lanes(keyval_h, latent_ref, lane)
        probs = softmax_rows(query_h, key_h, allowed)
        if h % 2 == 0:
            if h == heads - 1:
                one = jnp.concatenate([grad_mixed[:, h * HD :]] * 2, axis=1)
            else:
                pair = grad_mixed[:, h * HD : (h + 2) * HD]
                one = pltpu.roll(pair, HD, 1)
        else:
            one = pair
        value_grad = jnp.where(lane >= HD, one, 0.0).astype(bf16)
        turned = probs.astype(bf16).T
        grad_values = along(turned, value_grad)
        grad_probs = across(value_grad, keyval_h)
        delta = jnp.sum(probs * grad_probs, axis=1, keepdims=True)
        grad_scores = (probs * (grad_probs - delta)).astype(bf16)
        grad_q = along(grad_scores, key_h) * score_scale
        grad_k = along(grad_scores.T, query_h) * score_scale
        grad_query_ref[:, at] = turn(grad_q, table_ref, -1.0).astype(bf16)
        grad_keyval_ref[:, at] = jnp.where(lane < HD, grad_k, grad_values).astype(bf16)
        grad_rope = grad_rope + grad_k
    rope = jnp.where(lane >= HD, turn(grad_rope, table_ref, -1.0), 0.0)
    term_ref[:, :QR] = across(grad_query_ref[...], query_w_ref[...]).astype(bf16)
    term_ref[:, QR : QR + KR] = across(grad_keyval_ref[...], keyval_w_ref[...]).astype(bf16)
    term_ref[:, QR + KR :] = rope.astype(bf16)


def attend_back(
    index, grad, query, keyval, latent, table, seg, query_w, keyval_w, out_w
):
    tokens = latent.shape[1]
    heads = query_w.shape[1] // LANES
    width = out_w.shape[1]
    bf16 = jnp.bfloat16
    return pl.pallas_call(
        functools.partial(attend_back_kernel, heads),
        grid=(1,),
        out_specs=[
            pl.BlockSpec((tokens, cols), lambda i: (0, 0))
            for cols in (LATENT, heads * LANES, heads * LANES)
        ],
        in_specs=[entire(array) for array in (grad, query, keyval)]
        + [nth(array, index) for array in (latent, table, seg)]
        + [entire(array) for array in (query_w, keyval_w, out_w)],
        out_shape=[
            jax.ShapeDtypeStruct((tokens, LATENT), bf16),
            jax.ShapeDtypeStruct((tokens, heads * LANES), bf16),
            jax.ShapeDtypeStruct((tokens, heads * LANES), bf16),
        ],
        compiler_params=pltpu.CompilerParams(vmem_limit_bytes=VMEM_BYTES),
        cost_estimate=pl.CostEstimate(
            flops=2 * tokens * (heads * LANES * (QR + KR + 5 * tokens) + heads * HD * width),
            bytes_accessed=2 * (heads * LANES * (QR + KR) + heads * HD * width + tokens * width),
            transcendentals=heads * tokens * tokens,
        ),
        name="attend_back",
    )(grad, query, keyval, latent, table, seg, query_w, keyval_w, out_w)


def token_grad_kernel(count, *refs):
    left = refs[:count]
    right = refs[count : 2 * count]
    out_ref, turned, whole = refs[2 * count :]
    tokens = left[0].shape[0]
    for j in range(count):
        turned[:, j * tokens : (j + 1) * tokens] = left[j][...].T
        whole[j * tokens : (j + 1) * tokens, :] = right[j][...]
    out_ref[...] = along(turned[...], whole[...]).astype(jnp.bfloat16)


def token_grad(left, right, first, rows, name):
    count = len(right)
    tokens, cols = right[0].shape
    at = first // rows
    if isinstance(left, list):
        left_specs = [pl.BlockSpec((tokens, rows), lambda i: (0, at))] * count
    else:
        left_specs = [
            pl.BlockSpec((None, tokens, rows), lambda i, j=j: (j, 0, at)) for j in range(count)
        ]
        left = [left] * count
    return pl.pallas_call(
        functools.partial(token_grad_kernel, count),
        grid=(1,),
        in_specs=left_specs + [pl.BlockSpec((tokens, cols), lambda i: (0, 0))] * count,
        out_specs=pl.BlockSpec((rows, cols), lambda i: (0, 0)),
        out_shape=jax.ShapeDtypeStruct((rows, cols), jnp.bfloat16),
        scratch_shapes=[
            pltpu.VMEM((rows, count * tokens), jnp.bfloat16),
            pltpu.VMEM((count * tokens, cols), jnp.bfloat16),
        ],
        compiler_params=pltpu.CompilerParams(vmem_limit_bytes=VMEM_BYTES),
        cost_estimate=pl.CostEstimate(
            flops=2 * count * tokens * rows * cols,
            bytes_accessed=2 * (rows * cols + count * tokens * (rows + cols)),
            transcendentals=0,
        ),
        name=name,
    )(*left, *right)


MESH = pl.DeviceIdType.MESH


def partner(me, distance):
    bit = 1
    while bit <= distance:
        if distance & bit:
            me = me + bit - 2 * bit * lax.rem(lax.div(me, bit), 2)
        bit *= 2
    return me


def greet(peers, count):
    barrier = pltpu.get_barrier_semaphore()
    for peer in peers:
        pl.semaphore_signal(barrier, inc=1, device_id=peer, device_id_type=MESH)
    pl.semaphore_wait(barrier, count)


def send(src, dst, sems, index, peer):
    copy = pltpu.make_async_remote_copy(
        src_ref=src,
        dst_ref=dst,
        send_sem=sems.at[0, index],
        recv_sem=sems.at[1, index],
        device_id=peer,
        device_id_type=MESH,
    )
    copy.start()
    return copy


def tile_format(gate, up, store, tiles, tail):
    bf16 = jnp.bfloat16
    for t in range(tiles):
        store(2 * t * TILE, gate[:, t * TILE : (t + 1) * TILE].astype(bf16))
        store((2 * t + 1) * TILE, up[:, t * TILE : (t + 1) * TILE].astype(bf16))
    lane = lax.broadcasted_iota(jnp.int32, (gate.shape[0], TAIL), 1)
    for second, values in enumerate((gate, up)):
        last = values[:, tiles * TILE : tiles * TILE + TAIL]
        store(
            2 * tiles * TILE + second * TAIL, jnp.where(lane < tail, last, 0.0).astype(bf16)
        )


def head_table(seg_ref, rates_ref, table_ref):
    tokens = seg_ref.shape[1]
    row = lax.broadcasted_iota(jnp.int32, (tokens, tokens), 0)
    col = lax.broadcasted_iota(jnp.int32, (tokens, tokens), 1)
    before = (seg_column(seg_ref) == seg_ref[:1, :]) & (col < row)
    position = jnp.sum(jnp.where(before, 1.0, 0.0), axis=1, keepdims=True)
    angles = position * rates_ref[...]
    sine = jnp.sin(angles)
    lane = lane_index(tokens)
    middle = HD + RD // 2
    end = HD + RD
    table_ref[0] = jnp.where(lane < end, jnp.cos(angles), 0.0)
    table_ref[1] = jnp.where((lane >= HD) & (lane < middle), -sine, 0.0)
    table_ref[2] = jnp.where((lane >= middle) & (lane < end), sine, 0.0)


def share_small(group, me, peers, gains_ref, seg_ref, gains_all_ref, segs_ref, sems):
    mine = pl.ds(pl.multiple_of(me * 8, 8), 8)
    gains_all_ref[mine, :] = gains_ref[...]
    segs_ref[0] = seg_ref[...]
    copies = []
    for j in range(1, group):
        copies.append(send(gains_ref, gains_all_ref.at[mine, :], sems, 2 * (j - 1), peers[j - 1]))
        copies.append(send(seg_ref, segs_ref.at[j], sems, 2 * (j - 1) + 1, peers[j - 1]))
    return copies


def small_kernel(
    group, gains_ref, seg_ref, rates_ref, gains_all_ref, segs_ref, table_ref, small_sems
):
    me = lax.axis_index("shard")
    rep = lax.axis_index("rep")
    peers = [(partner(me, j), rep) for j in range(1, group)]
    greet(peers, group - 1)
    for copy in share_small(group, me, peers, gains_ref, seg_ref, gains_all_ref, segs_ref, small_sems):
        copy.wait()
    for j in range(group):
        head_table(segs_ref.at[j], rates_ref, table_ref.at[j])


def columns_kernel(
    group,
    replicas,
    hidden,
    slab,
    gate_up_ref,
    gains_ref,
    seg_ref,
    rates_ref,
    own_ref,
    pieces_ref,
    gains_all_ref,
    segs_ref,
    table_ref,
    own_slab,
    slabs,
    out_pieces,
    local_sems,
    sems,
    small_sems,
):
    me = lax.axis_index("shard")
    rep = lax.axis_index("rep")
    rows, share = own_slab.shape[1], slabs.shape[1]
    tiles = hidden // TILE
    tail = hidden - tiles * TILE
    main = 2 * tiles * TILE

    def begin(index, second):
        offset = index * hidden
        return pl.multiple_of(second * FF + offset - lax.rem(offset, LANES), LANES)

    loads = []
    for j in range(1, group):
        for second in range(2):
            at = 2 * (j - 1) + second
            copy = pltpu.make_async_copy(
                gate_up_ref.at[
                    pl.ds(pl.multiple_of(rep * share, 16), share), pl.ds(begin(partner(me, j), second), slab)
                ],
                slabs.at[at],
                local_sems.at[at],
            )
            copy.start()
            loads.append(copy)
    for second in range(2):
        at = 2 * (group - 1) + second
        copy = pltpu.make_async_copy(
            gate_up_ref.at[:, pl.ds(begin(me, second), slab)],
            own_slab.at[second],
            local_sems.at[at],
        )
        copy.start()
        loads.append(copy)
    peers = [(partner(me, j), rep) for j in range(1, group)]
    greet(peers, group - 1)
    small = share_small(group, me, peers, gains_ref, seg_ref, gains_all_ref, segs_ref, small_sems)

    def shifted(ref, index):
        amount = lax.rem(slab - lax.rem(index * hidden, LANES), slab)
        return pltpu.roll(ref[...].astype(jnp.float32), amount, 1)

    sent = []
    for j in range(1, group):
        for second in range(2):
            loads[2 * (j - 1) + second].wait()

        def store(first, values, j=j):
            out_pieces[j - 1, :, first : first + values.shape[1]] = values

        tile_format(
            shifted(slabs.at[2 * (j - 1)], partner(me, j)),
            shifted(slabs.at[2 * (j - 1) + 1], partner(me, j)),
            store,
            tiles,
            tail,
        )
        sent.append(
            send(
                out_pieces.at[j - 1, :, pl.ds(0, main)],
                pieces_ref.at[:, pl.ds((j - 1) * main, main)],
                sems,
                2 * (j - 1),
                peers[j - 1],
            )
        )
        sent.append(
            send(
                out_pieces.at[j - 1, :, pl.ds(main, 2 * TAIL)],
                pieces_ref.at[:, pl.ds((group - 1) * main + (j - 1) * 2 * TAIL, 2 * TAIL)],
                sems,
                2 * (j - 1) + 1,
                peers[j - 1],
            )
        )
    for second in range(2):
        loads[2 * (group - 1) + second].wait()

    def store_own(first, values):
        own_ref[:, first : first + values.shape[1]] = values

    tile_format(
        shifted(own_slab.at[0], me), shifted(own_slab.at[1], me), store_own, tiles, tail
    )
    for copy in small:
        copy.wait()
    for j in range(group):
        head_table(segs_ref.at[j], rates_ref, table_ref.at[j])
    for copy in sent:
        copy.wait()


def small_shapes(gains, seg, group):
    rows, tokens = seg.shape
    f32 = jnp.float32
    return [
        jax.ShapeDtypeStruct((group * rows, gains.shape[1]), f32),
        jax.ShapeDtypeStruct((group, rows, tokens), f32),
        jax.ShapeDtypeStruct((group, 3, tokens, LANES), f32),
    ]


def small_things(gains, seg, group):
    return pl.pallas_call(
        functools.partial(small_kernel, group),
        in_specs=[pl.BlockSpec(memory_space=pltpu.VMEM)] * 3,
        out_specs=[pl.BlockSpec(memory_space=pltpu.VMEM)] * 3,
        out_shape=small_shapes(gains, seg, group),
        scratch_shapes=[pltpu.SemaphoreType.DMA((2, 2 * (group - 1)))],
        compiler_params=pltpu.CompilerParams(
            collective_id=3, has_side_effects=True, vmem_limit_bytes=VMEM_BYTES
        ),
        name="small_things",
    )(gains, seg, rotation_rates())


def hidden_pieces(gate_up, gains, seg, group, replicas):
    rows = gate_up.shape[0]
    share = rows // replicas
    hidden = FF // group
    whole = 2 * (hidden // TILE * TILE + TAIL)
    slab = -(-(hidden + LANES - math.gcd(hidden, LANES)) // LANES) * LANES
    bf16 = jnp.bfloat16
    others = group - 1
    return pl.pallas_call(
        functools.partial(columns_kernel, group, replicas, hidden, slab),
        in_specs=[pl.BlockSpec(memory_space=pl.ANY)] + [pl.BlockSpec(memory_space=pltpu.VMEM)] * 3,
        out_specs=[pl.BlockSpec(memory_space=pltpu.VMEM)] * 5,
        out_shape=[
            jax.ShapeDtypeStruct((rows, whole), bf16),
            jax.ShapeDtypeStruct((share, others * whole), bf16),
        ]
        + small_shapes(gains, seg, group),
        scratch_shapes=[
            pltpu.VMEM((2, rows, slab), bf16),
            pltpu.VMEM((2 * others, share, slab), bf16),
            pltpu.VMEM((others, share, whole), bf16),
            pltpu.SemaphoreType.DMA((2 * group,)),
            pltpu.SemaphoreType.DMA((2, 2 * others)),
            pltpu.SemaphoreType.DMA((2, 2 * others)),
        ],
        compiler_params=pltpu.CompilerParams(
            collective_id=1, has_side_effects=True, vmem_limit_bytes=VMEM_BYTES
        ),
        cost_estimate=pl.CostEstimate(flops=0, bytes_accessed=100_000_000, transcendentals=0),
        name="hidden_pieces",
    )(gate_up, gains, seg, rotation_rates())


def latent_kernel(
    group,
    tokens_ref,
    gains_ref,
    latent_gains_ref,
    table_ref,
    latent_proj_ref,
    query_ref,
    keyval_ref,
    parts_ref,
    rows_ref,
    normed_ref,
    latent_w_ref,
    query_w_ref,
    keyval_w_ref,
    local_sems,
    fetch_sems,
    swap_sems,
    weight_sems,
    weight_swap_sems,
    part_sems,
):
    f32 = jnp.float32
    bf16 = jnp.bfloat16
    me = lax.axis_index("shard")
    rep = lax.axis_index("rep")
    core = lax.rem(rep, 2)
    tokens = tokens_ref.shape[0]
    rows_d = latent_proj_ref.shape[0]
    half = rows_d // 2
    query_rows = query_ref.shape[0]
    keyval_rows = keyval_ref.shape[0]
    width = query_w_ref.shape[1]
    others = range(1, group)
    peers = [None] + [(partner(me, j), rep) for j in others]
    sibling = (me, rep + 1 - 2 * core)
    greet(peers[1:] + [sibling], group)

    def block(index, which):
        return pl.ds(pl.multiple_of(index * rows_d + which * half, 16), half)

    fetched = [None] + [
        send(
            latent_proj_ref.at[pl.ds(pl.multiple_of(core * half, 16), half), :],
            latent_w_ref.at[block(me, core), :],
            fetch_sems,
            j - 1,
            peers[j],
        )
        for j in others
    ]
    own = pltpu.make_async_copy(
        latent_proj_ref,
        latent_w_ref.at[pl.ds(pl.multiple_of(me * rows_d, 16), rows_d), :],
        local_sems.at[0],
    )
    own.start()
    kinds = ((query_ref, query_w_ref, query_rows), (keyval_ref, keyval_w_ref, keyval_rows))

    def weight_rows(index, rows):
        return pl.ds(pl.multiple_of(index * rows + core * (rows // 2), 16), rows // 2)

    def fetch_weights():
        return [
            send(
                ref.at[
                    pl.ds(pl.multiple_of(core * (rows // 2), 16), rows // 2),
                    pl.ds(pl.multiple_of(partner(me, j) * width, LANES), width),
                ],
                out_ref.at[weight_rows(me, rows), :],
                weight_sems,
                kind * (group - 1) + j - 1,
                peers[j],
            )
            for kind, (ref, out_ref, rows) in enumerate(kinds)
            for j in others
        ]

    def swap_weights(copies):
        swaps = []
        for kind, (ref, out_ref, rows) in enumerate(kinds):
            for j in others:
                index = kind * (group - 1) + j - 1
                copies[index].wait_recv()
                where = weight_rows(partner(me, j), rows)
                swaps.append(
                    send(
                        out_ref.at[where, :],
                        out_ref.at[where, :],
                        weight_swap_sems,
                        index,
                        sibling,
                    )
                )
        return swaps

    mine = []
    for at, (ref, out_ref, rows) in enumerate(kinds):
        copy = pltpu.make_async_copy(
            ref.at[:, pl.ds(pl.multiple_of(me * width, LANES), width)],
            out_ref.at[pl.ds(pl.multiple_of(me * rows, 16), rows), :],
            local_sems.at[1 + at],
        )
        copy.start()
        mine.append(copy)

    rows_in = tokens_ref[...].astype(f32)
    scale = lax.rsqrt(jnp.mean(rows_in * rows_in, axis=1, keepdims=True) + norm_eps)
    normed_ref[...] = (rows_in * scale * gains_ref[...]).astype(bf16)

    swaps = []
    for j in others:
        fetched[j].wait_recv()
        where = block(partner(me, j), core)
        swaps.append(
            send(latent_w_ref.at[where, :], latent_w_ref.at[where, :], swap_sems, j - 1, sibling)
        )
    weights = fetch_weights()
    own.wait()
    for copy in swaps:
        copy.wait()
    for j in others:
        fetched[j].wait_send()
    latent = along(normed_ref[...], latent_w_ref[...])
    rows_ref[...] = latent

    def rms(values):
        return values * lax.rsqrt(jnp.mean(values * values, axis=1, keepdims=True) + norm_eps)

    query = rms(latent[:, :QR]) * latent_gains_ref[:, :QR]
    keyval = rms(latent[:, QR : QR + KR]) * latent_gains_ref[:, QR:]
    rope = latent[:, QR + KR :]
    wide = jnp.concatenate(
        [jnp.zeros((tokens, HD), f32), rope, jnp.zeros((tokens, LANES - HD - RD), f32)], axis=1
    )
    parts_ref[0, :, :QR] = query.astype(bf16)
    parts_ref[0, :, QR : QR + KR] = keyval.astype(bf16)
    parts_ref[0, :, QR + KR :] = turn(wide, table_ref, 1.0).astype(bf16)

    direct = (1, 2) if group == 4 else others
    near = [
        send(parts_ref.at[0], parts_ref.at[j], part_sems, j - 1, peers[j]) for j in direct
    ]
    swaps = swap_weights(weights)
    far = []
    if group == 4:
        part = tokens // 2
        top = pl.ds(0, part)
        low = pl.ds(part, part)
        near[0].wait_recv()
        far.append(send(parts_ref.at[1, top], parts_ref.at[3, top], part_sems, 2, peers[2]))
        near[1].wait_recv()
        far.append(send(parts_ref.at[2, low], parts_ref.at[3, low], part_sems, 3, peers[1]))
        for copy in near:
            copy.wait_send()
    else:
        for copy in near:
            copy.wait()
    for copy in far + swaps + mine:
        copy.wait()
    for copy in weights:
        copy.wait_send()


def latent_front(tokens, gain_in, latent_gains, table, latent_proj, query_pad, keyval, group):
    rows = tokens.shape[0]
    heads = query_pad.shape[1] // LANES // group
    bf16 = jnp.bfloat16
    others = group - 1
    dma = pltpu.SemaphoreType.DMA
    width = latent_proj.shape[1]
    return pl.pallas_call(
        functools.partial(latent_kernel, group),
        in_specs=[pl.BlockSpec(memory_space=pltpu.VMEM)] * 7,
        out_specs=[pl.BlockSpec(memory_space=pltpu.VMEM)] * 6,
        out_shape=[
            jax.ShapeDtypeStruct((group, rows, LATENT), bf16),
            jax.ShapeDtypeStruct((rows, width), jnp.float32),
            jax.ShapeDtypeStruct((rows, D), bf16),
            jax.ShapeDtypeStruct((D, width), bf16),
            jax.ShapeDtypeStruct((QR, heads * LANES), bf16),
            jax.ShapeDtypeStruct((KR, heads * LANES), bf16),
        ],
        scratch_shapes=[
            dma((3,)),
            dma((2, others)),
            dma((2, others)),
            dma((2, 2 * others)),
            dma((2, 2 * others)),
            dma((2, max(others, 4))),
        ],
        compiler_params=pltpu.CompilerParams(
            collective_id=2, has_side_effects=True, vmem_limit_bytes=VMEM_BYTES
        ),
        cost_estimate=pl.CostEstimate(
            flops=2 * rows * D * width, bytes_accessed=60_000_000, transcendentals=0
        ),
        name="latent_front",
    )(tokens, gain_in, latent_gains, table, latent_proj, query_pad, keyval)


def hop(array, group, distance):
    return lax.ppermute(array, "shard", [(i, i ^ distance) for i in range(group)])


def near_blocks(array, group):
    return [hop(array, group, j) for j in ((1, 2) if group == 4 else range(1, group))]


def all_blocks(array, near, group):
    if group != 4:
        return [array] + near
    half = array.shape[0] // 2
    far_top = hop(near[0][:half], group, 2)
    far_low = hop(near[1][half:], group, 1)
    return [array] + near + [jnp.concatenate([far_top, far_low], axis=0)]


def gather_blocks(array, group):
    return all_blocks(array, near_blocks(array, group), group)


def scatter_sum(parts, group):
    low = jnp.bfloat16
    f32 = jnp.float32
    total = parts[0].astype(f32)
    if group != 4:
        for j in range(1, group):
            total = total + hop(parts[j], group, j).astype(f32)
        return total
    half = parts[0].shape[0] // 2
    top = hop(parts[3][:half], group, 1)
    bottom = hop(parts[3][half:], group, 2)

    def add(left, right):
        return (left.astype(f32) + right.astype(f32)).astype(low)

    two = jnp.concatenate([add(parts[2][:half], top), parts[2][half:]], axis=0)
    one = jnp.concatenate([parts[1][:half], add(parts[1][half:], bottom)], axis=0)
    return total + hop(one, group, 1).astype(f32) + hop(two, group, 2).astype(f32)


def place(blocks, me):
    rows = blocks[0].shape[0]
    whole = jnp.zeros((rows * len(blocks),) + blocks[0].shape[1:], blocks[0].dtype)
    for j, block in enumerate(blocks):
        whole = lax.dynamic_update_slice_in_dim(whole, block, (me ^ j) * rows, 0)
    return whole


def pick(whole, me, group):
    rows = whole.shape[0] // group
    return [lax.dynamic_slice_in_dim(whole, (me ^ j) * rows, rows, 0) for j in range(group)]


def columns(array, index, width):
    return lax.dynamic_slice_in_dim(array, index * width, width, 1)


def per_device(
    group,
    replicas,
    tokens,
    segments,
    cotangent,
    latent_proj,
    query_up,
    keyval_up,
    out_proj,
    gate_up,
    down_proj,
    norm_gains,
    latent_mean,
    query_mean,
    keyval_mean,
    outproj_mean,
    gateup_mean,
    down_mean,
    gains_mean,
    latent_square,
    query_square,
    keyval_square,
    outproj_square,
    gateup_square,
    down_square,
    gains_square,
):
    f32 = jnp.float32
    bf16 = jnp.bfloat16
    me = lax.axis_index("shard")
    rep = lax.axis_index("rep")
    seq_len = tokens.shape[0]
    heads = H // group
    hidden_part = FF // group
    tiles = hidden_part // TILE
    tail = hidden_part - tiles * TILE
    rows_d = D // group
    others = range(1, group)
    order = jnp.stack([me ^ j for j in range(group)]).astype(jnp.int32)

    share = rows_d // replicas
    fast = group == 4 and share % 16 == 0
    gains_rows = jnp.broadcast_to(norm_gains.astype(f32), (8,) + norm_gains.shape)
    seg_rows = jnp.broadcast_to(segments.astype(f32), (8, seq_len))
    query_pad = jnp.pad(
        query_up.reshape(-1, H, HD + RD), ((0, 0), (0, 0), (0, LANES - HD - RD))
    ).reshape(-1, H * LANES)

    def hidden_columns(array, index):
        gate = columns(array, index, hidden_part)
        up = lax.dynamic_slice_in_dim(array, FF + index * hidden_part, hidden_part, 1)
        cut = []
        for t in range(tiles):
            cut += [gate[:, t * TILE : (t + 1) * TILE], up[:, t * TILE : (t + 1) * TILE]]
        for last in (gate, up):
            cut.append(jnp.pad(last[:, tiles * TILE :], ((0, 0), (0, TAIL - tail))))
        return jnp.concatenate(cut, axis=1)

    share = rows_d // replicas
    cot_near = near_blocks(cotangent, group)
    if share % 16 == 0:
        own_columns, pieces, gains_all, segs, tables = hidden_pieces(
            gate_up, gains_rows, seg_rows, group, replicas
        )
    else:
        gains_all, segs, tables = small_things(gains_rows, seg_rows, group)
        own_share = lax.dynamic_slice_in_dim(gate_up, rep * share, share, 0)
        own_columns = hidden_columns(gate_up, me)
        main = 2 * tiles * TILE
        pieces = [hop(hidden_columns(own_share, me ^ j), group, j) for j in others]
        pieces = jnp.concatenate(
            [piece[:, :main] for piece in pieces] + [piece[:, main:] for piece in pieces], axis=1
        )
    gathered_columns = lax.all_gather(pieces, "rep", axis=0, tiled=True)
    gains_f = gains_all.reshape(group, 8, -1)[:, 0, :].reshape(-1)
    gain_in = gains_f[:D]
    gain_query = gains_f[D : D + QR]
    gain_keyval = gains_f[D + QR : D + QR + KR]
    gain_mlp = gains_f[D + QR + KR :]

    latent_late, _ = lax.optimization_barrier((latent_proj, pieces))
    latent_parts, latent_all, normed_in, latent_w, query_w, keyval_w = latent_front(
        tokens,
        gain_in.reshape(1, D),
        gains_f[D : D + QR + KR].reshape(1, QR + KR),
        tables[0],
        latent_late,
        query_pad,
        keyval_up,
        group,
    )
    rows_in = tokens.astype(f32)
    inv_in = inverse_rms(rows_in)
    query_lat = latent_all[:, :QR]
    keyval_lat = latent_all[:, QR : QR + KR]
    inv_query = inverse_rms(query_lat)
    inv_keyval = inverse_rms(keyval_lat)

    attention = [None] * group
    latents_next = latent_parts
    for at, j in enumerate((*reversed(others), 0)):
        if at == 1:
            latents_next, cot_near = lax.optimization_barrier((latents_next, cot_near))
            cot_parts = all_blocks(cotangent, cot_near, group)
        if j == 0:
            latents_next, _ = lax.optimization_barrier((latents_next, cot_parts[1:]))
        attention[j] = attend(j, latents_next, tables, segs, query_w, keyval_w, out_proj)
        latents_next, _ = lax.optimization_barrier((latent_parts, attention[j][0]))
    out_terms = [part[0] for part in attention]
    hidden = rows_in + residual_scale * scatter_sum(out_terms, group)
    inv_hidden = inverse_rms(hidden)
    normed_mlp = (hidden * inv_hidden * gain_mlp).astype(bf16)

    near = near_blocks(normed_mlp, group)
    half_tiles = tiles // 2
    if fast:
        mlp_parts = all_blocks(normed_mlp, near, group)

        def some_tiles(earlier, first, count):
            return layer_part(
                order,
                mlp_parts,
                cot_parts,
                own_columns,
                gathered_columns,
                down_proj,
                earlier,
                first,
                count,
                group,
                replicas,
            )

        early = some_tiles(None, 0, half_tiles)
        act_all, grad_late, back_all = some_tiles(early, half_tiles, tiles - half_tiles)
        cuts = [(0, half_tiles), (half_tiles, tiles)]
        grad_cuts = [early[1].reshape(D, -1), grad_late.reshape(D, -1)]
        hidden_terms = [back_all[j * seq_len : (j + 1) * seq_len] for j in range(group)]
    else:
        branch_parts = [(residual_scale * part.astype(f32)).astype(bf16) for part in cot_parts]

        def mlp_block(j, normed, earlier):
            return mlp_part(
                order,
                normed,
                branch_parts[j],
                own_columns,
                gathered_columns,
                down_proj,
                earlier,
                j,
                group,
            )

        first = mlp_block(0, normed_mlp, ())
        near, first = lax.optimization_barrier((near, first))
        mlp_parts = all_blocks(normed_mlp, near, group)
        terms = [first]
        for j in others:
            terms.append(mlp_block(j, mlp_parts[j], terms[-1][:2]))
        act_all, grad_all = terms[-1][:2]
        down_terms = [term[2] for term in terms]
        hidden_terms = [term[3] for term in terms]
        cuts = [(0, tiles)]
        grad_gateup = jnp.einsum(
            "td,tf->df", jnp.concatenate(mlp_parts), grad_all, preferred_element_type=f32
        )
        grad_cuts = [
            grad_gateup.astype(bf16)
            .reshape(group, replicas, share, -1)
            .transpose(1, 0, 2, 3)
            .reshape(D, -1)
        ]
    normed_late, _ = lax.optimization_barrier((normed_in, mlp_parts[1:]))
    normed_columns = [columns(normed_late, me, rows_d)] + [
        hop(columns(normed_late, me ^ j, rows_d), group, j) for j in others
    ]
    grad_normed_mlp = scatter_sum(hidden_terms, group)

    grad_down = down_grad(act_all, cot_parts, hidden_part, group)

    def to_owner_rows(block_rows):
        blocks = pick(block_rows, me, group)
        blocks = [blocks[0]] + [hop(blocks[j], group, j) for j in others]
        return place(blocks, me).reshape((group,) + blocks[0].shape)

    grad_top = cotangent.astype(f32)
    grad_gain_mlp = jnp.sum(grad_normed_mlp * hidden * inv_hidden, axis=0)
    grad_hidden = grad_top + norm_back(grad_normed_mlp * gain_mlp, hidden, inv_hidden)
    grad_attn = (residual_scale * grad_hidden).astype(bf16)
    grad_attn, grad_down = lax.optimization_barrier((grad_attn, grad_down))

    def back_block(j, grad):
        return attend_back(
            j,
            grad,
            attention[j][1],
            attention[j][2],
            latent_parts,
            tables,
            segs,
            query_w,
            keyval_w,
            out_proj,
        )

    near = near_blocks(grad_attn, group)
    back = [back_block(0, grad_attn)]
    near, back = lax.optimization_barrier((near, back))
    attn_parts = all_blocks(grad_attn, near, group)
    back += [back_block(j, attn_parts[j]) for j in others]
    summed = []
    for at, grad_cut in enumerate(grad_cuts):
        if at:
            grad_cut, _ = lax.optimization_barrier((grad_cut, (summed[-1], grad_attn)))
        summed.append(lax.psum_scatter(grad_cut, "rep", scatter_dimension=0, tiled=True))
    owned = [to_owner_rows(rows) for rows in summed]

    def unpack(q, second):
        pieces = []
        for (start, stop), rows in zip(cuts, owned):
            for t in range(stop - start):
                first = (2 * t + second) * TILE
                pieces.append(rows[q, :, first : first + TILE])
        first = 2 * (cuts[-1][1] - cuts[-1][0]) * TILE + second * TAIL
        return pieces + [owned[-1][q, :, first : first + tail]]

    gateup_total = jnp.concatenate(
        [piece for second in (0, 1) for q in range(group) for piece in unpack(q, second)], axis=1
    )
    latent_terms = [part[0] for part in back]
    grad_out = token_grad([part[3] for part in attention], attn_parts, 0, heads * HD, "out_grad")
    grad_query = token_grad(latent_parts, [part[1] for part in back], 0, QR, "query_grad")
    grad_keyval = token_grad(latent_parts, [part[2] for part in back], QR, KR, "keyval_grad")
    query_rows = QR // (group * replicas)
    keyval_rows = KR // (group * replicas)
    unit = heads * LANES
    pair_rows = group * (query_rows + keyval_rows)
    out_units = D // unit
    out_count = heads * HD // replicas
    pair = (
        jnp.concatenate(
            [
                grad_query.reshape(group, replicas, query_rows, unit),
                grad_keyval.reshape(group, replicas, keyval_rows, unit),
            ],
            axis=2,
        )
        .transpose(1, 0, 2, 3)
        .reshape(replicas, pair_rows, unit)
    )
    grad_out = grad_out.reshape(replicas, out_count, D)
    grad_out = [grad_out[:, :, k * unit : (k + 1) * unit] for k in range(out_units)]

    grad_latent_low = scatter_sum(latent_terms, group)
    grad_normed_query = grad_latent_low[:, :QR]
    grad_normed_keyval = grad_latent_low[:, QR : QR + KR]
    grad_key_rope = grad_latent_low[:, QR + KR + HD : QR + KR + HD + RD]
    grad_gain_query = jnp.sum(grad_normed_query * query_lat * inv_query, axis=0)
    grad_gain_keyval = jnp.sum(grad_normed_keyval * keyval_lat * inv_keyval, axis=0)
    grad_latent_rows = jnp.concatenate(
        [
            norm_back(grad_normed_query * gain_query, query_lat, inv_query),
            norm_back(grad_normed_keyval * gain_keyval, keyval_lat, inv_keyval),
            grad_key_rope,
        ],
        axis=1,
    ).astype(bf16)
    grad_latent_parts = gather_blocks(grad_latent_rows, group)
    act_late, _ = lax.optimization_barrier((act_all, grad_latent_rows))
    if fast:
        down_all = jnp.dot(
            act_late[:, :hidden_part], down_proj, preferred_element_type=f32
        ).astype(bf16)
        down_terms = [down_all[j * seq_len : (j + 1) * seq_len] for j in range(group)]
    block_out = (hidden + residual_scale * scatter_sum(down_terms, group)).astype(bf16)
    grad_down, _ = lax.optimization_barrier((grad_down, (summed[-1], grad_latent_rows)))
    down_total = lax.psum_scatter(grad_down, "rep", scatter_dimension=0, tiled=True)
    grad_normed_in = jnp.einsum(
        "tc,dc->td", grad_latent_rows, latent_w, preferred_element_type=f32
    )
    grad_gain_in = jnp.sum(grad_normed_in * rows_in * inv_in, axis=0)
    input_grad = grad_hidden + norm_back(grad_normed_in * gain_in, rows_in, inv_in)
    grad_gains = jnp.concatenate([grad_gain_in, grad_gain_query, grad_gain_keyval, grad_gain_mlp])
    gain_blocks = pick(grad_gains, me, group)
    gains_sum = gain_blocks[0]
    for j in others:
        gains_sum = gains_sum + hop(gain_blocks[j].astype(bf16), group, j).astype(f32)
    grad_latent = jnp.einsum(
        "td,tc->dc",
        jnp.concatenate(normed_columns, axis=0),
        jnp.concatenate(grad_latent_parts, axis=0),
        preferred_element_type=f32,
    ).astype(bf16)
    width = grad_latent.shape[1]
    latent_units = -(-width // unit)
    grad_latent = jnp.pad(
        grad_latent.reshape(replicas, share, width), ((0, 0), (0, 0), (0, latent_units * unit - width))
    )
    grad_latent = [grad_latent[:, :, k * unit : (k + 1) * unit] for k in range(latent_units)]
    gains_row = gains_sum.reshape(replicas, 1, -1).astype(bf16)
    gains_row = jnp.pad(gains_row, ((0, 0), (0, 15), (0, unit - gains_row.shape[2])))
    last = jnp.concatenate([pair] + grad_out + grad_latent + [gains_row], axis=1)
    last, _ = lax.optimization_barrier((last.reshape(-1, unit), down_total))
    last = lax.psum_scatter(last, "rep", scatter_dimension=0, tiled=True)
    pair_own = to_owner_rows(last[:pair_rows])
    query_total = (
        pair_own[:, :query_rows]
        .reshape(group, query_rows, heads, LANES)[..., : HD + RD]
        .transpose(1, 0, 2, 3)
        .reshape(query_rows, H * (HD + RD))
    )
    keyval_total = pair_own[:, query_rows:].transpose(1, 0, 2).reshape(keyval_rows, 2 * H * HD)

    def side_by_side(first, count, pieces):
        return jnp.concatenate(
            [last[first + k * count : first + (k + 1) * count] for k in range(pieces)], axis=1
        )

    outproj_total = side_by_side(pair_rows, out_count, out_units)
    latent_at = pair_rows + out_units * out_count
    latent_total = side_by_side(latent_at, share, latent_units)[:, :width]
    gains_total = last[latent_at + latent_units * share, : gains_mean.shape[0]]

    updates = [
        adam_step(latent_proj, latent_total, latent_mean, latent_square, D ** (-0.5), decay_rate),
        adam_step(query_up, query_total, query_mean, query_square, QR ** (-0.5), decay_rate),
        adam_step(keyval_up, keyval_total, keyval_mean, keyval_square, KR ** (-0.5), decay_rate),
        adam_step(
            out_proj,
            outproj_total,
            outproj_mean,
            outproj_square,
            max(H * HD // 512, 1) ** (-0.5),
            decay_rate,
        ),
        adam_step(gate_up, gateup_total, gateup_mean, gateup_square, D ** (-0.5), decay_rate),
        adam_step(
            down_proj, down_total, down_mean, down_square, max(FF // 32, 1) ** (-0.5), decay_rate
        ),
        adam_step(norm_gains, gains_total, gains_mean, gains_square, gain_rate, 0.0),
    ]
    return (block_out, input_grad) + tuple(value for update in updates for value in update)


def solution(mesh):
    return jax.shard_map(
        functools.partial(per_device, mesh.shape["shard"], mesh.shape["rep"]),
        mesh=mesh,
        in_specs=(
            P(("shard", "rep"), None),
            P(("shard", "rep"), None),
            P(("shard", "rep"), None),
            P("shard", None),
            P("shard", None),
            P("shard", None),
            P("shard", None),
            P("shard", None),
            P("shard", None),
            P("shard"),
            P(("shard", "rep"), None),
            P(("shard", "rep"), None),
            P(("shard", "rep"), None),
            P(("shard", "rep"), None),
            P(("shard", "rep"), None),
            P(("shard", "rep"), None),
            P(("shard", "rep")),
            P(("shard", "rep"), None),
            P(("shard", "rep"), None),
            P(("shard", "rep"), None),
            P(("shard", "rep"), None),
            P(("shard", "rep"), None),
            P(("shard", "rep"), None),
            P(("shard", "rep")),
        ),
        out_specs=(
            P(("shard", "rep"), None),
            P(("shard", "rep"), None),
            P(("shard", "rep"), None),
            P(("shard", "rep"), None),
            P(("shard", "rep"), None),
            P(("shard", "rep"), None),
            P(("shard", "rep"), None),
            P(("shard", "rep"), None),
            P(("shard", "rep"), None),
            P(("shard", "rep"), None),
            P(("shard", "rep"), None),
            P(("shard", "rep"), None),
            P(("shard", "rep"), None),
            P(("shard", "rep"), None),
            P(("shard", "rep"), None),
            P(("shard", "rep"), None),
            P(("shard", "rep"), None),
            P(("shard", "rep"), None),
            P(("shard", "rep"), None),
            P(("shard", "rep"), None),
            P(("shard", "rep")),
            P(("shard", "rep")),
            P(("shard", "rep")),
        ),
        check_vma=False,
    )
```

```python
import functools
import math

import jax
import jax.numpy as jnp
from jax import lax
from jax.experimental import pallas as pl
from jax.experimental.pallas import tpu as pltpu
from jax.sharding import PartitionSpec as P

D = 2560
H = 40
HD = 64
RD = 32
QR = 768
KR = 256
FF = 6400
STEP = 10


norm_eps = 1e-05
residual_scale = 1.4 / math.sqrt(62.0)
beta_one = 0.9
beta_two = 0.95
adam_eps = 1e-08
decay_rate = 0.1
gain_rate = 0.8


def inverse_rms(values):
    return lax.rsqrt(jnp.mean(values * values, axis=-1, keepdims=True) + norm_eps)


def norm_back(incoming, operand, inv_scale):
    return inv_scale * (
        incoming
        - operand * inv_scale * inv_scale * jnp.mean(incoming * operand, axis=-1, keepdims=True)
    )


def rotation_rates():
    rates = [0.0] * LANES
    for i in range(RD // 2):
        rates[HD + i] = rates[HD + RD // 2 + i] = 10000.0 ** (-2.0 * i / RD)
    return jnp.array([rates], jnp.float32)


def own_rows(weight, gradient):
    count = gradient.shape[0]
    start = lax.axis_index("rep") * count
    return lax.dynamic_slice_in_dim(weight, start, count, 0)


def adam_step(weight, gradient, mean_old, square_old, step_rate, decay_factor):
    weight_f = own_rows(weight, gradient).astype(jnp.float32)
    gradient = gradient.astype(jnp.float32)
    mean_new = beta_one * mean_old.astype(jnp.float32) + (1.0 - beta_one) * gradient
    square_new = beta_two * square_old.astype(jnp.float32) + (1.0 - beta_two) * gradient * gradient
    ratio = (
        mean_new
        / (1.0 - beta_one**STEP)
        / (jnp.sqrt(square_new / (1.0 - beta_two**STEP)) + adam_eps)
    )
    updated = weight_f - step_rate * (ratio + decay_factor * weight_f)
    return (updated, mean_new, square_new)


TILE = 256
TAIL = 128
LANES = 128
LATENT = QR + KR + LANES
score_scale = (HD + RD) ** (-0.5)
VMEM_BYTES = 48 * 1024 * 1024


def across(a, b):
    return lax.dot_general(a, b, (((1,), (1,)), ((), ())), preferred_element_type=jnp.float32)


def along(a, b):
    return lax.dot_general(a, b, (((1,), (0,)), ((), ())), preferred_element_type=jnp.float32)


def mlp_kernel(group, tiles, tail, rows_d, order_ref, normed_ref, branch_ref, *refs):
    blocks = refs[:group]
    tails = refs[group : 2 * group]
    down_ref, down_tail_ref = refs[2 * group : 2 * group + 2]
    out_refs = refs[-9:]
    act_ref, grad_ref, sum_ref, back_ref, whole, whole_tail, down_wide, sum_acc, back_acc = out_refs
    step = pl.program_id(0)
    bf16 = jnp.bfloat16

    for j in range(group):
        start = pl.multiple_of(order_ref[j] * rows_d, 16)
        whole[pl.ds(start, rows_d), :] = blocks[j][...]

    def part(weights, down, width):
        both = along(normed_ref[...], weights)
        gate = both[:, :width]
        up = both[:, width:]
        sigmoid = 1.0 / (1.0 + jnp.exp(-gate))
        silu = gate * sigmoid
        act = (silu * up).astype(bf16)
        grad_act = across(branch_ref[...], down)
        grad_gate = grad_act * up * sigmoid * (1.0 + gate * (1.0 - sigmoid))
        grad_up = grad_act * silu
        grad = jnp.concatenate([grad_gate.astype(bf16), grad_up.astype(bf16)], axis=1)
        return act, grad, along(act, down), across(grad, weights)

    act, grad, term, back = part(whole[...], down_ref[...], TILE)
    first = pl.multiple_of(step * TILE, TILE)
    act_ref[:, pl.ds(first, TILE)] = act
    grad_ref[:, pl.ds(pl.multiple_of(2 * first, 2 * TILE), 2 * TILE)] = grad

    @pl.when(step == 0)
    def _():
        sum_acc[...] = term
        back_acc[...] = back

    @pl.when(step > 0)
    def _():
        sum_acc[...] += term
        back_acc[...] += back

    @pl.when(step == tiles - 1)
    def _():
        for j in range(group):
            start = pl.multiple_of(order_ref[j] * rows_d, 16)
            whole_tail[pl.ds(start, rows_d), :] = tails[j][...]
        down_wide[...] = jnp.zeros_like(down_wide)
        down_wide[:tail, :] = down_tail_ref[...]
        act, grad, term, back = part(whole_tail[...], down_wide[...], TAIL)
        act_ref[:, tiles * TILE :] = act
        grad_ref[:, 2 * tiles * TILE :] = grad
        sum_ref[...] = (sum_acc[...] + term).astype(bf16)
        back_ref[...] = (back_acc[...] + back).astype(bf16)


def mlp_part(order, normed, branch, own, gathered, down, earlier, index, group):
    tokens, width = normed.shape
    hidden = down.shape[0]
    tiles = hidden // TILE
    tail = hidden - tiles * TILE
    rows_d = width // group
    bf16 = jnp.bfloat16
    f32 = jnp.float32
    fixed = lambda t: (0, 0)
    weights = [own] + [gathered] * (group - 1)
    return pl.pallas_call(
        functools.partial(mlp_kernel, group, tiles, tail, rows_d),
        grid=(tiles,),
        in_specs=[
            pl.BlockSpec(memory_space=pltpu.SMEM),
            pl.BlockSpec((tokens, width), fixed),
            pl.BlockSpec((tokens, width), fixed),
        ]
        + [pl.BlockSpec((rows_d, 2 * TILE), lambda t: (0, t))]
        + [
            pl.BlockSpec((rows_d, 2 * TILE), lambda t, j=j: (0, j * tiles + t))
            for j in range(group - 1)
        ]
        + [pl.BlockSpec((rows_d, 2 * TAIL), lambda t: (0, tiles * TILE // TAIL))]
        + [
            pl.BlockSpec(
                (rows_d, 2 * TAIL), lambda t, j=j: (0, (group - 1) * tiles * TILE // TAIL + j)
            )
            for j in range(group - 1)
        ]
        + [
            pl.BlockSpec((TILE, width), lambda t: (t, 0)),
            pl.BlockSpec((tail, width), lambda t: (tiles * TILE // tail, 0)),
        ]
        + [pl.BlockSpec(memory_space=pl.ANY)] * len(earlier),
        out_specs=[
            pl.BlockSpec((tokens, tiles * TILE + TAIL), lambda t: (index, 0)),
            pl.BlockSpec((tokens, 2 * (tiles * TILE + TAIL)), lambda t: (index, 0)),
            pl.BlockSpec((tokens, width), fixed),
            pl.BlockSpec((tokens, width), fixed),
        ],
        out_shape=[
            jax.ShapeDtypeStruct((group * tokens, tiles * TILE + TAIL), bf16),
            jax.ShapeDtypeStruct((group * tokens, 2 * (tiles * TILE + TAIL)), bf16),
            jax.ShapeDtypeStruct((tokens, width), bf16),
            jax.ShapeDtypeStruct((tokens, width), bf16),
        ],
        scratch_shapes=[
            pltpu.VMEM((width, 2 * TILE), bf16),
            pltpu.VMEM((width, 2 * TAIL), bf16),
            pltpu.VMEM((TAIL, width), bf16),
            pltpu.VMEM((tokens, width), f32),
            pltpu.VMEM((tokens, width), f32),
        ],
        input_output_aliases={5 + 2 * group + i: i for i in range(len(earlier))},
        compiler_params=pltpu.CompilerParams(vmem_limit_bytes=VMEM_BYTES),
        cost_estimate=pl.CostEstimate(
            flops=12 * tokens * width * hidden,
            bytes_accessed=6 * width * hidden + 8 * tokens * width,
            transcendentals=tokens * hidden,
        ),
        name="mlp_part",
    )(order, normed, branch, *weights, *weights, down, down, *earlier)


def layer_kernel(group, base, tiles, tail, rows_d, shares, last, order_ref, *refs):
    normed_in = refs[:group]
    top_in = refs[group : 2 * group]
    at = 2 * group
    blocks = refs[at : at + group]
    at += group
    if last:
        tails = refs[at : at + group]
        at += group
        down_ref, down_tail_ref, act_old, acc_in = refs[at : at + 4]
        at += 4
    else:
        down_ref = refs[at]
        at += 1
    act_out, grad_out, back_out = refs[at : at + 3]
    normed, turned, branch, whole, acc, stage, act_stage, in_sems, out_sems, back_sem = refs[
        at + 3 : at + 13
    ]
    if last:
        whole_tail, down_wide, tail_stage, tail_act, tail_sems = refs[at + 13 :]
    bf16 = jnp.bfloat16
    f32 = jnp.float32
    step = pl.program_id(0)
    slot = lax.rem(step, 2)
    tokens = normed_in[0].shape[0]
    width = normed.shape[1]
    rows = rows_d // shares

    def arrivals():
        copies = []
        for j in range(group):
            copies.append(
                pltpu.make_async_copy(
                    normed_in[j], normed.at[pl.ds(j * tokens, tokens), :], in_sems.at[j]
                )
            )
            copies.append(
                pltpu.make_async_copy(
                    top_in[j], branch.at[pl.ds(j * tokens, tokens), :], in_sems.at[group + j]
                )
            )
        return copies

    @pl.when(step == 0)
    def _():
        copies = arrivals()
        for copy in copies:
            copy.start()
        if last:
            pltpu.make_async_copy(acc_in, acc, back_sem).start()
        else:
            acc[...] = jnp.zeros_like(acc)
        for j in range(group):
            at = pl.ds(j * tokens, tokens)
            copies[2 * j].wait()
            turned[:, j * tokens : (j + 1) * tokens] = normed[at, :].T
            copies[2 * j + 1].wait()
            branch[at, :] = (residual_scale * branch[at, :].astype(f32)).astype(bf16)
        if last:
            pltpu.make_async_copy(acc_in, acc, back_sem).wait()

    for j in range(group):
        start = pl.multiple_of(order_ref[j] * rows_d, 16)
        whole[pl.ds(start, rows_d), :] = blocks[j][...]

    def part(weights_ref, down, wide, act_to, grad_to):
        both = along(normed[...], weights_ref[...])
        gate = both[:, :wide]
        up = both[:, wide:]
        sigmoid = 1.0 / (1.0 + jnp.exp(-gate))
        silu = gate * sigmoid
        act_to[...] = (silu * up).astype(bf16)
        grad_act = across(branch[...], down)
        grad_gate = grad_act * up * sigmoid * (1.0 + gate * (1.0 - sigmoid))
        grad_up = grad_act * silu
        grad = jnp.concatenate([grad_gate.astype(bf16), grad_up.astype(bf16)], axis=1)
        cut = 512
        for c in range(width // cut):
            here = slice(c * cut, (c + 1) * cut)
            acc[:, here] += across(grad, weights_ref[here, :])
        for g in range(group):
            result = along(turned[g * rows_d : (g + 1) * rows_d, :], grad).astype(bf16)
            for r in range(shares):
                grad_to[r, g] = result[r * rows : (r + 1) * rows, :]

    def leaving(index, slot_index):
        first = pl.multiple_of((base + index) * TILE, TILE)
        return (
            pltpu.make_async_copy(
                act_stage.at[slot_index],
                act_out.at[:, pl.ds(first, TILE)],
                out_sems.at[0, slot_index],
            ),
            pltpu.make_async_copy(
                stage.at[slot_index],
                grad_out.at[:, :, :, pl.ds(pl.multiple_of(index * 2 * TILE, 2 * TILE), 2 * TILE)],
                out_sems.at[1, slot_index],
            ),
        )

    @pl.when(step >= 2)
    def _():
        for copy in leaving(step - 2, slot):
            copy.wait()

    part(whole, down_ref[...], TILE, act_stage.at[slot], stage.at[slot])
    for copy in leaving(step, slot):
        copy.start()

    @pl.when(step == tiles - 1)
    def _():
        if last:
            for j in range(group):
                start = pl.multiple_of(order_ref[j] * rows_d, 16)
                whole_tail[pl.ds(start, rows_d), :] = tails[j][...]
            down_wide[...] = jnp.zeros_like(down_wide)
            down_wide[:tail, :] = down_tail_ref[...]
            part(whole_tail, down_wide[...], TAIL, tail_act, tail_stage)
            final = [
                pltpu.make_async_copy(
                    tail_act, act_out.at[:, pl.ds((base + tiles) * TILE, TAIL)], tail_sems.at[0]
                ),
                pltpu.make_async_copy(
                    tail_stage,
                    grad_out.at[:, :, :, pl.ds(2 * tiles * TILE, 2 * TAIL)],
                    tail_sems.at[1],
                ),
            ]
            normed[...] = acc[...].astype(bf16)
            final.append(pltpu.make_async_copy(normed, back_out, back_sem))
        else:
            final = [pltpu.make_async_copy(acc, back_out, back_sem)]
        for copy in final:
            copy.start()
        for k in range(max(tiles - 2, 0), tiles):
            for copy in leaving(k, k % 2):
                copy.wait()
        for copy in final:
            copy.wait()


def layer_part(order, normed, top, own, gathered, down, earlier, tiles_from, tiles, group, shares):
    tokens, width = normed[0].shape
    hidden = down.shape[0]
    all_tiles = hidden // TILE
    tail = hidden - all_tiles * TILE
    rows_d = width // group
    rows = rows_d // shares
    bf16 = jnp.bfloat16
    f32 = jnp.float32
    last = earlier is not None
    total = group * tokens
    once = pl.Buffered(1)
    any_spec = pl.BlockSpec(memory_space=pl.ANY)
    weights = [own] + [gathered] * (group - 1)
    in_specs = [pl.BlockSpec(memory_space=pltpu.SMEM)] + [any_spec] * (2 * group)
    in_specs += [pl.BlockSpec((rows_d, 2 * TILE), lambda t: (0, tiles_from + t))]
    in_specs += [
        pl.BlockSpec((rows_d, 2 * TILE), lambda t, j=j: (0, j * all_tiles + tiles_from + t))
        for j in range(group - 1)
    ]
    inputs = [order] + normed + top + weights
    scratch = [
        pltpu.VMEM((total, width), bf16),
        pltpu.VMEM((width, total), bf16),
        pltpu.VMEM((total, width), bf16),
        pltpu.VMEM((width, 2 * TILE), bf16),
        pltpu.VMEM((total, width), f32),
        pltpu.VMEM((2, shares, group, rows, 2 * TILE), bf16),
        pltpu.VMEM((2, total, TILE), bf16),
        pltpu.SemaphoreType.DMA((2 * group,)),
        pltpu.SemaphoreType.DMA((2, 2)),
        pltpu.SemaphoreType.DMA,
    ]
    cols = 2 * tiles * TILE
    aliases = {}
    if last:
        first_tail = all_tiles * TILE // TAIL
        in_specs += [
            pl.BlockSpec((rows_d, 2 * TAIL), lambda t: (0, first_tail), pipeline_mode=once)
        ]
        in_specs += [
            pl.BlockSpec(
                (rows_d, 2 * TAIL),
                lambda t, j=j: (0, (group - 1) * first_tail + j),
                pipeline_mode=once,
            )
            for j in range(group - 1)
        ]
        inputs += weights
        cols += 2 * TAIL
    in_specs.append(pl.BlockSpec((TILE, width), lambda t: (tiles_from + t, 0)))
    inputs.append(down)
    if last:
        in_specs.append(
            pl.BlockSpec(
                (tail, width), lambda t: (all_tiles * TILE // tail, 0), pipeline_mode=once
            )
        )
        inputs.append(down)
        in_specs += [any_spec, any_spec]
        aliases = {len(inputs): 0}
        inputs += [earlier[0], earlier[2]]
        scratch += [
            pltpu.VMEM((width, 2 * TAIL), bf16),
            pltpu.VMEM((TAIL, width), bf16),
            pltpu.VMEM((shares, group, rows, 2 * TAIL), bf16),
            pltpu.VMEM((total, TAIL), bf16),
            pltpu.SemaphoreType.DMA((2,)),
        ]
    part_hidden = tiles * TILE + (tail if last else 0)
    return pl.pallas_call(
        functools.partial(
            layer_kernel, group, tiles_from, tiles, tail, rows_d, shares, last
        ),
        grid=(tiles,),
        in_specs=in_specs,
        out_specs=[any_spec] * 3,
        out_shape=[
            jax.ShapeDtypeStruct((total, all_tiles * TILE + TAIL), bf16),
            jax.ShapeDtypeStruct((shares, group, rows, cols), bf16),
            jax.ShapeDtypeStruct((total, width), bf16 if last else f32),
        ],
        scratch_shapes=scratch,
        input_output_aliases=aliases,
        compiler_params=pltpu.CompilerParams(vmem_limit_bytes=61 * 1024 * 1024),
        cost_estimate=pl.CostEstimate(
            flops=14 * total * width * part_hidden,
            bytes_accessed=12 * width * part_hidden + 16 * total * width,
            transcendentals=total * part_hidden,
        ),
        name="layer_part",
    )(*inputs)


def down_grad_kernel(group, tokens, act_ref, *refs):
    top = refs[:group]
    out_ref, whole = refs[group:]

    @pl.when(pl.program_id(0) == 0)
    def _():
        for j in range(group):
            whole[j * tokens : (j + 1) * tokens, :] = (
                residual_scale * top[j][...].astype(jnp.float32)
            ).astype(jnp.bfloat16)

    out_ref[...] = along(act_ref[...].T, whole[...]).astype(jnp.bfloat16)


def down_grad(act_all, top_parts, hidden, group):
    tokens, width = top_parts[0].shape
    tiles = (hidden + TILE - 1) // TILE
    return pl.pallas_call(
        functools.partial(down_grad_kernel, group, tokens),
        grid=(tiles,),
        in_specs=[pl.BlockSpec((group * tokens, TILE), lambda t: (0, t))]
        + [pl.BlockSpec((tokens, width), lambda t: (0, 0))] * group,
        out_specs=pl.BlockSpec((TILE, width), lambda t: (t, 0)),
        out_shape=jax.ShapeDtypeStruct((hidden, width), jnp.bfloat16),
        scratch_shapes=[pltpu.VMEM((group * tokens, width), jnp.bfloat16)],
        compiler_params=pltpu.CompilerParams(vmem_limit_bytes=VMEM_BYTES),
        cost_estimate=pl.CostEstimate(
            flops=2 * group * tokens * width * hidden,
            bytes_accessed=2 * width * hidden + 2 * group * tokens * (width + hidden),
            transcendentals=0,
        ),
        name="down_grad",
    )(act_all, *top_parts)


def lane_index(rows):
    return lax.broadcasted_iota(jnp.int32, (rows, LANES), 1)


def turn(values, table_ref, sign):
    ahead = pltpu.roll(values, LANES - RD // 2, 1)
    behind = pltpu.roll(values, RD // 2, 1)
    return values * table_ref[0] + sign * (ahead * table_ref[1] + behind * table_ref[2])


def seg_column(seg_ref):
    return seg_ref[...].T[:, :1]


def causal_mask(seg_ref):
    tokens = seg_ref.shape[1]
    row = lax.broadcasted_iota(jnp.int32, (tokens, tokens), 0)
    col = lax.broadcasted_iota(jnp.int32, (tokens, tokens), 1)
    return (seg_column(seg_ref) == seg_ref[:1, :]) & (col <= row)


def softmax_rows(query, key, allowed):
    scores = across(query, key) * score_scale
    masked = jnp.where(allowed, scores, -1e30)
    exponent = jnp.exp(masked - jnp.max(masked, axis=1, keepdims=True))
    return exponent * (1.0 / jnp.sum(exponent, axis=1, keepdims=True))


def key_lanes(keyval, latent_ref, lane):
    return jnp.where(lane < HD, keyval, latent_ref[:, QR + KR :])


def attend_kernel(
    heads,
    latent_ref,
    table_ref,
    seg_ref,
    query_w_ref,
    keyval_w_ref,
    out_w_ref,
    term_ref,
    query_ref,
    keyval_ref,
    mixed_ref,
):
    bf16 = jnp.bfloat16
    tokens = latent_ref.shape[0]
    lane = lane_index(tokens)
    allowed = causal_mask(seg_ref)
    query = along(latent_ref[:, :QR], query_w_ref[...])
    keyval_ref[...] = along(latent_ref[:, QR : QR + KR], keyval_w_ref[...]).astype(bf16)
    even = None
    for h in range(heads):
        at = slice(h * LANES, (h + 1) * LANES)
        query_h = turn(query[:, at], table_ref, 1.0).astype(bf16)
        query_ref[:, at] = query_h
        keyval_h = keyval_ref[:, at]
        probs = softmax_rows(query_h, key_lanes(keyval_h, latent_ref, lane), allowed).astype(bf16)
        mixed = along(probs, keyval_h)
        if h % 2 == 0:
            even = pltpu.roll(mixed, HD, 1)
            if h == heads - 1:
                mixed_ref[:, h * HD :] = even[:, :HD].astype(bf16)
        else:
            mixed_ref[:, (h - 1) * HD : (h + 1) * HD] = jnp.where(lane < HD, even, mixed).astype(
                bf16
            )
    term_ref[...] = along(mixed_ref[...], out_w_ref[...]).astype(bf16)


def nth(array, index):
    return pl.BlockSpec((None,) + array.shape[1:], lambda i: (index,) + (0,) * (array.ndim - 1))


def entire(array):
    return pl.BlockSpec(array.shape, lambda i: (0,) * array.ndim)


def attend(index, latent, table, seg, query_w, keyval_w, out_w):
    tokens = latent.shape[1]
    heads = query_w.shape[1] // LANES
    width = out_w.shape[1]
    bf16 = jnp.bfloat16
    return pl.pallas_call(
        functools.partial(attend_kernel, heads),
        grid=(1,),
        out_specs=[
            pl.BlockSpec((tokens, cols), lambda i: (0, 0))
            for cols in (width, heads * LANES, heads * LANES, heads * HD)
        ],
        in_specs=[nth(array, index) for array in (latent, table, seg)]
        + [entire(array) for array in (query_w, keyval_w, out_w)],
        out_shape=[
            jax.ShapeDtypeStruct((tokens, width), bf16),
            jax.ShapeDtypeStruct((tokens, heads * LANES), bf16),
            jax.ShapeDtypeStruct((tokens, heads * LANES), bf16),
            jax.ShapeDtypeStruct((tokens, heads * HD), bf16),
        ],
        compiler_params=pltpu.CompilerParams(vmem_limit_bytes=VMEM_BYTES),
        cost_estimate=pl.CostEstimate(
            flops=2 * tokens * (heads * LANES * (QR + KR + 2 * tokens) + heads * HD * width),
            bytes_accessed=2 * (heads * LANES * (QR + KR) + heads * HD * width + tokens * width),
            transcendentals=heads * tokens * tokens,
        ),
        name="attend",
    )(latent, table, seg, query_w, keyval_w, out_w)


def attend_back_kernel(
    heads,
    grad_ref,
    query_ref,
    keyval_ref,
    latent_ref,
    table_ref,
    seg_ref,
    query_w_ref,
    keyval_w_ref,
    out_w_ref,
    term_ref,
    grad_query_ref,
    grad_keyval_ref,
):
    bf16 = jnp.bfloat16
    f32 = jnp.float32
    tokens = latent_ref.shape[0]
    lane = lane_index(tokens)
    allowed = causal_mask(seg_ref)
    grad_mixed = across(grad_ref[...], out_w_ref[...])
    grad_rope = jnp.zeros((tokens, LANES), f32)
    for h in range(heads):
        at = slice(h * LANES, (h + 1) * LANES)
        query_h = query_ref[:, at]
        keyval_h = keyval_ref[:, at]
        key_h = key_lanes(keyval_h, latent_ref, lane)
        probs = softmax_rows(query_h, key_h, allowed)
        if h % 2 == 0:
            if h == heads - 1:
                one = jnp.concatenate([grad_mixed[:, h * HD :]] * 2, axis=1)
            else:
                pair = grad_mixed[:, h * HD : (h + 2) * HD]
                one = pltpu.roll(pair, HD, 1)
        else:
            one = pair
        value_grad = jnp.where(lane >= HD, one, 0.0).astype(bf16)
        turned = probs.astype(bf16).T
        grad_values = along(turned, value_grad)
        grad_probs = across(value_grad, keyval_h)
        delta = jnp.sum(probs * grad_probs, axis=1, keepdims=True)
        grad_scores = (probs * (grad_probs - delta)).astype(bf16)
        grad_q = along(grad_scores, key_h) * score_scale
        grad_k = along(grad_scores.T, query_h) * score_scale
        grad_query_ref[:, at] = turn(grad_q, table_ref, -1.0).astype(bf16)
        grad_keyval_ref[:, at] = jnp.where(lane < HD, grad_k, grad_values).astype(bf16)
        grad_rope = grad_rope + grad_k
    rope = jnp.where(lane >= HD, turn(grad_rope, table_ref, -1.0), 0.0)
    term_ref[:, :QR] = across(grad_query_ref[...], query_w_ref[...]).astype(bf16)
    term_ref[:, QR : QR + KR] = across(grad_keyval_ref[...], keyval_w_ref[...]).astype(bf16)
    term_ref[:, QR + KR :] = rope.astype(bf16)


def attend_back(
    index, grad, query, keyval, latent, table, seg, query_w, keyval_w, out_w
):
    tokens = latent.shape[1]
    heads = query_w.shape[1] // LANES
    width = out_w.shape[1]
    bf16 = jnp.bfloat16
    return pl.pallas_call(
        functools.partial(attend_back_kernel, heads),
        grid=(1,),
        out_specs=[
            pl.BlockSpec((tokens, cols), lambda i: (0, 0))
            for cols in (LATENT, heads * LANES, heads * LANES)
        ],
        in_specs=[entire(array) for array in (grad, query, keyval)]
        + [nth(array, index) for array in (latent, table, seg)]
        + [entire(array) for array in (query_w, keyval_w, out_w)],
        out_shape=[
            jax.ShapeDtypeStruct((tokens, LATENT), bf16),
            jax.ShapeDtypeStruct((tokens, heads * LANES), bf16),
            jax.ShapeDtypeStruct((tokens, heads * LANES), bf16),
        ],
        compiler_params=pltpu.CompilerParams(vmem_limit_bytes=VMEM_BYTES),
        cost_estimate=pl.CostEstimate(
            flops=2 * tokens * (heads * LANES * (QR + KR + 5 * tokens) + heads * HD * width),
            bytes_accessed=2 * (heads * LANES * (QR + KR) + heads * HD * width + tokens * width),
            transcendentals=heads * tokens * tokens,
        ),
        name="attend_back",
    )(grad, query, keyval, latent, table, seg, query_w, keyval_w, out_w)


def token_grad_kernel(count, *refs):
    left = refs[:count]
    right = refs[count : 2 * count]
    out_ref, turned, whole = refs[2 * count :]
    tokens = left[0].shape[0]
    for j in range(count):
        turned[:, j * tokens : (j + 1) * tokens] = left[j][...].T
        whole[j * tokens : (j + 1) * tokens, :] = right[j][...]
    out_ref[...] = along(turned[...], whole[...]).astype(jnp.bfloat16)


def token_grad(left, right, first, rows, name):
    count = len(right)
    tokens, cols = right[0].shape
    at = first // rows
    if isinstance(left, list):
        left_specs = [pl.BlockSpec((tokens, rows), lambda i: (0, at))] * count
    else:
        left_specs = [
            pl.BlockSpec((None, tokens, rows), lambda i, j=j: (j, 0, at)) for j in range(count)
        ]
        left = [left] * count
    return pl.pallas_call(
        functools.partial(token_grad_kernel, count),
        grid=(1,),
        in_specs=left_specs + [pl.BlockSpec((tokens, cols), lambda i: (0, 0))] * count,
        out_specs=pl.BlockSpec((rows, cols), lambda i: (0, 0)),
        out_shape=jax.ShapeDtypeStruct((rows, cols), jnp.bfloat16),
        scratch_shapes=[
            pltpu.VMEM((rows, count * tokens), jnp.bfloat16),
            pltpu.VMEM((count * tokens, cols), jnp.bfloat16),
        ],
        compiler_params=pltpu.CompilerParams(vmem_limit_bytes=VMEM_BYTES),
        cost_estimate=pl.CostEstimate(
            flops=2 * count * tokens * rows * cols,
            bytes_accessed=2 * (rows * cols + count * tokens * (rows + cols)),
            transcendentals=0,
        ),
        name=name,
    )(*left, *right)


MESH = pl.DeviceIdType.MESH


def partner(me, distance):
    bit = 1
    while bit <= distance:
        if distance & bit:
            me = me + bit - 2 * bit * lax.rem(lax.div(me, bit), 2)
        bit *= 2
    return me


def greet(peers, count):
    barrier = pltpu.get_barrier_semaphore()
    for peer in peers:
        pl.semaphore_signal(barrier, inc=1, device_id=peer, device_id_type=MESH)
    pl.semaphore_wait(barrier, count)


def send(src, dst, sems, index, peer):
    copy = pltpu.make_async_remote_copy(
        src_ref=src,
        dst_ref=dst,
        send_sem=sems.at[0, index],
        recv_sem=sems.at[1, index],
        device_id=peer,
        device_id_type=MESH,
    )
    copy.start()
    return copy


def tile_format(gate, up, store, tiles, tail):
    bf16 = jnp.bfloat16
    for t in range(tiles):
        store(2 * t * TILE, gate[:, t * TILE : (t + 1) * TILE].astype(bf16))
        store((2 * t + 1) * TILE, up[:, t * TILE : (t + 1) * TILE].astype(bf16))
    lane = lax.broadcasted_iota(jnp.int32, (gate.shape[0], TAIL), 1)
    for second, values in enumerate((gate, up)):
        last = values[:, tiles * TILE : tiles * TILE + TAIL]
        store(
            2 * tiles * TILE + second * TAIL, jnp.where(lane < tail, last, 0.0).astype(bf16)
        )


def head_table(seg_ref, rates_ref, table_ref):
    tokens = seg_ref.shape[1]
    row = lax.broadcasted_iota(jnp.int32, (tokens, tokens), 0)
    col = lax.broadcasted_iota(jnp.int32, (tokens, tokens), 1)
    before = (seg_column(seg_ref) == seg_ref[:1, :]) & (col < row)
    position = jnp.sum(jnp.where(before, 1.0, 0.0), axis=1, keepdims=True)
    angles = position * rates_ref[...]
    sine = jnp.sin(angles)
    lane = lane_index(tokens)
    middle = HD + RD // 2
    end = HD + RD
    table_ref[0] = jnp.where(lane < end, jnp.cos(angles), 0.0)
    table_ref[1] = jnp.where((lane >= HD) & (lane < middle), -sine, 0.0)
    table_ref[2] = jnp.where((lane >= middle) & (lane < end), sine, 0.0)


def share_small(group, me, peers, gains_ref, seg_ref, gains_all_ref, segs_ref, sems):
    mine = pl.ds(pl.multiple_of(me * 8, 8), 8)
    gains_all_ref[mine, :] = gains_ref[...]
    segs_ref[0] = seg_ref[...]
    copies = []
    for j in range(1, group):
        copies.append(send(gains_ref, gains_all_ref.at[mine, :], sems, 2 * (j - 1), peers[j - 1]))
        copies.append(send(seg_ref, segs_ref.at[j], sems, 2 * (j - 1) + 1, peers[j - 1]))
    return copies


def small_kernel(
    group, gains_ref, seg_ref, rates_ref, gains_all_ref, segs_ref, table_ref, small_sems
):
    me = lax.axis_index("shard")
    rep = lax.axis_index("rep")
    peers = [(partner(me, j), rep) for j in range(1, group)]
    greet(peers, group - 1)
    for copy in share_small(group, me, peers, gains_ref, seg_ref, gains_all_ref, segs_ref, small_sems):
        copy.wait()
    for j in range(group):
        head_table(segs_ref.at[j], rates_ref, table_ref.at[j])


def columns_kernel(
    group,
    replicas,
    hidden,
    slab,
    gate_up_ref,
    gains_ref,
    seg_ref,
    rates_ref,
    own_ref,
    pieces_ref,
    gains_all_ref,
    segs_ref,
    table_ref,
    own_slab,
    slabs,
    out_pieces,
    local_sems,
    sems,
    small_sems,
):
    me = lax.axis_index("shard")
    rep = lax.axis_index("rep")
    rows, share = own_slab.shape[1], slabs.shape[1]
    tiles = hidden // TILE
    tail = hidden - tiles * TILE
    main = 2 * tiles * TILE

    def begin(index, second):
        offset = index * hidden
        return pl.multiple_of(second * FF + offset - lax.rem(offset, LANES), LANES)

    loads = []
    for j in range(1, group):
        for second in range(2):
            at = 2 * (j - 1) + second
            copy = pltpu.make_async_copy(
                gate_up_ref.at[
                    pl.ds(pl.multiple_of(rep * share, 16), share), pl.ds(begin(partner(me, j), second), slab)
                ],
                slabs.at[at],
                local_sems.at[at],
            )
            copy.start()
            loads.append(copy)
    for second in range(2):
        at = 2 * (group - 1) + second
        copy = pltpu.make_async_copy(
            gate_up_ref.at[:, pl.ds(begin(me, second), slab)],
            own_slab.at[second],
            local_sems.at[at],
        )
        copy.start()
        loads.append(copy)
    peers = [(partner(me, j), rep) for j in range(1, group)]
    greet(peers, group - 1)
    small = share_small(group, me, peers, gains_ref, seg_ref, gains_all_ref, segs_ref, small_sems)

    def shifted(ref, index):
        amount = lax.rem(slab - lax.rem(index * hidden, LANES), slab)
        return pltpu.roll(ref[...].astype(jnp.float32), amount, 1)

    sent = []
    for j in range(1, group):
        for second in range(2):
            loads[2 * (j - 1) + second].wait()

        def store(first, values, j=j):
            out_pieces[j - 1, :, first : first + values.shape[1]] = values

        tile_format(
            shifted(slabs.at[2 * (j - 1)], partner(me, j)),
            shifted(slabs.at[2 * (j - 1) + 1], partner(me, j)),
            store,
            tiles,
            tail,
        )
        sent.append(
            send(
                out_pieces.at[j - 1, :, pl.ds(0, main)],
                pieces_ref.at[:, pl.ds((j - 1) * main, main)],
                sems,
                2 * (j - 1),
                peers[j - 1],
            )
        )
        sent.append(
            send(
                out_pieces.at[j - 1, :, pl.ds(main, 2 * TAIL)],
                pieces_ref.at[:, pl.ds((group - 1) * main + (j - 1) * 2 * TAIL, 2 * TAIL)],
                sems,
                2 * (j - 1) + 1,
                peers[j - 1],
            )
        )
    for second in range(2):
        loads[2 * (group - 1) + second].wait()

    def store_own(first, values):
        own_ref[:, first : first + values.shape[1]] = values

    tile_format(
        shifted(own_slab.at[0], me), shifted(own_slab.at[1], me), store_own, tiles, tail
    )
    for copy in small:
        copy.wait()
    for j in range(group):
        head_table(segs_ref.at[j], rates_ref, table_ref.at[j])
    for copy in sent:
        copy.wait()


def small_shapes(gains, seg, group):
    rows, tokens = seg.shape
    f32 = jnp.float32
    return [
        jax.ShapeDtypeStruct((group * rows, gains.shape[1]), f32),
        jax.ShapeDtypeStruct((group, rows, tokens), f32),
        jax.ShapeDtypeStruct((group, 3, tokens, LANES), f32),
    ]


def small_things(gains, seg, group):
    return pl.pallas_call(
        functools.partial(small_kernel, group),
        in_specs=[pl.BlockSpec(memory_space=pltpu.VMEM)] * 3,
        out_specs=[pl.BlockSpec(memory_space=pltpu.VMEM)] * 3,
        out_shape=small_shapes(gains, seg, group),
        scratch_shapes=[pltpu.SemaphoreType.DMA((2, 2 * (group - 1)))],
        compiler_params=pltpu.CompilerParams(
            collective_id=3, has_side_effects=True, vmem_limit_bytes=VMEM_BYTES
        ),
        name="small_things",
    )(gains, seg, rotation_rates())


def hidden_pieces(gate_up, gains, seg, group, replicas):
    rows = gate_up.shape[0]
    share = rows // replicas
    hidden = FF // group
    whole = 2 * (hidden // TILE * TILE + TAIL)
    slab = -(-(hidden + LANES - math.gcd(hidden, LANES)) // LANES) * LANES
    bf16 = jnp.bfloat16
    others = group - 1
    return pl.pallas_call(
        functools.partial(columns_kernel, group, replicas, hidden, slab),
        in_specs=[pl.BlockSpec(memory_space=pl.ANY)] + [pl.BlockSpec(memory_space=pltpu.VMEM)] * 3,
        out_specs=[pl.BlockSpec(memory_space=pltpu.VMEM)] * 5,
        out_shape=[
            jax.ShapeDtypeStruct((rows, whole), bf16),
            jax.ShapeDtypeStruct((share, others * whole), bf16),
        ]
        + small_shapes(gains, seg, group),
        scratch_shapes=[
            pltpu.VMEM((2, rows, slab), bf16),
            pltpu.VMEM((2 * others, share, slab), bf16),
            pltpu.VMEM((others, share, whole), bf16),
            pltpu.SemaphoreType.DMA((2 * group,)),
            pltpu.SemaphoreType.DMA((2, 2 * others)),
            pltpu.SemaphoreType.DMA((2, 2 * others)),
        ],
        compiler_params=pltpu.CompilerParams(
            collective_id=1, has_side_effects=True, vmem_limit_bytes=VMEM_BYTES
        ),
        cost_estimate=pl.CostEstimate(flops=0, bytes_accessed=100_000_000, transcendentals=0),
        name="hidden_pieces",
    )(gate_up, gains, seg, rotation_rates())


def latent_kernel(
    group,
    tokens_ref,
    gains_ref,
    latent_gains_ref,
    table_ref,
    latent_proj_ref,
    query_ref,
    keyval_ref,
    parts_ref,
    rows_ref,
    normed_ref,
    latent_w_ref,
    query_w_ref,
    keyval_w_ref,
    local_sems,
    fetch_sems,
    swap_sems,
    weight_sems,
    weight_swap_sems,
    part_sems,
):
    f32 = jnp.float32
    bf16 = jnp.bfloat16
    me = lax.axis_index("shard")
    rep = lax.axis_index("rep")
    core = lax.rem(rep, 2)
    tokens = tokens_ref.shape[0]
    rows_d = latent_proj_ref.shape[0]
    half = rows_d // 2
    query_rows = query_ref.shape[0]
    keyval_rows = keyval_ref.shape[0]
    width = query_w_ref.shape[1]
    others = range(1, group)
    peers = [None] + [(partner(me, j), rep) for j in others]
    sibling = (me, rep + 1 - 2 * core)
    greet(peers[1:] + [sibling], group)

    def block(index, which):
        return pl.ds(pl.multiple_of(index * rows_d + which * half, 16), half)

    fetched = [None] + [
        send(
            latent_proj_ref.at[pl.ds(pl.multiple_of(core * half, 16), half), :],
            latent_w_ref.at[block(me, core), :],
            fetch_sems,
            j - 1,
            peers[j],
        )
        for j in others
    ]
    own = pltpu.make_async_copy(
        latent_proj_ref,
        latent_w_ref.at[pl.ds(pl.multiple_of(me * rows_d, 16), rows_d), :],
        local_sems.at[0],
    )
    own.start()
    kinds = ((query_ref, query_w_ref, query_rows), (keyval_ref, keyval_w_ref, keyval_rows))

    def weight_rows(index, rows):
        return pl.ds(pl.multiple_of(index * rows + core * (rows // 2), 16), rows // 2)

    def fetch_weights():
        return [
            send(
                ref.at[
                    pl.ds(pl.multiple_of(core * (rows // 2), 16), rows // 2),
                    pl.ds(pl.multiple_of(partner(me, j) * width, LANES), width),
                ],
                out_ref.at[weight_rows(me, rows), :],
                weight_sems,
                kind * (group - 1) + j - 1,
                peers[j],
            )
            for kind, (ref, out_ref, rows) in enumerate(kinds)
            for j in others
        ]

    def swap_weights(copies):
        swaps = []
        for kind, (ref, out_ref, rows) in enumerate(kinds):
            for j in others:
                index = kind * (group - 1) + j - 1
                copies[index].wait_recv()
                where = weight_rows(partner(me, j), rows)
                swaps.append(
                    send(
                        out_ref.at[where, :],
                        out_ref.at[where, :],
                        weight_swap_sems,
                        index,
                        sibling,
                    )
                )
        return swaps

    mine = []
    for at, (ref, out_ref, rows) in enumerate(kinds):
        copy = pltpu.make_async_copy(
            ref.at[:, pl.ds(pl.multiple_of(me * width, LANES), width)],
            out_ref.at[pl.ds(pl.multiple_of(me * rows, 16), rows), :],
            local_sems.at[1 + at],
        )
        copy.start()
        mine.append(copy)

    rows_in = tokens_ref[...].astype(f32)
    scale = lax.rsqrt(jnp.mean(rows_in * rows_in, axis=1, keepdims=True) + norm_eps)
    normed_ref[...] = (rows_in * scale * gains_ref[...]).astype(bf16)

    swaps = []
    for j in others:
        fetched[j].wait_recv()
        where = block(partner(me, j), core)
        swaps.append(
            send(latent_w_ref.at[where, :], latent_w_ref.at[where, :], swap_sems, j - 1, sibling)
        )
    weights = fetch_weights()
    own.wait()
    for copy in swaps:
        copy.wait()
    for j in others:
        fetched[j].wait_send()
    latent = along(normed_ref[...], latent_w_ref[...])
    rows_ref[...] = latent

    def rms(values):
        return values * lax.rsqrt(jnp.mean(values * values, axis=1, keepdims=True) + norm_eps)

    query = rms(latent[:, :QR]) * latent_gains_ref[:, :QR]
    keyval = rms(latent[:, QR : QR + KR]) * latent_gains_ref[:, QR:]
    rope = latent[:, QR + KR :]
    wide = jnp.concatenate(
        [jnp.zeros((tokens, HD), f32), rope, jnp.zeros((tokens, LANES - HD - RD), f32)], axis=1
    )
    parts_ref[0, :, :QR] = query.astype(bf16)
    parts_ref[0, :, QR : QR + KR] = keyval.astype(bf16)
    parts_ref[0, :, QR + KR :] = turn(wide, table_ref, 1.0).astype(bf16)

    direct = (1, 2) if group == 4 else others
    near = [
        send(parts_ref.at[0], parts_ref.at[j], part_sems, j - 1, peers[j]) for j in direct
    ]
    swaps = swap_weights(weights)
    far = []
    if group == 4:
        part = tokens // 2
        top = pl.ds(0, part)
        low = pl.ds(part, part)
        near[0].wait_recv()
        far.append(send(parts_ref.at[1, top], parts_ref.at[3, top], part_sems, 2, peers[2]))
        near[1].wait_recv()
        far.append(send(parts_ref.at[2, low], parts_ref.at[3, low], part_sems, 3, peers[1]))
        for copy in near:
            copy.wait_send()
    else:
        for copy in near:
            copy.wait()
    for copy in far + swaps + mine:
        copy.wait()
    for copy in weights:
        copy.wait_send()


def latent_front(tokens, gain_in, latent_gains, table, latent_proj, query_pad, keyval, group):
    rows = tokens.shape[0]
    heads = query_pad.shape[1] // LANES // group
    bf16 = jnp.bfloat16
    others = group - 1
    dma = pltpu.SemaphoreType.DMA
    width = latent_proj.shape[1]
    return pl.pallas_call(
        functools.partial(latent_kernel, group),
        in_specs=[pl.BlockSpec(memory_space=pltpu.VMEM)] * 7,
        out_specs=[pl.BlockSpec(memory_space=pltpu.VMEM)] * 6,
        out_shape=[
            jax.ShapeDtypeStruct((group, rows, LATENT), bf16),
            jax.ShapeDtypeStruct((rows, width), jnp.float32),
            jax.ShapeDtypeStruct((rows, D), bf16),
            jax.ShapeDtypeStruct((D, width), bf16),
            jax.ShapeDtypeStruct((QR, heads * LANES), bf16),
            jax.ShapeDtypeStruct((KR, heads * LANES), bf16),
        ],
        scratch_shapes=[
            dma((3,)),
            dma((2, others)),
            dma((2, others)),
            dma((2, 2 * others)),
            dma((2, 2 * others)),
            dma((2, max(others, 4))),
        ],
        compiler_params=pltpu.CompilerParams(
            collective_id=2, has_side_effects=True, vmem_limit_bytes=VMEM_BYTES
        ),
        cost_estimate=pl.CostEstimate(
            flops=2 * rows * D * width, bytes_accessed=60_000_000, transcendentals=0
        ),
        name="latent_front",
    )(tokens, gain_in, latent_gains, table, latent_proj, query_pad, keyval)


def hop(array, group, distance):
    return lax.ppermute(array, "shard", [(i, i ^ distance) for i in range(group)])


def near_blocks(array, group):
    return [hop(array, group, j) for j in ((1, 2) if group == 4 else range(1, group))]


def all_blocks(array, near, group):
    if group != 4:
        return [array] + near
    half = array.shape[0] // 2
    far_top = hop(near[0][:half], group, 2)
    far_low = hop(near[1][half:], group, 1)
    return [array] + near + [jnp.concatenate([far_top, far_low], axis=0)]


def gather_blocks(array, group):
    return all_blocks(array, near_blocks(array, group), group)


def scatter_sum(parts, group):
    low = jnp.bfloat16
    f32 = jnp.float32
    total = parts[0].astype(f32)
    if group != 4:
        for j in range(1, group):
            total = total + hop(parts[j], group, j).astype(f32)
        return total
    half = parts[0].shape[0] // 2
    top = hop(parts[3][:half], group, 1)
    bottom = hop(parts[3][half:], group, 2)

    def add(left, right):
        return (left.astype(f32) + right.astype(f32)).astype(low)

    two = jnp.concatenate([add(parts[2][:half], top), parts[2][half:]], axis=0)
    one = jnp.concatenate([parts[1][:half], add(parts[1][half:], bottom)], axis=0)
    return total + hop(one, group, 1).astype(f32) + hop(two, group, 2).astype(f32)


def place(blocks, me):
    rows = blocks[0].shape[0]
    whole = jnp.zeros((rows * len(blocks),) + blocks[0].shape[1:], blocks[0].dtype)
    for j, block in enumerate(blocks):
        whole = lax.dynamic_update_slice_in_dim(whole, block, (me ^ j) * rows, 0)
    return whole


def pick(whole, me, group):
    rows = whole.shape[0] // group
    return [lax.dynamic_slice_in_dim(whole, (me ^ j) * rows, rows, 0) for j in range(group)]


def columns(array, index, width):
    return lax.dynamic_slice_in_dim(array, index * width, width, 1)


def per_device(
    group,
    replicas,
    tokens,
    segments,
    cotangent,
    latent_proj,
    query_up,
    keyval_up,
    out_proj,
    gate_up,
    down_proj,
    norm_gains,
    latent_mean,
    query_mean,
    keyval_mean,
    outproj_mean,
    gateup_mean,
    down_mean,
    gains_mean,
    latent_square,
    query_square,
    keyval_square,
    outproj_square,
    gateup_square,
    down_square,
    gains_square,
):
    f32 = jnp.float32
    bf16 = jnp.bfloat16
    me = lax.axis_index("shard")
    rep = lax.axis_index("rep")
    seq_len = tokens.shape[0]
    heads = H // group
    hidden_part = FF // group
    tiles = hidden_part // TILE
    tail = hidden_part - tiles * TILE
    rows_d = D // group
    others = range(1, group)
    order = jnp.stack([me ^ j for j in range(group)]).astype(jnp.int32)

    share = rows_d // replicas
    fast = group == 4 and share % 16 == 0
    gains_rows = jnp.broadcast_to(norm_gains.astype(f32), (8,) + norm_gains.shape)
    seg_rows = jnp.broadcast_to(segments.astype(f32), (8, seq_len))
    query_pad = jnp.pad(
        query_up.reshape(-1, H, HD + RD), ((0, 0), (0, 0), (0, LANES - HD - RD))
    ).reshape(-1, H * LANES)

    def hidden_columns(array, index):
        gate = columns(array, index, hidden_part)
        up = lax.dynamic_slice_in_dim(array, FF + index * hidden_part, hidden_part, 1)
        cut = []
        for t in range(tiles):
            cut += [gate[:, t * TILE : (t + 1) * TILE], up[:, t * TILE : (t + 1) * TILE]]
        for last in (gate, up):
            cut.append(jnp.pad(last[:, tiles * TILE :], ((0, 0), (0, TAIL - tail))))
        return jnp.concatenate(cut, axis=1)

    share = rows_d // replicas
    cot_near = near_blocks(cotangent, group)
    if share % 16 == 0:
        own_columns, pieces, gains_all, segs, tables = hidden_pieces(
            gate_up, gains_rows, seg_rows, group, replicas
        )
    else:
        gains_all, segs, tables = small_things(gains_rows, seg_rows, group)
        own_share = lax.dynamic_slice_in_dim(gate_up, rep * share, share, 0)
        own_columns = hidden_columns(gate_up, me)
        main = 2 * tiles * TILE
        pieces = [hop(hidden_columns(own_share, me ^ j), group, j) for j in others]
        pieces = jnp.concatenate(
            [piece[:, :main] for piece in pieces] + [piece[:, main:] for piece in pieces], axis=1
        )
    gathered_columns = lax.all_gather(pieces, "rep", axis=0, tiled=True)
    gains_f = gains_all.reshape(group, 8, -1)[:, 0, :].reshape(-1)
    gain_in = gains_f[:D]
    gain_query = gains_f[D : D + QR]
    gain_keyval = gains_f[D + QR : D + QR + KR]
    gain_mlp = gains_f[D + QR + KR :]

    latent_late, _ = lax.optimization_barrier((latent_proj, pieces))
    latent_parts, latent_all, normed_in, latent_w, query_w, keyval_w = latent_front(
        tokens,
        gain_in.reshape(1, D),
        gains_f[D : D + QR + KR].reshape(1, QR + KR),
        tables[0],
        latent_late,
        query_pad,
        keyval_up,
        group,
    )
    rows_in = tokens.astype(f32)
    inv_in = inverse_rms(rows_in)
    query_lat = latent_all[:, :QR]
    keyval_lat = latent_all[:, QR : QR + KR]
    inv_query = inverse_rms(query_lat)
    inv_keyval = inverse_rms(keyval_lat)

    attention = [None] * group
    latents_next = latent_parts
    for at, j in enumerate((*reversed(others), 0)):
        if at == 0:
            latents_next, cot_near = lax.optimization_barrier((latents_next, cot_near))
            cot_parts = all_blocks(cotangent, cot_near, group)
        if at == 1:
            latents_next, cot_parts = lax.optimization_barrier((latents_next, cot_parts))
        attention[j] = attend(j, latents_next, tables, segs, query_w, keyval_w, out_proj)
        latents_next, _ = lax.optimization_barrier((latent_parts, attention[j][0]))
    out_terms = [part[0] for part in attention]
    hidden = rows_in + residual_scale * scatter_sum(out_terms, group)
    inv_hidden = inverse_rms(hidden)
    normed_mlp = (hidden * inv_hidden * gain_mlp).astype(bf16)

    near = near_blocks(normed_mlp, group)
    half_tiles = tiles // 2
    if fast:
        mlp_parts = all_blocks(normed_mlp, near, group)

        def some_tiles(earlier, first, count):
            return layer_part(
                order,
                mlp_parts,
                cot_parts,
                own_columns,
                gathered_columns,
                down_proj,
                earlier,
                first,
                count,
                group,
                replicas,
            )

        early = some_tiles(None, 0, half_tiles)
        act_all, grad_late, back_all = some_tiles(early, half_tiles, tiles - half_tiles)
        cuts = [(0, half_tiles), (half_tiles, tiles)]
        grad_cuts = [early[1].reshape(D, -1), grad_late.reshape(D, -1)]
        hidden_terms = [back_all[j * seq_len : (j + 1) * seq_len] for j in range(group)]
    else:
        branch_parts = [(residual_scale * part.astype(f32)).astype(bf16) for part in cot_parts]

        def mlp_block(j, normed, earlier):
            return mlp_part(
                order,
                normed,
                branch_parts[j],
                own_columns,
                gathered_columns,
                down_proj,
                earlier,
                j,
                group,
            )

        first = mlp_block(0, normed_mlp, ())
        near, first = lax.optimization_barrier((near, first))
        mlp_parts = all_blocks(normed_mlp, near, group)
        terms = [first]
        for j in others:
            terms.append(mlp_block(j, mlp_parts[j], terms[-1][:2]))
        act_all, grad_all = terms[-1][:2]
        down_terms = [term[2] for term in terms]
        hidden_terms = [term[3] for term in terms]
        cuts = [(0, tiles)]
        grad_gateup = jnp.einsum(
            "td,tf->df", jnp.concatenate(mlp_parts), grad_all, preferred_element_type=f32
        )
        grad_cuts = [
            grad_gateup.astype(bf16)
            .reshape(group, replicas, share, -1)
            .transpose(1, 0, 2, 3)
            .reshape(D, -1)
        ]
    normed_late, _ = lax.optimization_barrier((normed_in, mlp_parts[1:]))
    normed_columns = [columns(normed_late, me, rows_d)] + [
        hop(columns(normed_late, me ^ j, rows_d), group, j) for j in others
    ]
    grad_normed_mlp = scatter_sum(hidden_terms, group)

    grad_down = down_grad(act_all, cot_parts, hidden_part, group)

    def to_owner_rows(block_rows):
        blocks = pick(block_rows, me, group)
        blocks = [blocks[0]] + [hop(blocks[j], group, j) for j in others]
        return place(blocks, me).reshape((group,) + blocks[0].shape)

    summed = [lax.psum_scatter(grad_cuts[0], "rep", scatter_dimension=0, tiled=True)]
    grad_normed_mlp, summed[0] = lax.optimization_barrier((grad_normed_mlp, summed[0]))
    for grad_cut in grad_cuts[1:]:
        grad_cut, _ = lax.optimization_barrier((grad_cut, summed[-1]))
        summed.append(lax.psum_scatter(grad_cut, "rep", scatter_dimension=0, tiled=True))
    grad_top = cotangent.astype(f32)
    grad_gain_mlp = jnp.sum(grad_normed_mlp * hidden * inv_hidden, axis=0)
    grad_hidden = grad_top + norm_back(grad_normed_mlp * gain_mlp, hidden, inv_hidden)
    grad_attn = (residual_scale * grad_hidden).astype(bf16)
    grad_attn, grad_down = lax.optimization_barrier((grad_attn, grad_down))

    def back_block(j, grad):
        return attend_back(
            j,
            grad,
            attention[j][1],
            attention[j][2],
            latent_parts,
            tables,
            segs,
            query_w,
            keyval_w,
            out_proj,
        )

    near = near_blocks(grad_attn, group)
    back = [back_block(0, grad_attn)]
    if fast:
        act_late, _ = lax.optimization_barrier((act_all, grad_attn))
        down_all = jnp.dot(
            act_late[:, :hidden_part], down_proj, preferred_element_type=f32
        ).astype(bf16)
        down_terms = [down_all[j * seq_len : (j + 1) * seq_len] for j in range(group)]
    near, back, down_terms = lax.optimization_barrier((near, back, down_terms))
    attn_parts = all_blocks(grad_attn, near, group)
    back += [back_block(j, attn_parts[j]) for j in others]
    down_terms, _ = lax.optimization_barrier((down_terms, attn_parts[1:]))
    block_out = (hidden + residual_scale * scatter_sum(down_terms, group)).astype(bf16)
    owned = [to_owner_rows(rows) for rows in summed]

    def unpack(q, second):
        pieces = []
        for (start, stop), rows in zip(cuts, owned):
            for t in range(stop - start):
                first = (2 * t + second) * TILE
                pieces.append(rows[q, :, first : first + TILE])
        first = 2 * (cuts[-1][1] - cuts[-1][0]) * TILE + second * TAIL
        return pieces + [owned[-1][q, :, first : first + tail]]

    gateup_total = jnp.concatenate(
        [piece for second in (0, 1) for q in range(group) for piece in unpack(q, second)], axis=1
    )
    latent_terms = [part[0] for part in back]
    grad_latent_low = scatter_sum(latent_terms, group)
    grad_normed_query = grad_latent_low[:, :QR]
    grad_normed_keyval = grad_latent_low[:, QR : QR + KR]
    grad_key_rope = grad_latent_low[:, QR + KR + HD : QR + KR + HD + RD]
    grad_gain_query = jnp.sum(grad_normed_query * query_lat * inv_query, axis=0)
    grad_gain_keyval = jnp.sum(grad_normed_keyval * keyval_lat * inv_keyval, axis=0)
    grad_latent_rows = jnp.concatenate(
        [
            norm_back(grad_normed_query * gain_query, query_lat, inv_query),
            norm_back(grad_normed_keyval * gain_keyval, keyval_lat, inv_keyval),
            grad_key_rope,
        ],
        axis=1,
    ).astype(bf16)
    grad_latent_parts = gather_blocks(grad_latent_rows, group)
    block_out, grad_latent_parts = lax.optimization_barrier((block_out, grad_latent_parts))
    grad_down, _ = lax.optimization_barrier((grad_down, (summed[-1], grad_latent_rows)))
    down_total = lax.psum_scatter(grad_down, "rep", scatter_dimension=0, tiled=True)
    mixed_late, late_query, late_keyval, _ = lax.optimization_barrier(
        (
            [part[3] for part in attention],
            [part[1] for part in back],
            [part[2] for part in back],
            grad_latent_rows,
        )
    )
    grad_out = token_grad(mixed_late, attn_parts, 0, heads * HD, "out_grad")
    grad_query = token_grad(latent_parts, late_query, 0, QR, "query_grad")
    grad_keyval = token_grad(latent_parts, late_keyval, QR, KR, "keyval_grad")
    query_rows = QR // (group * replicas)
    keyval_rows = KR // (group * replicas)
    unit = heads * LANES
    pair_rows = group * (query_rows + keyval_rows)
    out_units = D // unit
    out_count = heads * HD // replicas
    pair = (
        jnp.concatenate(
            [
                grad_query.reshape(group, replicas, query_rows, unit),
                grad_keyval.reshape(group, replicas, keyval_rows, unit),
            ],
            axis=2,
        )
        .transpose(1, 0, 2, 3)
        .reshape(replicas, pair_rows, unit)
    )
    grad_out = grad_out.reshape(replicas, out_count, D)
    grad_out = [grad_out[:, :, k * unit : (k + 1) * unit] for k in range(out_units)]

    grad_normed_in = jnp.einsum(
        "tc,dc->td", grad_latent_rows, latent_w, preferred_element_type=f32
    )
    grad_gain_in = jnp.sum(grad_normed_in * rows_in * inv_in, axis=0)
    input_grad = grad_hidden + norm_back(grad_normed_in * gain_in, rows_in, inv_in)
    grad_gains = jnp.concatenate([grad_gain_in, grad_gain_query, grad_gain_keyval, grad_gain_mlp])
    gain_blocks = pick(grad_gains, me, group)
    gains_sum = gain_blocks[0]
    for j in others:
        gains_sum = gains_sum + hop(gain_blocks[j].astype(bf16), group, j).astype(f32)
    grad_latent = jnp.einsum(
        "td,tc->dc",
        jnp.concatenate(normed_columns, axis=0),
        jnp.concatenate(grad_latent_parts, axis=0),
        preferred_element_type=f32,
    ).astype(bf16)
    width = grad_latent.shape[1]
    latent_units = -(-width // unit)
    grad_latent = jnp.pad(
        grad_latent.reshape(replicas, share, width), ((0, 0), (0, 0), (0, latent_units * unit - width))
    )
    grad_latent = [grad_latent[:, :, k * unit : (k + 1) * unit] for k in range(latent_units)]
    gains_row = gains_sum.reshape(replicas, 1, -1).astype(bf16)
    gains_row = jnp.pad(gains_row, ((0, 0), (0, 15), (0, unit - gains_row.shape[2])))
    last = jnp.concatenate([pair] + grad_out + grad_latent + [gains_row], axis=1)
    last, _ = lax.optimization_barrier((last.reshape(-1, unit), down_total))
    last = lax.psum_scatter(last, "rep", scatter_dimension=0, tiled=True)
    pair_own = to_owner_rows(last[:pair_rows])
    query_total = (
        pair_own[:, :query_rows]
        .reshape(group, query_rows, heads, LANES)[..., : HD + RD]
        .transpose(1, 0, 2, 3)
        .reshape(query_rows, H * (HD + RD))
    )
    keyval_total = pair_own[:, query_rows:].transpose(1, 0, 2).reshape(keyval_rows, 2 * H * HD)

    def side_by_side(first, count, pieces):
        return jnp.concatenate(
            [last[first + k * count : first + (k + 1) * count] for k in range(pieces)], axis=1
        )

    outproj_total = side_by_side(pair_rows, out_count, out_units)
    latent_at = pair_rows + out_units * out_count
    latent_total = side_by_side(latent_at, share, latent_units)[:, :width]
    gains_total = last[latent_at + latent_units * share, : gains_mean.shape[0]]

    updates = [
        adam_step(latent_proj, latent_total, latent_mean, latent_square, D ** (-0.5), decay_rate),
        adam_step(query_up, query_total, query_mean, query_square, QR ** (-0.5), decay_rate),
        adam_step(keyval_up, keyval_total, keyval_mean, keyval_square, KR ** (-0.5), decay_rate),
        adam_step(
            out_proj,
            outproj_total,
            outproj_mean,
            outproj_square,
            max(H * HD // 512, 1) ** (-0.5),
            decay_rate,
        ),
        adam_step(gate_up, gateup_total, gateup_mean, gateup_square, D ** (-0.5), decay_rate),
        adam_step(
            down_proj, down_total, down_mean, down_square, max(FF // 32, 1) ** (-0.5), decay_rate
        ),
        adam_step(norm_gains, gains_total, gains_mean, gains_square, gain_rate, 0.0),
    ]
    return (block_out, input_grad) + tuple(value for update in updates for value in update)


def solution(mesh):
    return jax.shard_map(
        functools.partial(per_device, mesh.shape["shard"], mesh.shape["rep"]),
        mesh=mesh,
        in_specs=(
            P(("shard", "rep"), None),
            P(("shard", "rep"), None),
            P(("shard", "rep"), None),
            P("shard", None),
            P("shard", None),
            P("shard", None),
            P("shard", None),
            P("shard", None),
            P("shard", None),
            P("shard"),
            P(("shard", "rep"), None),
            P(("shard", "rep"), None),
            P(("shard", "rep"), None),
            P(("shard", "rep"), None),
            P(("shard", "rep"), None),
            P(("shard", "rep"), None),
            P(("shard", "rep")),
            P(("shard", "rep"), None),
            P(("shard", "rep"), None),
            P(("shard", "rep"), None),
            P(("shard", "rep"), None),
            P(("shard", "rep"), None),
            P(("shard", "rep"), None),
            P(("shard", "rep")),
        ),
        out_specs=(
            P(("shard", "rep"), None),
            P(("shard", "rep"), None),
            P(("shard", "rep"), None),
            P(("shard", "rep"), None),
            P(("shard", "rep"), None),
            P(("shard", "rep"), None),
            P(("shard", "rep"), None),
            P(("shard", "rep"), None),
            P(("shard", "rep"), None),
            P(("shard", "rep"), None),
            P(("shard", "rep"), None),
            P(("shard", "rep"), None),
            P(("shard", "rep"), None),
            P(("shard", "rep"), None),
            P(("shard", "rep"), None),
            P(("shard", "rep"), None),
            P(("shard", "rep"), None),
            P(("shard", "rep"), None),
            P(("shard", "rep"), None),
            P(("shard", "rep"), None),
            P(("shard", "rep")),
            P(("shard", "rep")),
            P(("shard", "rep")),
        ),
        check_vma=False,
    )
```

```python
import functools
import math

import jax
import jax.numpy as jnp
from jax import lax
from jax.experimental import pallas as pl
from jax.experimental.pallas import tpu as pltpu
from jax.sharding import PartitionSpec as P

D = 2560
H = 40
HD = 64
RD = 32
QR = 768
KR = 256
FF = 6400
STEP = 10


norm_eps = 1e-05
residual_scale = 1.4 / math.sqrt(62.0)
beta_one = 0.9
beta_two = 0.95
adam_eps = 1e-08
decay_rate = 0.1
gain_rate = 0.8


def inverse_rms(values):
    return lax.rsqrt(jnp.mean(values * values, axis=-1, keepdims=True) + norm_eps)


def norm_back(incoming, operand, inv_scale):
    return inv_scale * (
        incoming
        - operand * inv_scale * inv_scale * jnp.mean(incoming * operand, axis=-1, keepdims=True)
    )


def rotation_rates():
    rates = [0.0] * LANES
    for i in range(RD // 2):
        rates[HD + i] = rates[HD + RD // 2 + i] = 10000.0 ** (-2.0 * i / RD)
    return jnp.array([rates], jnp.float32)


def own_rows(weight, gradient):
    count = gradient.shape[0]
    start = lax.axis_index("rep") * count
    return lax.dynamic_slice_in_dim(weight, start, count, 0)


def adam_step(weight, gradient, mean_old, square_old, step_rate, decay_factor):
    weight_f = own_rows(weight, gradient).astype(jnp.float32)
    gradient = gradient.astype(jnp.float32)
    mean_new = beta_one * mean_old.astype(jnp.float32) + (1.0 - beta_one) * gradient
    square_new = beta_two * square_old.astype(jnp.float32) + (1.0 - beta_two) * gradient * gradient
    ratio = (
        mean_new
        / (1.0 - beta_one**STEP)
        / (jnp.sqrt(square_new / (1.0 - beta_two**STEP)) + adam_eps)
    )
    updated = weight_f - step_rate * (ratio + decay_factor * weight_f)
    return (updated, mean_new, square_new)


TILE = 256
TAIL = 128
LANES = 128
LATENT = QR + KR + LANES
score_scale = (HD + RD) ** (-0.5)
VMEM_BYTES = 48 * 1024 * 1024


def across(a, b):
    return lax.dot_general(a, b, (((1,), (1,)), ((), ())), preferred_element_type=jnp.float32)


def along(a, b):
    return lax.dot_general(a, b, (((1,), (0,)), ((), ())), preferred_element_type=jnp.float32)


def mlp_kernel(group, tiles, tail, rows_d, order_ref, normed_ref, branch_ref, *refs):
    blocks = refs[:group]
    tails = refs[group : 2 * group]
    down_ref, down_tail_ref = refs[2 * group : 2 * group + 2]
    out_refs = refs[-9:]
    act_ref, grad_ref, sum_ref, back_ref, whole, whole_tail, down_wide, sum_acc, back_acc = out_refs
    step = pl.program_id(0)
    bf16 = jnp.bfloat16

    for j in range(group):
        start = pl.multiple_of(order_ref[j] * rows_d, 16)
        whole[pl.ds(start, rows_d), :] = blocks[j][...]

    def part(weights, down, width):
        both = along(normed_ref[...], weights)
        gate = both[:, :width]
        up = both[:, width:]
        sigmoid = 1.0 / (1.0 + jnp.exp(-gate))
        silu = gate * sigmoid
        act = (silu * up).astype(bf16)
        grad_act = across(branch_ref[...], down)
        grad_gate = grad_act * up * sigmoid * (1.0 + gate * (1.0 - sigmoid))
        grad_up = grad_act * silu
        grad = jnp.concatenate([grad_gate.astype(bf16), grad_up.astype(bf16)], axis=1)
        return act, grad, along(act, down), across(grad, weights)

    act, grad, term, back = part(whole[...], down_ref[...], TILE)
    first = pl.multiple_of(step * TILE, TILE)
    act_ref[:, pl.ds(first, TILE)] = act
    grad_ref[:, pl.ds(pl.multiple_of(2 * first, 2 * TILE), 2 * TILE)] = grad

    @pl.when(step == 0)
    def _():
        sum_acc[...] = term
        back_acc[...] = back

    @pl.when(step > 0)
    def _():
        sum_acc[...] += term
        back_acc[...] += back

    @pl.when(step == tiles - 1)
    def _():
        for j in range(group):
            start = pl.multiple_of(order_ref[j] * rows_d, 16)
            whole_tail[pl.ds(start, rows_d), :] = tails[j][...]
        down_wide[...] = jnp.zeros_like(down_wide)
        down_wide[:tail, :] = down_tail_ref[...]
        act, grad, term, back = part(whole_tail[...], down_wide[...], TAIL)
        act_ref[:, tiles * TILE :] = act
        grad_ref[:, 2 * tiles * TILE :] = grad
        sum_ref[...] = (sum_acc[...] + term).astype(bf16)
        back_ref[...] = (back_acc[...] + back).astype(bf16)


def mlp_part(order, normed, branch, own, gathered, down, earlier, index, group):
    tokens, width = normed.shape
    hidden = down.shape[0]
    tiles = hidden // TILE
    tail = hidden - tiles * TILE
    rows_d = width // group
    bf16 = jnp.bfloat16
    f32 = jnp.float32
    fixed = lambda t: (0, 0)
    weights = [own] + [gathered] * (group - 1)
    return pl.pallas_call(
        functools.partial(mlp_kernel, group, tiles, tail, rows_d),
        grid=(tiles,),
        in_specs=[
            pl.BlockSpec(memory_space=pltpu.SMEM),
            pl.BlockSpec((tokens, width), fixed),
            pl.BlockSpec((tokens, width), fixed),
        ]
        + [pl.BlockSpec((rows_d, 2 * TILE), lambda t: (0, t))]
        + [
            pl.BlockSpec((rows_d, 2 * TILE), lambda t, j=j: (0, j * tiles + t))
            for j in range(group - 1)
        ]
        + [pl.BlockSpec((rows_d, 2 * TAIL), lambda t: (0, tiles * TILE // TAIL))]
        + [
            pl.BlockSpec(
                (rows_d, 2 * TAIL), lambda t, j=j: (0, (group - 1) * tiles * TILE // TAIL + j)
            )
            for j in range(group - 1)
        ]
        + [
            pl.BlockSpec((TILE, width), lambda t: (t, 0)),
            pl.BlockSpec((tail, width), lambda t: (tiles * TILE // tail, 0)),
        ]
        + [pl.BlockSpec(memory_space=pl.ANY)] * len(earlier),
        out_specs=[
            pl.BlockSpec((tokens, tiles * TILE + TAIL), lambda t: (index, 0)),
            pl.BlockSpec((tokens, 2 * (tiles * TILE + TAIL)), lambda t: (index, 0)),
            pl.BlockSpec((tokens, width), fixed),
            pl.BlockSpec((tokens, width), fixed),
        ],
        out_shape=[
            jax.ShapeDtypeStruct((group * tokens, tiles * TILE + TAIL), bf16),
            jax.ShapeDtypeStruct((group * tokens, 2 * (tiles * TILE + TAIL)), bf16),
            jax.ShapeDtypeStruct((tokens, width), bf16),
            jax.ShapeDtypeStruct((tokens, width), bf16),
        ],
        scratch_shapes=[
            pltpu.VMEM((width, 2 * TILE), bf16),
            pltpu.VMEM((width, 2 * TAIL), bf16),
            pltpu.VMEM((TAIL, width), bf16),
            pltpu.VMEM((tokens, width), f32),
            pltpu.VMEM((tokens, width), f32),
        ],
        input_output_aliases={5 + 2 * group + i: i for i in range(len(earlier))},
        compiler_params=pltpu.CompilerParams(vmem_limit_bytes=VMEM_BYTES),
        cost_estimate=pl.CostEstimate(
            flops=12 * tokens * width * hidden,
            bytes_accessed=6 * width * hidden + 8 * tokens * width,
            transcendentals=tokens * hidden,
        ),
        name="mlp_part",
    )(order, normed, branch, *weights, *weights, down, down, *earlier)


def layer_kernel(group, base, tiles, tail, rows_d, shares, last, order_ref, *refs):
    normed_in = refs[:group]
    top_in = refs[group : 2 * group]
    at = 2 * group
    blocks = refs[at : at + group]
    at += group
    if last:
        tails = refs[at : at + group]
        at += group
        down_ref, down_tail_ref, act_old, acc_in = refs[at : at + 4]
        at += 4
    else:
        down_ref = refs[at]
        at += 1
    act_out, grad_out, back_out = refs[at : at + 3]
    normed, turned, branch, whole, acc, stage, act_stage, in_sems, out_sems, back_sem = refs[
        at + 3 : at + 13
    ]
    if last:
        whole_tail, down_wide, tail_stage, tail_act, tail_sems = refs[at + 13 :]
    bf16 = jnp.bfloat16
    f32 = jnp.float32
    step = pl.program_id(0)
    slot = lax.rem(step, 2)
    tokens = normed_in[0].shape[0]
    width = normed.shape[1]
    rows = rows_d // shares

    def arrivals():
        copies = []
        for j in range(group):
            copies.append(
                pltpu.make_async_copy(
                    normed_in[j], normed.at[pl.ds(j * tokens, tokens), :], in_sems.at[j]
                )
            )
            copies.append(
                pltpu.make_async_copy(
                    top_in[j], branch.at[pl.ds(j * tokens, tokens), :], in_sems.at[group + j]
                )
            )
        return copies

    @pl.when(step == 0)
    def _():
        copies = arrivals()
        for copy in copies:
            copy.start()
        if last:
            pltpu.make_async_copy(acc_in, acc, back_sem).start()
        else:
            acc[...] = jnp.zeros_like(acc)
        for j in range(group):
            at = pl.ds(j * tokens, tokens)
            copies[2 * j].wait()
            turned[:, j * tokens : (j + 1) * tokens] = normed[at, :].T
            copies[2 * j + 1].wait()
            branch[at, :] = (residual_scale * branch[at, :].astype(f32)).astype(bf16)
        if last:
            pltpu.make_async_copy(acc_in, acc, back_sem).wait()

    for j in range(group):
        start = pl.multiple_of(order_ref[j] * rows_d, 16)
        whole[pl.ds(start, rows_d), :] = blocks[j][...]

    def part(weights_ref, down, wide, act_to, grad_to):
        both = along(normed[...], weights_ref[...])
        gate = both[:, :wide]
        up = both[:, wide:]
        sigmoid = 1.0 / (1.0 + jnp.exp(-gate))
        silu = gate * sigmoid
        act_to[...] = (silu * up).astype(bf16)
        grad_act = across(branch[...], down)
        grad_gate = grad_act * up * sigmoid * (1.0 + gate * (1.0 - sigmoid))
        grad_up = grad_act * silu
        grad = jnp.concatenate([grad_gate.astype(bf16), grad_up.astype(bf16)], axis=1)
        cut = 512
        for c in range(width // cut):
            here = slice(c * cut, (c + 1) * cut)
            acc[:, here] += across(grad, weights_ref[here, :])
        for g in range(group):
            result = along(turned[g * rows_d : (g + 1) * rows_d, :], grad).astype(bf16)
            for r in range(shares):
                grad_to[r, g] = result[r * rows : (r + 1) * rows, :]

    def leaving(index, slot_index):
        first = pl.multiple_of((base + index) * TILE, TILE)
        return (
            pltpu.make_async_copy(
                act_stage.at[slot_index],
                act_out.at[:, pl.ds(first, TILE)],
                out_sems.at[0, slot_index],
            ),
            pltpu.make_async_copy(
                stage.at[slot_index],
                grad_out.at[:, :, :, pl.ds(pl.multiple_of(index * 2 * TILE, 2 * TILE), 2 * TILE)],
                out_sems.at[1, slot_index],
            ),
        )

    @pl.when(step >= 2)
    def _():
        for copy in leaving(step - 2, slot):
            copy.wait()

    part(whole, down_ref[...], TILE, act_stage.at[slot], stage.at[slot])
    for copy in leaving(step, slot):
        copy.start()

    @pl.when(step == tiles - 1)
    def _():
        if last:
            for j in range(group):
                start = pl.multiple_of(order_ref[j] * rows_d, 16)
                whole_tail[pl.ds(start, rows_d), :] = tails[j][...]
            down_wide[...] = jnp.zeros_like(down_wide)
            down_wide[:tail, :] = down_tail_ref[...]
            part(whole_tail, down_wide[...], TAIL, tail_act, tail_stage)
            final = [
                pltpu.make_async_copy(
                    tail_act, act_out.at[:, pl.ds((base + tiles) * TILE, TAIL)], tail_sems.at[0]
                ),
                pltpu.make_async_copy(
                    tail_stage,
                    grad_out.at[:, :, :, pl.ds(2 * tiles * TILE, 2 * TAIL)],
                    tail_sems.at[1],
                ),
            ]
            normed[...] = acc[...].astype(bf16)
            final.append(pltpu.make_async_copy(normed, back_out, back_sem))
        else:
            final = [pltpu.make_async_copy(acc, back_out, back_sem)]
        for copy in final:
            copy.start()
        for k in range(max(tiles - 2, 0), tiles):
            for copy in leaving(k, k % 2):
                copy.wait()
        for copy in final:
            copy.wait()


def layer_part(order, normed, top, own, gathered, down, earlier, tiles_from, tiles, group, shares):
    tokens, width = normed[0].shape
    hidden = down.shape[0]
    all_tiles = hidden // TILE
    tail = hidden - all_tiles * TILE
    rows_d = width // group
    rows = rows_d // shares
    bf16 = jnp.bfloat16
    f32 = jnp.float32
    last = earlier is not None
    total = group * tokens
    once = pl.Buffered(1)
    any_spec = pl.BlockSpec(memory_space=pl.ANY)
    weights = [own] + [gathered] * (group - 1)
    in_specs = [pl.BlockSpec(memory_space=pltpu.SMEM)] + [any_spec] * (2 * group)
    in_specs += [pl.BlockSpec((rows_d, 2 * TILE), lambda t: (0, tiles_from + t))]
    in_specs += [
        pl.BlockSpec((rows_d, 2 * TILE), lambda t, j=j: (0, j * all_tiles + tiles_from + t))
        for j in range(group - 1)
    ]
    inputs = [order] + normed + top + weights
    scratch = [
        pltpu.VMEM((total, width), bf16),
        pltpu.VMEM((width, total), bf16),
        pltpu.VMEM((total, width), bf16),
        pltpu.VMEM((width, 2 * TILE), bf16),
        pltpu.VMEM((total, width), f32),
        pltpu.VMEM((2, shares, group, rows, 2 * TILE), bf16),
        pltpu.VMEM((2, total, TILE), bf16),
        pltpu.SemaphoreType.DMA((2 * group,)),
        pltpu.SemaphoreType.DMA((2, 2)),
        pltpu.SemaphoreType.DMA,
    ]
    cols = 2 * tiles * TILE
    aliases = {}
    if last:
        first_tail = all_tiles * TILE // TAIL
        in_specs += [
            pl.BlockSpec((rows_d, 2 * TAIL), lambda t: (0, first_tail), pipeline_mode=once)
        ]
        in_specs += [
            pl.BlockSpec(
                (rows_d, 2 * TAIL),
                lambda t, j=j: (0, (group - 1) * first_tail + j),
                pipeline_mode=once,
            )
            for j in range(group - 1)
        ]
        inputs += weights
        cols += 2 * TAIL
    in_specs.append(pl.BlockSpec((TILE, width), lambda t: (tiles_from + t, 0)))
    inputs.append(down)
    if last:
        in_specs.append(
            pl.BlockSpec(
                (tail, width), lambda t: (all_tiles * TILE // tail, 0), pipeline_mode=once
            )
        )
        inputs.append(down)
        in_specs += [any_spec, any_spec]
        aliases = {len(inputs): 0}
        inputs += [earlier[0], earlier[2]]
        scratch += [
            pltpu.VMEM((width, 2 * TAIL), bf16),
            pltpu.VMEM((TAIL, width), bf16),
            pltpu.VMEM((shares, group, rows, 2 * TAIL), bf16),
            pltpu.VMEM((total, TAIL), bf16),
            pltpu.SemaphoreType.DMA((2,)),
        ]
    part_hidden = tiles * TILE + (tail if last else 0)
    return pl.pallas_call(
        functools.partial(
            layer_kernel, group, tiles_from, tiles, tail, rows_d, shares, last
        ),
        grid=(tiles,),
        in_specs=in_specs,
        out_specs=[any_spec] * 3,
        out_shape=[
            jax.ShapeDtypeStruct((total, all_tiles * TILE + TAIL), bf16),
            jax.ShapeDtypeStruct((shares, group, rows, cols), bf16),
            jax.ShapeDtypeStruct((total, width), bf16 if last else f32),
        ],
        scratch_shapes=scratch,
        input_output_aliases=aliases,
        compiler_params=pltpu.CompilerParams(vmem_limit_bytes=61 * 1024 * 1024),
        cost_estimate=pl.CostEstimate(
            flops=14 * total * width * part_hidden,
            bytes_accessed=12 * width * part_hidden + 16 * total * width,
            transcendentals=total * part_hidden,
        ),
        name="layer_part",
    )(*inputs)


def down_grad_kernel(group, tokens, act_ref, *refs):
    top = refs[:group]
    out_ref, whole = refs[group:]

    @pl.when(pl.program_id(0) == 0)
    def _():
        for j in range(group):
            whole[j * tokens : (j + 1) * tokens, :] = (
                residual_scale * top[j][...].astype(jnp.float32)
            ).astype(jnp.bfloat16)

    out_ref[...] = along(act_ref[...].T, whole[...]).astype(jnp.bfloat16)


def down_grad(act_all, top_parts, hidden, group):
    tokens, width = top_parts[0].shape
    tiles = (hidden + TILE - 1) // TILE
    return pl.pallas_call(
        functools.partial(down_grad_kernel, group, tokens),
        grid=(tiles,),
        in_specs=[pl.BlockSpec((group * tokens, TILE), lambda t: (0, t))]
        + [pl.BlockSpec((tokens, width), lambda t: (0, 0))] * group,
        out_specs=pl.BlockSpec((TILE, width), lambda t: (t, 0)),
        out_shape=jax.ShapeDtypeStruct((hidden, width), jnp.bfloat16),
        scratch_shapes=[pltpu.VMEM((group * tokens, width), jnp.bfloat16)],
        compiler_params=pltpu.CompilerParams(vmem_limit_bytes=VMEM_BYTES),
        cost_estimate=pl.CostEstimate(
            flops=2 * group * tokens * width * hidden,
            bytes_accessed=2 * width * hidden + 2 * group * tokens * (width + hidden),
            transcendentals=0,
        ),
        name="down_grad",
    )(act_all, *top_parts)


def lane_index(rows):
    return lax.broadcasted_iota(jnp.int32, (rows, LANES), 1)


def turn(values, table_ref, sign):
    ahead = pltpu.roll(values, LANES - RD // 2, 1)
    behind = pltpu.roll(values, RD // 2, 1)
    return values * table_ref[0] + sign * (ahead * table_ref[1] + behind * table_ref[2])


def seg_column(seg_ref):
    return seg_ref[...].T[:, :1]


def causal_mask(seg_ref):
    tokens = seg_ref.shape[1]
    row = lax.broadcasted_iota(jnp.int32, (tokens, tokens), 0)
    col = lax.broadcasted_iota(jnp.int32, (tokens, tokens), 1)
    return (seg_column(seg_ref) == seg_ref[:1, :]) & (col <= row)


def softmax_rows(query, key, allowed):
    scores = across(query, key) * score_scale
    masked = jnp.where(allowed, scores, -1e30)
    exponent = jnp.exp(masked - jnp.max(masked, axis=1, keepdims=True))
    return exponent * (1.0 / jnp.sum(exponent, axis=1, keepdims=True))


def key_lanes(keyval, latent_ref, lane):
    return jnp.where(lane < HD, keyval, latent_ref[:, QR + KR :])


def attend_kernel(
    heads,
    latent_ref,
    table_ref,
    seg_ref,
    query_w_ref,
    keyval_w_ref,
    out_w_ref,
    term_ref,
    query_ref,
    keyval_ref,
    mixed_ref,
):
    bf16 = jnp.bfloat16
    tokens = latent_ref.shape[0]
    lane = lane_index(tokens)
    allowed = causal_mask(seg_ref)
    query = along(latent_ref[:, :QR], query_w_ref[...])
    keyval_ref[...] = along(latent_ref[:, QR : QR + KR], keyval_w_ref[...]).astype(bf16)
    even = None
    for h in range(heads):
        at = slice(h * LANES, (h + 1) * LANES)
        query_h = turn(query[:, at], table_ref, 1.0).astype(bf16)
        query_ref[:, at] = query_h
        keyval_h = keyval_ref[:, at]
        probs = softmax_rows(query_h, key_lanes(keyval_h, latent_ref, lane), allowed).astype(bf16)
        mixed = along(probs, keyval_h)
        if h % 2 == 0:
            even = pltpu.roll(mixed, HD, 1)
            if h == heads - 1:
                mixed_ref[:, h * HD :] = even[:, :HD].astype(bf16)
        else:
            mixed_ref[:, (h - 1) * HD : (h + 1) * HD] = jnp.where(lane < HD, even, mixed).astype(
                bf16
            )
    term_ref[...] = along(mixed_ref[...], out_w_ref[...]).astype(bf16)


def nth(array, index):
    return pl.BlockSpec((None,) + array.shape[1:], lambda i: (index,) + (0,) * (array.ndim - 1))


def entire(array):
    return pl.BlockSpec(array.shape, lambda i: (0,) * array.ndim)


def attend(index, latent, table, seg, query_w, keyval_w, out_w):
    tokens = latent.shape[1]
    heads = query_w.shape[1] // LANES
    width = out_w.shape[1]
    bf16 = jnp.bfloat16
    return pl.pallas_call(
        functools.partial(attend_kernel, heads),
        grid=(1,),
        out_specs=[
            pl.BlockSpec((tokens, cols), lambda i: (0, 0))
            for cols in (width, heads * LANES, heads * LANES, heads * HD)
        ],
        in_specs=[nth(array, index) for array in (latent, table, seg)]
        + [entire(array) for array in (query_w, keyval_w, out_w)],
        out_shape=[
            jax.ShapeDtypeStruct((tokens, width), bf16),
            jax.ShapeDtypeStruct((tokens, heads * LANES), bf16),
            jax.ShapeDtypeStruct((tokens, heads * LANES), bf16),
            jax.ShapeDtypeStruct((tokens, heads * HD), bf16),
        ],
        compiler_params=pltpu.CompilerParams(vmem_limit_bytes=VMEM_BYTES),
        cost_estimate=pl.CostEstimate(
            flops=2 * tokens * (heads * LANES * (QR + KR + 2 * tokens) + heads * HD * width),
            bytes_accessed=2 * (heads * LANES * (QR + KR) + heads * HD * width + tokens * width),
            transcendentals=heads * tokens * tokens,
        ),
        name="attend",
    )(latent, table, seg, query_w, keyval_w, out_w)


def attend_back_kernel(
    heads,
    grad_ref,
    query_ref,
    keyval_ref,
    latent_ref,
    table_ref,
    seg_ref,
    query_w_ref,
    keyval_w_ref,
    out_w_ref,
    term_ref,
    grad_query_ref,
    grad_keyval_ref,
):
    bf16 = jnp.bfloat16
    f32 = jnp.float32
    tokens = latent_ref.shape[0]
    lane = lane_index(tokens)
    allowed = causal_mask(seg_ref)
    grad_mixed = across(grad_ref[...], out_w_ref[...])
    grad_rope = jnp.zeros((tokens, LANES), f32)
    for h in range(heads):
        at = slice(h * LANES, (h + 1) * LANES)
        query_h = query_ref[:, at]
        keyval_h = keyval_ref[:, at]
        key_h = key_lanes(keyval_h, latent_ref, lane)
        probs = softmax_rows(query_h, key_h, allowed)
        if h % 2 == 0:
            if h == heads - 1:
                one = jnp.concatenate([grad_mixed[:, h * HD :]] * 2, axis=1)
            else:
                pair = grad_mixed[:, h * HD : (h + 2) * HD]
                one = pltpu.roll(pair, HD, 1)
        else:
            one = pair
        value_grad = jnp.where(lane >= HD, one, 0.0).astype(bf16)
        turned = probs.astype(bf16).T
        grad_values = along(turned, value_grad)
        grad_probs = across(value_grad, keyval_h)
        delta = jnp.sum(probs * grad_probs, axis=1, keepdims=True)
        grad_scores = (probs * (grad_probs - delta)).astype(bf16)
        grad_q = along(grad_scores, key_h) * score_scale
        grad_k = along(grad_scores.T, query_h) * score_scale
        grad_query_ref[:, at] = turn(grad_q, table_ref, -1.0).astype(bf16)
        grad_keyval_ref[:, at] = jnp.where(lane < HD, grad_k, grad_values).astype(bf16)
        grad_rope = grad_rope + grad_k
    rope = jnp.where(lane >= HD, turn(grad_rope, table_ref, -1.0), 0.0)
    term_ref[:, :QR] = across(grad_query_ref[...], query_w_ref[...]).astype(bf16)
    term_ref[:, QR : QR + KR] = across(grad_keyval_ref[...], keyval_w_ref[...]).astype(bf16)
    term_ref[:, QR + KR :] = rope.astype(bf16)


def attend_back(
    index, grad, query, keyval, latent, table, seg, query_w, keyval_w, out_w
):
    tokens = latent.shape[1]
    heads = query_w.shape[1] // LANES
    width = out_w.shape[1]
    bf16 = jnp.bfloat16
    return pl.pallas_call(
        functools.partial(attend_back_kernel, heads),
        grid=(1,),
        out_specs=[
            pl.BlockSpec((tokens, cols), lambda i: (0, 0))
            for cols in (LATENT, heads * LANES, heads * LANES)
        ],
        in_specs=[entire(array) for array in (grad, query, keyval)]
        + [nth(array, index) for array in (latent, table, seg)]
        + [entire(array) for array in (query_w, keyval_w, out_w)],
        out_shape=[
            jax.ShapeDtypeStruct((tokens, LATENT), bf16),
            jax.ShapeDtypeStruct((tokens, heads * LANES), bf16),
            jax.ShapeDtypeStruct((tokens, heads * LANES), bf16),
        ],
        compiler_params=pltpu.CompilerParams(vmem_limit_bytes=VMEM_BYTES),
        cost_estimate=pl.CostEstimate(
            flops=2 * tokens * (heads * LANES * (QR + KR + 5 * tokens) + heads * HD * width),
            bytes_accessed=2 * (heads * LANES * (QR + KR) + heads * HD * width + tokens * width),
            transcendentals=heads * tokens * tokens,
        ),
        name="attend_back",
    )(grad, query, keyval, latent, table, seg, query_w, keyval_w, out_w)


def token_grad_kernel(count, *refs):
    left = refs[:count]
    right = refs[count : 2 * count]
    out_ref, turned, whole = refs[2 * count :]
    tokens = left[0].shape[0]
    for j in range(count):
        turned[:, j * tokens : (j + 1) * tokens] = left[j][...].T
        whole[j * tokens : (j + 1) * tokens, :] = right[j][...]
    out_ref[...] = along(turned[...], whole[...]).astype(jnp.bfloat16)


def token_grad(left, right, first, rows, name):
    count = len(right)
    tokens, cols = right[0].shape
    at = first // rows
    if isinstance(left, list):
        left_specs = [pl.BlockSpec((tokens, rows), lambda i: (0, at))] * count
    else:
        left_specs = [
            pl.BlockSpec((None, tokens, rows), lambda i, j=j: (j, 0, at)) for j in range(count)
        ]
        left = [left] * count
    return pl.pallas_call(
        functools.partial(token_grad_kernel, count),
        grid=(1,),
        in_specs=left_specs + [pl.BlockSpec((tokens, cols), lambda i: (0, 0))] * count,
        out_specs=pl.BlockSpec((rows, cols), lambda i: (0, 0)),
        out_shape=jax.ShapeDtypeStruct((rows, cols), jnp.bfloat16),
        scratch_shapes=[
            pltpu.VMEM((rows, count * tokens), jnp.bfloat16),
            pltpu.VMEM((count * tokens, cols), jnp.bfloat16),
        ],
        compiler_params=pltpu.CompilerParams(vmem_limit_bytes=VMEM_BYTES),
        cost_estimate=pl.CostEstimate(
            flops=2 * count * tokens * rows * cols,
            bytes_accessed=2 * (rows * cols + count * tokens * (rows + cols)),
            transcendentals=0,
        ),
        name=name,
    )(*left, *right)


MESH = pl.DeviceIdType.MESH


def partner(me, distance):
    bit = 1
    while bit <= distance:
        if distance & bit:
            me = me + bit - 2 * bit * lax.rem(lax.div(me, bit), 2)
        bit *= 2
    return me


def greet(peers, count):
    barrier = pltpu.get_barrier_semaphore()
    for peer in peers:
        pl.semaphore_signal(barrier, inc=1, device_id=peer, device_id_type=MESH)
    pl.semaphore_wait(barrier, count)


def send(src, dst, sems, index, peer):
    copy = pltpu.make_async_remote_copy(
        src_ref=src,
        dst_ref=dst,
        send_sem=sems.at[0, index],
        recv_sem=sems.at[1, index],
        device_id=peer,
        device_id_type=MESH,
    )
    copy.start()
    return copy


def tile_format(gate, up, store, tiles, tail):
    bf16 = jnp.bfloat16
    for t in range(tiles):
        store(2 * t * TILE, gate[:, t * TILE : (t + 1) * TILE].astype(bf16))
        store((2 * t + 1) * TILE, up[:, t * TILE : (t + 1) * TILE].astype(bf16))
    lane = lax.broadcasted_iota(jnp.int32, (gate.shape[0], TAIL), 1)
    for second, values in enumerate((gate, up)):
        last = values[:, tiles * TILE : tiles * TILE + TAIL]
        store(
            2 * tiles * TILE + second * TAIL, jnp.where(lane < tail, last, 0.0).astype(bf16)
        )


def head_table(seg_ref, rates_ref, table_ref):
    tokens = seg_ref.shape[1]
    row = lax.broadcasted_iota(jnp.int32, (tokens, tokens), 0)
    col = lax.broadcasted_iota(jnp.int32, (tokens, tokens), 1)
    before = (seg_column(seg_ref) == seg_ref[:1, :]) & (col < row)
    position = jnp.sum(jnp.where(before, 1.0, 0.0), axis=1, keepdims=True)
    angles = position * rates_ref[...]
    sine = jnp.sin(angles)
    lane = lane_index(tokens)
    middle = HD + RD // 2
    end = HD + RD
    table_ref[0] = jnp.where(lane < end, jnp.cos(angles), 0.0)
    table_ref[1] = jnp.where((lane >= HD) & (lane < middle), -sine, 0.0)
    table_ref[2] = jnp.where((lane >= middle) & (lane < end), sine, 0.0)


def share_small(group, me, peers, gains_ref, seg_ref, gains_all_ref, segs_ref, sems):
    mine = pl.ds(pl.multiple_of(me * 8, 8), 8)
    gains_all_ref[mine, :] = gains_ref[...]
    segs_ref[0] = seg_ref[...]
    copies = []
    for j in range(1, group):
        copies.append(send(gains_ref, gains_all_ref.at[mine, :], sems, 2 * (j - 1), peers[j - 1]))
        copies.append(send(seg_ref, segs_ref.at[j], sems, 2 * (j - 1) + 1, peers[j - 1]))
    return copies


def small_kernel(
    group, gains_ref, seg_ref, rates_ref, gains_all_ref, segs_ref, table_ref, small_sems
):
    me = lax.axis_index("shard")
    rep = lax.axis_index("rep")
    peers = [(partner(me, j), rep) for j in range(1, group)]
    greet(peers, group - 1)
    for copy in share_small(group, me, peers, gains_ref, seg_ref, gains_all_ref, segs_ref, small_sems):
        copy.wait()
    for j in range(group):
        head_table(segs_ref.at[j], rates_ref, table_ref.at[j])


def columns_kernel(
    group,
    replicas,
    hidden,
    slab,
    gate_up_ref,
    query_ref,
    gains_ref,
    seg_ref,
    rates_ref,
    own_ref,
    pieces_ref,
    query_pad_ref,
    gains_all_ref,
    segs_ref,
    table_ref,
    own_slab,
    slabs,
    out_pieces,
    local_sems,
    sems,
    small_sems,
):
    me = lax.axis_index("shard")
    rep = lax.axis_index("rep")
    rows, share = own_slab.shape[1], slabs.shape[1]
    tiles = hidden // TILE
    tail = hidden - tiles * TILE
    main = 2 * tiles * TILE

    def begin(index, second):
        offset = index * hidden
        return pl.multiple_of(second * FF + offset - lax.rem(offset, LANES), LANES)

    loads = []
    for j in range(1, group):
        for second in range(2):
            at = 2 * (j - 1) + second
            copy = pltpu.make_async_copy(
                gate_up_ref.at[
                    pl.ds(pl.multiple_of(rep * share, 16), share), pl.ds(begin(partner(me, j), second), slab)
                ],
                slabs.at[at],
                local_sems.at[at],
            )
            copy.start()
            loads.append(copy)
    for second in range(2):
        at = 2 * (group - 1) + second
        copy = pltpu.make_async_copy(
            gate_up_ref.at[:, pl.ds(begin(me, second), slab)],
            own_slab.at[second],
            local_sems.at[at],
        )
        copy.start()
        loads.append(copy)
    peers = [(partner(me, j), rep) for j in range(1, group)]
    greet(peers, group - 1)
    small = share_small(group, me, peers, gains_ref, seg_ref, gains_all_ref, segs_ref, small_sems)

    def shifted(ref, index):
        amount = lax.rem(slab - lax.rem(index * hidden, LANES), slab)
        return pltpu.roll(ref[...].astype(jnp.float32), amount, 1)

    sent = []
    for j in range(1, group):
        for second in range(2):
            loads[2 * (j - 1) + second].wait()

        def store(first, values, j=j):
            out_pieces[j - 1, :, first : first + values.shape[1]] = values

        tile_format(
            shifted(slabs.at[2 * (j - 1)], partner(me, j)),
            shifted(slabs.at[2 * (j - 1) + 1], partner(me, j)),
            store,
            tiles,
            tail,
        )
        sent.append(
            send(
                out_pieces.at[j - 1, :, pl.ds(0, main)],
                pieces_ref.at[:, pl.ds((j - 1) * main, main)],
                sems,
                2 * (j - 1),
                peers[j - 1],
            )
        )
        sent.append(
            send(
                out_pieces.at[j - 1, :, pl.ds(main, 2 * TAIL)],
                pieces_ref.at[:, pl.ds((group - 1) * main + (j - 1) * 2 * TAIL, 2 * TAIL)],
                sems,
                2 * (j - 1) + 1,
                peers[j - 1],
            )
        )
    for second in range(2):
        loads[2 * (group - 1) + second].wait()

    def store_own(first, values):
        own_ref[:, first : first + values.shape[1]] = values

    tile_format(
        shifted(own_slab.at[0], me), shifted(own_slab.at[1], me), store_own, tiles, tail
    )
    rest = jnp.zeros((query_ref.shape[0], LANES - HD - RD), jnp.float32)
    for h in range(H):
        head = query_ref[:, h * (HD + RD) : (h + 1) * (HD + RD)].astype(jnp.float32)
        query_pad_ref[:, h * LANES : (h + 1) * LANES] = jnp.concatenate(
            [head, rest], axis=1
        ).astype(jnp.bfloat16)
    for copy in small:
        copy.wait()
    for j in range(group):
        head_table(segs_ref.at[j], rates_ref, table_ref.at[j])
    for copy in sent:
        copy.wait()


def small_shapes(gains, seg, group):
    rows, tokens = seg.shape
    f32 = jnp.float32
    return [
        jax.ShapeDtypeStruct((group * rows, gains.shape[1]), f32),
        jax.ShapeDtypeStruct((group, rows, tokens), f32),
        jax.ShapeDtypeStruct((group, 3, tokens, LANES), f32),
    ]


def small_things(gains, seg, group):
    return pl.pallas_call(
        functools.partial(small_kernel, group),
        in_specs=[pl.BlockSpec(memory_space=pltpu.VMEM)] * 3,
        out_specs=[pl.BlockSpec(memory_space=pltpu.VMEM)] * 3,
        out_shape=small_shapes(gains, seg, group),
        scratch_shapes=[pltpu.SemaphoreType.DMA((2, 2 * (group - 1)))],
        compiler_params=pltpu.CompilerParams(
            collective_id=3, has_side_effects=True, vmem_limit_bytes=VMEM_BYTES
        ),
        name="small_things",
    )(gains, seg, rotation_rates())


def hidden_pieces(gate_up, query_up, gains, seg, group, replicas):
    rows = gate_up.shape[0]
    share = rows // replicas
    hidden = FF // group
    whole = 2 * (hidden // TILE * TILE + TAIL)
    slab = -(-(hidden + LANES - math.gcd(hidden, LANES)) // LANES) * LANES
    bf16 = jnp.bfloat16
    others = group - 1
    return pl.pallas_call(
        functools.partial(columns_kernel, group, replicas, hidden, slab),
        in_specs=[pl.BlockSpec(memory_space=pl.ANY)] + [pl.BlockSpec(memory_space=pltpu.VMEM)] * 4,
        out_specs=[pl.BlockSpec(memory_space=pltpu.VMEM)] * 6,
        out_shape=[
            jax.ShapeDtypeStruct((rows, whole), bf16),
            jax.ShapeDtypeStruct((share, others * whole), bf16),
            jax.ShapeDtypeStruct((query_up.shape[0], H * LANES), bf16),
        ]
        + small_shapes(gains, seg, group),
        scratch_shapes=[
            pltpu.VMEM((2, rows, slab), bf16),
            pltpu.VMEM((2 * others, share, slab), bf16),
            pltpu.VMEM((others, share, whole), bf16),
            pltpu.SemaphoreType.DMA((2 * group,)),
            pltpu.SemaphoreType.DMA((2, 2 * others)),
            pltpu.SemaphoreType.DMA((2, 2 * others)),
        ],
        compiler_params=pltpu.CompilerParams(
            collective_id=1, has_side_effects=True, vmem_limit_bytes=VMEM_BYTES
        ),
        cost_estimate=pl.CostEstimate(flops=0, bytes_accessed=100_000_000, transcendentals=0),
        name="hidden_pieces",
    )(gate_up, query_up, gains, seg, rotation_rates())


def latent_kernel(
    group,
    tokens_ref,
    gains_ref,
    latent_gains_ref,
    table_ref,
    latent_proj_ref,
    query_ref,
    keyval_ref,
    parts_ref,
    rows_ref,
    normed_ref,
    latent_w_ref,
    query_w_ref,
    keyval_w_ref,
    local_sems,
    fetch_sems,
    swap_sems,
    weight_sems,
    weight_swap_sems,
    part_sems,
):
    f32 = jnp.float32
    bf16 = jnp.bfloat16
    me = lax.axis_index("shard")
    rep = lax.axis_index("rep")
    core = lax.rem(rep, 2)
    tokens = tokens_ref.shape[0]
    rows_d = latent_proj_ref.shape[0]
    half = rows_d // 2
    query_rows = query_ref.shape[0]
    keyval_rows = keyval_ref.shape[0]
    width = query_w_ref.shape[1]
    others = range(1, group)
    peers = [None] + [(partner(me, j), rep) for j in others]
    sibling = (me, rep + 1 - 2 * core)
    greet(peers[1:] + [sibling], group)

    def block(index, which):
        return pl.ds(pl.multiple_of(index * rows_d + which * half, 16), half)

    fetched = [None] + [
        send(
            latent_proj_ref.at[pl.ds(pl.multiple_of(core * half, 16), half), :],
            latent_w_ref.at[block(me, core), :],
            fetch_sems,
            j - 1,
            peers[j],
        )
        for j in others
    ]
    own = pltpu.make_async_copy(
        latent_proj_ref,
        latent_w_ref.at[pl.ds(pl.multiple_of(me * rows_d, 16), rows_d), :],
        local_sems.at[0],
    )
    own.start()
    kinds = ((query_ref, query_w_ref, query_rows), (keyval_ref, keyval_w_ref, keyval_rows))

    def weight_rows(index, rows):
        return pl.ds(pl.multiple_of(index * rows + core * (rows // 2), 16), rows // 2)

    def fetch_weights():
        return [
            send(
                ref.at[
                    pl.ds(pl.multiple_of(core * (rows // 2), 16), rows // 2),
                    pl.ds(pl.multiple_of(partner(me, j) * width, LANES), width),
                ],
                out_ref.at[weight_rows(me, rows), :],
                weight_sems,
                kind * (group - 1) + j - 1,
                peers[j],
            )
            for kind, (ref, out_ref, rows) in enumerate(kinds)
            for j in others
        ]

    def swap_weights(copies):
        swaps = []
        for kind, (ref, out_ref, rows) in enumerate(kinds):
            for j in others:
                index = kind * (group - 1) + j - 1
                copies[index].wait_recv()
                where = weight_rows(partner(me, j), rows)
                swaps.append(
                    send(
                        out_ref.at[where, :],
                        out_ref.at[where, :],
                        weight_swap_sems,
                        index,
                        sibling,
                    )
                )
        return swaps

    mine = []
    for at, (ref, out_ref, rows) in enumerate(kinds):
        copy = pltpu.make_async_copy(
            ref.at[:, pl.ds(pl.multiple_of(me * width, LANES), width)],
            out_ref.at[pl.ds(pl.multiple_of(me * rows, 16), rows), :],
            local_sems.at[1 + at],
        )
        copy.start()
        mine.append(copy)

    rows_in = tokens_ref[...].astype(f32)
    scale = lax.rsqrt(jnp.mean(rows_in * rows_in, axis=1, keepdims=True) + norm_eps)
    normed_ref[...] = (rows_in * scale * gains_ref[...]).astype(bf16)

    swaps = []
    for j in others:
        fetched[j].wait_recv()
        where = block(partner(me, j), core)
        swaps.append(
            send(latent_w_ref.at[where, :], latent_w_ref.at[where, :], swap_sems, j - 1, sibling)
        )
    weights = fetch_weights()
    own.wait()
    for copy in swaps:
        copy.wait()
    for j in others:
        fetched[j].wait_send()
    latent = along(normed_ref[...], latent_w_ref[...])
    rows_ref[...] = latent

    def rms(values):
        return values * lax.rsqrt(jnp.mean(values * values, axis=1, keepdims=True) + norm_eps)

    query = rms(latent[:, :QR]) * latent_gains_ref[:, :QR]
    keyval = rms(latent[:, QR : QR + KR]) * latent_gains_ref[:, QR:]
    rope = latent[:, QR + KR :]
    wide = jnp.concatenate(
        [jnp.zeros((tokens, HD), f32), rope, jnp.zeros((tokens, LANES - HD - RD), f32)], axis=1
    )
    parts_ref[0, :, :QR] = query.astype(bf16)
    parts_ref[0, :, QR : QR + KR] = keyval.astype(bf16)
    parts_ref[0, :, QR + KR :] = turn(wide, table_ref, 1.0).astype(bf16)

    direct = (1, 2) if group == 4 else others
    near = [
        send(parts_ref.at[0], parts_ref.at[j], part_sems, j - 1, peers[j]) for j in direct
    ]
    swaps = swap_weights(weights)
    far = []
    if group == 4:
        part = tokens // 2
        top = pl.ds(0, part)
        low = pl.ds(part, part)
        near[0].wait_recv()
        far.append(send(parts_ref.at[1, top], parts_ref.at[3, top], part_sems, 2, peers[2]))
        near[1].wait_recv()
        far.append(send(parts_ref.at[2, low], parts_ref.at[3, low], part_sems, 3, peers[1]))
        for copy in near:
            copy.wait_send()
    else:
        for copy in near:
            copy.wait()
    for copy in far + swaps + mine:
        copy.wait()
    for copy in weights:
        copy.wait_send()


def latent_front(tokens, gain_in, latent_gains, table, latent_proj, query_pad, keyval, group):
    rows = tokens.shape[0]
    heads = query_pad.shape[1] // LANES // group
    bf16 = jnp.bfloat16
    others = group - 1
    dma = pltpu.SemaphoreType.DMA
    width = latent_proj.shape[1]
    return pl.pallas_call(
        functools.partial(latent_kernel, group),
        in_specs=[pl.BlockSpec(memory_space=pltpu.VMEM)] * 7,
        out_specs=[pl.BlockSpec(memory_space=pltpu.VMEM)] * 6,
        out_shape=[
            jax.ShapeDtypeStruct((group, rows, LATENT), bf16),
            jax.ShapeDtypeStruct((rows, width), jnp.float32),
            jax.ShapeDtypeStruct((rows, D), bf16),
            jax.ShapeDtypeStruct((D, width), bf16),
            jax.ShapeDtypeStruct((QR, heads * LANES), bf16),
            jax.ShapeDtypeStruct((KR, heads * LANES), bf16),
        ],
        scratch_shapes=[
            dma((3,)),
            dma((2, others)),
            dma((2, others)),
            dma((2, 2 * others)),
            dma((2, 2 * others)),
            dma((2, max(others, 4))),
        ],
        compiler_params=pltpu.CompilerParams(
            collective_id=2, has_side_effects=True, vmem_limit_bytes=VMEM_BYTES
        ),
        cost_estimate=pl.CostEstimate(
            flops=2 * rows * D * width, bytes_accessed=60_000_000, transcendentals=0
        ),
        name="latent_front",
    )(tokens, gain_in, latent_gains, table, latent_proj, query_pad, keyval)


def hop(array, group, distance):
    return lax.ppermute(array, "shard", [(i, i ^ distance) for i in range(group)])


def near_blocks(array, group):
    return [hop(array, group, j) for j in ((1, 2) if group == 4 else range(1, group))]


def all_blocks(array, near, group):
    if group != 4:
        return [array] + near
    half = array.shape[0] // 2
    far_top = hop(near[0][:half], group, 2)
    far_low = hop(near[1][half:], group, 1)
    return [array] + near + [jnp.concatenate([far_top, far_low], axis=0)]


def gather_blocks(array, group):
    return all_blocks(array, near_blocks(array, group), group)


def scatter_sum(parts, group):
    low = jnp.bfloat16
    f32 = jnp.float32
    total = parts[0].astype(f32)
    if group != 4:
        for j in range(1, group):
            total = total + hop(parts[j], group, j).astype(f32)
        return total
    half = parts[0].shape[0] // 2
    top = hop(parts[3][:half], group, 1)
    bottom = hop(parts[3][half:], group, 2)

    def add(left, right):
        return (left.astype(f32) + right.astype(f32)).astype(low)

    two = jnp.concatenate([add(parts[2][:half], top), parts[2][half:]], axis=0)
    one = jnp.concatenate([parts[1][:half], add(parts[1][half:], bottom)], axis=0)
    return total + hop(one, group, 1).astype(f32) + hop(two, group, 2).astype(f32)


def place(blocks, me):
    rows = blocks[0].shape[0]
    whole = jnp.zeros((rows * len(blocks),) + blocks[0].shape[1:], blocks[0].dtype)
    for j, block in enumerate(blocks):
        whole = lax.dynamic_update_slice_in_dim(whole, block, (me ^ j) * rows, 0)
    return whole


def pick(whole, me, group):
    rows = whole.shape[0] // group
    return [lax.dynamic_slice_in_dim(whole, (me ^ j) * rows, rows, 0) for j in range(group)]


def columns(array, index, width):
    return lax.dynamic_slice_in_dim(array, index * width, width, 1)


def per_device(
    group,
    replicas,
    tokens,
    segments,
    cotangent,
    latent_proj,
    query_up,
    keyval_up,
    out_proj,
    gate_up,
    down_proj,
    norm_gains,
    latent_mean,
    query_mean,
    keyval_mean,
    outproj_mean,
    gateup_mean,
    down_mean,
    gains_mean,
    latent_square,
    query_square,
    keyval_square,
    outproj_square,
    gateup_square,
    down_square,
    gains_square,
):
    f32 = jnp.float32
    bf16 = jnp.bfloat16
    me = lax.axis_index("shard")
    rep = lax.axis_index("rep")
    seq_len = tokens.shape[0]
    heads = H // group
    hidden_part = FF // group
    tiles = hidden_part // TILE
    tail = hidden_part - tiles * TILE
    rows_d = D // group
    others = range(1, group)
    order = jnp.stack([me ^ j for j in range(group)]).astype(jnp.int32)

    share = rows_d // replicas
    fast = group == 4 and share % 16 == 0
    gains_rows = jnp.broadcast_to(norm_gains.astype(f32), (8,) + norm_gains.shape)
    seg_rows = jnp.broadcast_to(segments.astype(f32), (8, seq_len))
    def hidden_columns(array, index):
        gate = columns(array, index, hidden_part)
        up = lax.dynamic_slice_in_dim(array, FF + index * hidden_part, hidden_part, 1)
        cut = []
        for t in range(tiles):
            cut += [gate[:, t * TILE : (t + 1) * TILE], up[:, t * TILE : (t + 1) * TILE]]
        for last in (gate, up):
            cut.append(jnp.pad(last[:, tiles * TILE :], ((0, 0), (0, TAIL - tail))))
        return jnp.concatenate(cut, axis=1)

    share = rows_d // replicas
    cot_near = near_blocks(cotangent, group)
    if share % 16 == 0:
        own_columns, pieces, query_pad, gains_all, segs, tables = hidden_pieces(
            gate_up, query_up, gains_rows, seg_rows, group, replicas
        )
    else:
        gains_all, segs, tables = small_things(gains_rows, seg_rows, group)
        query_pad = jnp.pad(
            query_up.reshape(-1, H, HD + RD), ((0, 0), (0, 0), (0, LANES - HD - RD))
        ).reshape(-1, H * LANES)
        own_share = lax.dynamic_slice_in_dim(gate_up, rep * share, share, 0)
        own_columns = hidden_columns(gate_up, me)
        main = 2 * tiles * TILE
        pieces = [hop(hidden_columns(own_share, me ^ j), group, j) for j in others]
        pieces = jnp.concatenate(
            [piece[:, :main] for piece in pieces] + [piece[:, main:] for piece in pieces], axis=1
        )
    gathered_columns = lax.all_gather(pieces, "rep", axis=0, tiled=True)
    gains_f = gains_all.reshape(group, 8, -1)[:, 0, :].reshape(-1)
    gain_in = gains_f[:D]
    gain_query = gains_f[D : D + QR]
    gain_keyval = gains_f[D + QR : D + QR + KR]
    gain_mlp = gains_f[D + QR + KR :]

    latent_late, _ = lax.optimization_barrier((latent_proj, pieces))
    latent_parts, latent_all, normed_in, latent_w, query_w, keyval_w = latent_front(
        tokens,
        gain_in.reshape(1, D),
        gains_f[D : D + QR + KR].reshape(1, QR + KR),
        tables[0],
        latent_late,
        query_pad,
        keyval_up,
        group,
    )
    rows_in = tokens.astype(f32)
    inv_in = inverse_rms(rows_in)
    query_lat = latent_all[:, :QR]
    keyval_lat = latent_all[:, QR : QR + KR]
    inv_query = inverse_rms(query_lat)
    inv_keyval = inverse_rms(keyval_lat)

    attention = [None] * group
    latents_next = latent_parts
    for at, j in enumerate((*reversed(others), 0)):
        if at == 0:
            latents_next, cot_near = lax.optimization_barrier((latents_next, cot_near))
            cot_parts = all_blocks(cotangent, cot_near, group)
        if at == 1:
            latents_next, cot_parts = lax.optimization_barrier((latents_next, cot_parts))
        attention[j] = attend(j, latents_next, tables, segs, query_w, keyval_w, out_proj)
        latents_next, _ = lax.optimization_barrier((latent_parts, attention[j][0]))
    out_terms = [part[0] for part in attention]
    hidden = rows_in + residual_scale * scatter_sum(out_terms, group)
    inv_hidden = inverse_rms(hidden)
    normed_mlp = (hidden * inv_hidden * gain_mlp).astype(bf16)

    near = near_blocks(normed_mlp, group)
    half_tiles = tiles // 2
    if fast:
        mlp_parts = all_blocks(normed_mlp, near, group)

        def some_tiles(earlier, first, count):
            return layer_part(
                order,
                mlp_parts,
                cot_parts,
                own_columns,
                gathered_columns,
                down_proj,
                earlier,
                first,
                count,
                group,
                replicas,
            )

        early = some_tiles(None, 0, half_tiles)
        act_all, grad_late, back_all = some_tiles(early, half_tiles, tiles - half_tiles)
        cuts = [(0, half_tiles), (half_tiles, tiles)]
        grad_cuts = [early[1].reshape(D, -1), grad_late.reshape(D, -1)]
        hidden_terms = [back_all[j * seq_len : (j + 1) * seq_len] for j in range(group)]
    else:
        branch_parts = [(residual_scale * part.astype(f32)).astype(bf16) for part in cot_parts]

        def mlp_block(j, normed, earlier):
            return mlp_part(
                order,
                normed,
                branch_parts[j],
                own_columns,
                gathered_columns,
                down_proj,
                earlier,
                j,
                group,
            )

        first = mlp_block(0, normed_mlp, ())
        near, first = lax.optimization_barrier((near, first))
        mlp_parts = all_blocks(normed_mlp, near, group)
        terms = [first]
        for j in others:
            terms.append(mlp_block(j, mlp_parts[j], terms[-1][:2]))
        act_all, grad_all = terms[-1][:2]
        down_terms = [term[2] for term in terms]
        hidden_terms = [term[3] for term in terms]
        cuts = [(0, tiles)]
        grad_gateup = jnp.einsum(
            "td,tf->df", jnp.concatenate(mlp_parts), grad_all, preferred_element_type=f32
        )
        grad_cuts = [
            grad_gateup.astype(bf16)
            .reshape(group, replicas, share, -1)
            .transpose(1, 0, 2, 3)
            .reshape(D, -1)
        ]
    normed_late, _ = lax.optimization_barrier((normed_in, mlp_parts[1:]))
    normed_columns = [columns(normed_late, me, rows_d)] + [
        hop(columns(normed_late, me ^ j, rows_d), group, j) for j in others
    ]
    grad_normed_mlp = scatter_sum(hidden_terms, group)

    grad_down = down_grad(act_all, cot_parts, hidden_part, group)

    def to_owner_rows(block_rows):
        blocks = pick(block_rows, me, group)
        blocks = [blocks[0]] + [hop(blocks[j], group, j) for j in others]
        return place(blocks, me).reshape((group,) + blocks[0].shape)

    summed = [lax.psum_scatter(grad_cuts[0], "rep", scatter_dimension=0, tiled=True)]
    grad_down, summed[0] = lax.optimization_barrier((grad_down, summed[0]))
    grad_normed_mlp, grad_down = lax.optimization_barrier((grad_normed_mlp, grad_down))
    for grad_cut in grad_cuts[1:]:
        grad_cut, _ = lax.optimization_barrier((grad_cut, summed[-1]))
        summed.append(lax.psum_scatter(grad_cut, "rep", scatter_dimension=0, tiled=True))
    grad_top = cotangent.astype(f32)
    grad_gain_mlp = jnp.sum(grad_normed_mlp * hidden * inv_hidden, axis=0)
    grad_hidden = grad_top + norm_back(grad_normed_mlp * gain_mlp, hidden, inv_hidden)
    grad_attn = (residual_scale * grad_hidden).astype(bf16)

    def back_block(j, grad):
        return attend_back(
            j,
            grad,
            attention[j][1],
            attention[j][2],
            latent_parts,
            tables,
            segs,
            query_w,
            keyval_w,
            out_proj,
        )

    near = near_blocks(grad_attn, group)
    back = [back_block(0, grad_attn)]
    if fast:
        act_late, _ = lax.optimization_barrier((act_all, grad_attn))
        down_all = jnp.dot(
            act_late[:, :hidden_part], down_proj, preferred_element_type=f32
        ).astype(bf16)
        down_terms = [down_all[j * seq_len : (j + 1) * seq_len] for j in range(group)]
    near, back, down_terms = lax.optimization_barrier((near, back, down_terms))
    attn_parts = all_blocks(grad_attn, near, group)
    back += [back_block(j, attn_parts[j]) for j in others]
    owned = [to_owner_rows(rows) for rows in summed]

    def unpack(q, second):
        pieces = []
        for (start, stop), rows in zip(cuts, owned):
            for t in range(stop - start):
                first = (2 * t + second) * TILE
                pieces.append(rows[q, :, first : first + TILE])
        first = 2 * (cuts[-1][1] - cuts[-1][0]) * TILE + second * TAIL
        return pieces + [owned[-1][q, :, first : first + tail]]

    gateup_total = jnp.concatenate(
        [piece for second in (0, 1) for q in range(group) for piece in unpack(q, second)], axis=1
    )
    latent_terms = [part[0] for part in back]
    grad_latent_low = scatter_sum(latent_terms, group)
    grad_down, _ = lax.optimization_barrier((grad_down, (summed[-1], grad_latent_low)))
    down_total = lax.psum_scatter(grad_down, "rep", scatter_dimension=0, tiled=True)
    grad_normed_query = grad_latent_low[:, :QR]
    grad_normed_keyval = grad_latent_low[:, QR : QR + KR]
    grad_key_rope = grad_latent_low[:, QR + KR + HD : QR + KR + HD + RD]
    grad_gain_query = jnp.sum(grad_normed_query * query_lat * inv_query, axis=0)
    grad_gain_keyval = jnp.sum(grad_normed_keyval * keyval_lat * inv_keyval, axis=0)
    grad_latent_rows = jnp.concatenate(
        [
            norm_back(grad_normed_query * gain_query, query_lat, inv_query),
            norm_back(grad_normed_keyval * gain_keyval, keyval_lat, inv_keyval),
            grad_key_rope,
        ],
        axis=1,
    ).astype(bf16)
    grad_latent_parts = gather_blocks(grad_latent_rows, group)
    mixed_late, late_query, late_keyval, _ = lax.optimization_barrier(
        (
            [part[3] for part in attention],
            [part[1] for part in back],
            [part[2] for part in back],
            grad_latent_rows,
        )
    )
    grad_out = token_grad(mixed_late, attn_parts, 0, heads * HD, "out_grad")
    grad_query = token_grad(latent_parts, late_query, 0, QR, "query_grad")
    grad_keyval = token_grad(latent_parts, late_keyval, QR, KR, "keyval_grad")
    query_rows = QR // (group * replicas)
    keyval_rows = KR // (group * replicas)
    unit = heads * LANES
    pair_rows = group * (query_rows + keyval_rows)
    out_units = D // unit
    out_count = heads * HD // replicas
    pair = (
        jnp.concatenate(
            [
                grad_query.reshape(group, replicas, query_rows, unit),
                grad_keyval.reshape(group, replicas, keyval_rows, unit),
            ],
            axis=2,
        )
        .transpose(1, 0, 2, 3)
        .reshape(replicas, pair_rows, unit)
    )
    grad_out = grad_out.reshape(replicas, out_count, D)
    grad_out = [grad_out[:, :, k * unit : (k + 1) * unit] for k in range(out_units)]

    grad_normed_in = jnp.einsum(
        "tc,dc->td", grad_latent_rows, latent_w, preferred_element_type=f32
    )
    grad_gain_in = jnp.sum(grad_normed_in * rows_in * inv_in, axis=0)
    input_grad = grad_hidden + norm_back(grad_normed_in * gain_in, rows_in, inv_in)
    grad_gains = jnp.concatenate([grad_gain_in, grad_gain_query, grad_gain_keyval, grad_gain_mlp])
    gain_blocks = pick(grad_gains, me, group)
    gains_sum = gain_blocks[0]
    for j in others:
        gains_sum = gains_sum + hop(gain_blocks[j].astype(bf16), group, j).astype(f32)
    grad_latent = jnp.einsum(
        "td,tc->dc",
        jnp.concatenate(normed_columns, axis=0),
        jnp.concatenate(grad_latent_parts, axis=0),
        preferred_element_type=f32,
    ).astype(bf16)
    width = grad_latent.shape[1]
    latent_units = -(-width // unit)
    grad_latent = jnp.pad(
        grad_latent.reshape(replicas, share, width), ((0, 0), (0, 0), (0, latent_units * unit - width))
    )
    grad_latent = [grad_latent[:, :, k * unit : (k + 1) * unit] for k in range(latent_units)]
    gains_row = gains_sum.reshape(replicas, 1, -1).astype(bf16)
    gains_row = jnp.pad(gains_row, ((0, 0), (0, 15), (0, unit - gains_row.shape[2])))
    last = jnp.concatenate([pair] + grad_out + grad_latent + [gains_row], axis=1)
    last, down_terms = lax.optimization_barrier((last, down_terms))
    block_out = (hidden + residual_scale * scatter_sum(down_terms, group)).astype(bf16)
    last, _ = lax.optimization_barrier((last.reshape(-1, unit), down_total))
    last = lax.psum_scatter(last, "rep", scatter_dimension=0, tiled=True)
    pair_own = to_owner_rows(last[:pair_rows])
    query_total = (
        pair_own[:, :query_rows]
        .reshape(group, query_rows, heads, LANES)[..., : HD + RD]
        .transpose(1, 0, 2, 3)
        .reshape(query_rows, H * (HD + RD))
    )
    keyval_total = pair_own[:, query_rows:].transpose(1, 0, 2).reshape(keyval_rows, 2 * H * HD)

    def side_by_side(first, count, pieces):
        return jnp.concatenate(
            [last[first + k * count : first + (k + 1) * count] for k in range(pieces)], axis=1
        )

    outproj_total = side_by_side(pair_rows, out_count, out_units)
    latent_at = pair_rows + out_units * out_count
    latent_total = side_by_side(latent_at, share, latent_units)[:, :width]
    gains_total = last[latent_at + latent_units * share, : gains_mean.shape[0]]

    updates = [
        adam_step(latent_proj, latent_total, latent_mean, latent_square, D ** (-0.5), decay_rate),
        adam_step(query_up, query_total, query_mean, query_square, QR ** (-0.5), decay_rate),
        adam_step(keyval_up, keyval_total, keyval_mean, keyval_square, KR ** (-0.5), decay_rate),
        adam_step(
            out_proj,
            outproj_total,
            outproj_mean,
            outproj_square,
            max(H * HD // 512, 1) ** (-0.5),
            decay_rate,
        ),
        adam_step(gate_up, gateup_total, gateup_mean, gateup_square, D ** (-0.5), decay_rate),
        adam_step(
            down_proj, down_total, down_mean, down_square, max(FF // 32, 1) ** (-0.5), decay_rate
        ),
        adam_step(norm_gains, gains_total, gains_mean, gains_square, gain_rate, 0.0),
    ]
    return (block_out, input_grad) + tuple(value for update in updates for value in update)


def solution(mesh):
    return jax.shard_map(
        functools.partial(per_device, mesh.shape["shard"], mesh.shape["rep"]),
        mesh=mesh,
        in_specs=(
            P(("shard", "rep"), None),
            P(("shard", "rep"), None),
            P(("shard", "rep"), None),
            P("shard", None),
            P("shard", None),
            P("shard", None),
            P("shard", None),
            P("shard", None),
            P("shard", None),
            P("shard"),
            P(("shard", "rep"), None),
            P(("shard", "rep"), None),
            P(("shard", "rep"), None),
            P(("shard", "rep"), None),
            P(("shard", "rep"), None),
            P(("shard", "rep"), None),
            P(("shard", "rep")),
            P(("shard", "rep"), None),
            P(("shard", "rep"), None),
            P(("shard", "rep"), None),
            P(("shard", "rep"), None),
            P(("shard", "rep"), None),
            P(("shard", "rep"), None),
            P(("shard", "rep")),
        ),
        out_specs=(
            P(("shard", "rep"), None),
            P(("shard", "rep"), None),
            P(("shard", "rep"), None),
            P(("shard", "rep"), None),
            P(("shard", "rep"), None),
            P(("shard", "rep"), None),
            P(("shard", "rep"), None),
            P(("shard", "rep"), None),
            P(("shard", "rep"), None),
            P(("shard", "rep"), None),
            P(("shard", "rep"), None),
            P(("shard", "rep"), None),
            P(("shard", "rep"), None),
            P(("shard", "rep"), None),
            P(("shard", "rep"), None),
            P(("shard", "rep"), None),
            P(("shard", "rep"), None),
            P(("shard", "rep"), None),
            P(("shard", "rep"), None),
            P(("shard", "rep"), None),
            P(("shard", "rep")),
            P(("shard", "rep")),
            P(("shard", "rep")),
        ),
        check_vma=False,
    )
```

```python
import functools
import math

import jax
import jax.numpy as jnp
from jax import lax
from jax.experimental import pallas as pl
from jax.experimental.pallas import tpu as pltpu
from jax.sharding import PartitionSpec as P

D = 2560
H = 40
HD = 64
RD = 32
QR = 768
KR = 256
FF = 6400
STEP = 10


norm_eps = 1e-05
residual_scale = 1.4 / math.sqrt(62.0)
beta_one = 0.9
beta_two = 0.95
adam_eps = 1e-08
decay_rate = 0.1
gain_rate = 0.8


def inverse_rms(values):
    return lax.rsqrt(jnp.mean(values * values, axis=-1, keepdims=True) + norm_eps)


def norm_back(incoming, operand, inv_scale):
    return inv_scale * (
        incoming
        - operand * inv_scale * inv_scale * jnp.mean(incoming * operand, axis=-1, keepdims=True)
    )


def rotation_rates():
    rates = [0.0] * LANES
    for i in range(RD // 2):
        rates[HD + i] = rates[HD + RD // 2 + i] = 10000.0 ** (-2.0 * i / RD)
    return jnp.array([rates], jnp.float32)


def own_rows(weight, gradient):
    count = gradient.shape[0]
    start = lax.axis_index("rep") * count
    return lax.dynamic_slice_in_dim(weight, start, count, 0)


def adam_step(weight, gradient, mean_old, square_old, step_rate, decay_factor):
    weight_f = own_rows(weight, gradient).astype(jnp.float32)
    gradient = gradient.astype(jnp.float32)
    mean_new = beta_one * mean_old.astype(jnp.float32) + (1.0 - beta_one) * gradient
    square_new = beta_two * square_old.astype(jnp.float32) + (1.0 - beta_two) * gradient * gradient
    ratio = (
        mean_new
        / (1.0 - beta_one**STEP)
        / (jnp.sqrt(square_new / (1.0 - beta_two**STEP)) + adam_eps)
    )
    updated = weight_f - step_rate * (ratio + decay_factor * weight_f)
    return (updated, mean_new, square_new)


TILE = 256
TAIL = 128
LANES = 128
LATENT = QR + KR + LANES
score_scale = (HD + RD) ** (-0.5)
VMEM_BYTES = 48 * 1024 * 1024


def across(a, b):
    return lax.dot_general(a, b, (((1,), (1,)), ((), ())), preferred_element_type=jnp.float32)


def along(a, b):
    return lax.dot_general(a, b, (((1,), (0,)), ((), ())), preferred_element_type=jnp.float32)


def mlp_kernel(group, tiles, tail, rows_d, order_ref, normed_ref, branch_ref, *refs):
    blocks = refs[:group]
    tails = refs[group : 2 * group]
    down_ref, down_tail_ref = refs[2 * group : 2 * group + 2]
    out_refs = refs[-9:]
    act_ref, grad_ref, sum_ref, back_ref, whole, whole_tail, down_wide, sum_acc, back_acc = out_refs
    step = pl.program_id(0)
    bf16 = jnp.bfloat16

    for j in range(group):
        start = pl.multiple_of(order_ref[j] * rows_d, 16)
        whole[pl.ds(start, rows_d), :] = blocks[j][...]

    def part(weights, down, width):
        both = along(normed_ref[...], weights)
        gate = both[:, :width]
        up = both[:, width:]
        sigmoid = 1.0 / (1.0 + jnp.exp(-gate))
        silu = gate * sigmoid
        act = (silu * up).astype(bf16)
        grad_act = across(branch_ref[...], down)
        grad_gate = grad_act * up * sigmoid * (1.0 + gate * (1.0 - sigmoid))
        grad_up = grad_act * silu
        grad = jnp.concatenate([grad_gate.astype(bf16), grad_up.astype(bf16)], axis=1)
        return act, grad, along(act, down), across(grad, weights)

    act, grad, term, back = part(whole[...], down_ref[...], TILE)
    first = pl.multiple_of(step * TILE, TILE)
    act_ref[:, pl.ds(first, TILE)] = act
    grad_ref[:, pl.ds(pl.multiple_of(2 * first, 2 * TILE), 2 * TILE)] = grad

    @pl.when(step == 0)
    def _():
        sum_acc[...] = term
        back_acc[...] = back

    @pl.when(step > 0)
    def _():
        sum_acc[...] += term
        back_acc[...] += back

    @pl.when(step == tiles - 1)
    def _():
        for j in range(group):
            start = pl.multiple_of(order_ref[j] * rows_d, 16)
            whole_tail[pl.ds(start, rows_d), :] = tails[j][...]
        down_wide[...] = jnp.zeros_like(down_wide)
        down_wide[:tail, :] = down_tail_ref[...]
        act, grad, term, back = part(whole_tail[...], down_wide[...], TAIL)
        act_ref[:, tiles * TILE :] = act
        grad_ref[:, 2 * tiles * TILE :] = grad
        sum_ref[...] = (sum_acc[...] + term).astype(bf16)
        back_ref[...] = (back_acc[...] + back).astype(bf16)


def mlp_part(order, normed, branch, own, gathered, down, earlier, index, group):
    tokens, width = normed.shape
    hidden = down.shape[0]
    tiles = hidden // TILE
    tail = hidden - tiles * TILE
    rows_d = width // group
    bf16 = jnp.bfloat16
    f32 = jnp.float32
    fixed = lambda t: (0, 0)
    weights = [own] + [gathered] * (group - 1)
    return pl.pallas_call(
        functools.partial(mlp_kernel, group, tiles, tail, rows_d),
        grid=(tiles,),
        in_specs=[
            pl.BlockSpec(memory_space=pltpu.SMEM),
            pl.BlockSpec((tokens, width), fixed),
            pl.BlockSpec((tokens, width), fixed),
        ]
        + [pl.BlockSpec((rows_d, 2 * TILE), lambda t: (0, t))]
        + [
            pl.BlockSpec((rows_d, 2 * TILE), lambda t, j=j: (0, j * tiles + t))
            for j in range(group - 1)
        ]
        + [pl.BlockSpec((rows_d, 2 * TAIL), lambda t: (0, tiles * TILE // TAIL))]
        + [
            pl.BlockSpec(
                (rows_d, 2 * TAIL), lambda t, j=j: (0, (group - 1) * tiles * TILE // TAIL + j)
            )
            for j in range(group - 1)
        ]
        + [
            pl.BlockSpec((TILE, width), lambda t: (t, 0)),
            pl.BlockSpec((tail, width), lambda t: (tiles * TILE // tail, 0)),
        ]
        + [pl.BlockSpec(memory_space=pl.ANY)] * len(earlier),
        out_specs=[
            pl.BlockSpec((tokens, tiles * TILE + TAIL), lambda t: (index, 0)),
            pl.BlockSpec((tokens, 2 * (tiles * TILE + TAIL)), lambda t: (index, 0)),
            pl.BlockSpec((tokens, width), fixed),
            pl.BlockSpec((tokens, width), fixed),
        ],
        out_shape=[
            jax.ShapeDtypeStruct((group * tokens, tiles * TILE + TAIL), bf16),
            jax.ShapeDtypeStruct((group * tokens, 2 * (tiles * TILE + TAIL)), bf16),
            jax.ShapeDtypeStruct((tokens, width), bf16),
            jax.ShapeDtypeStruct((tokens, width), bf16),
        ],
        scratch_shapes=[
            pltpu.VMEM((width, 2 * TILE), bf16),
            pltpu.VMEM((width, 2 * TAIL), bf16),
            pltpu.VMEM((TAIL, width), bf16),
            pltpu.VMEM((tokens, width), f32),
            pltpu.VMEM((tokens, width), f32),
        ],
        input_output_aliases={5 + 2 * group + i: i for i in range(len(earlier))},
        compiler_params=pltpu.CompilerParams(vmem_limit_bytes=VMEM_BYTES),
        cost_estimate=pl.CostEstimate(
            flops=12 * tokens * width * hidden,
            bytes_accessed=6 * width * hidden + 8 * tokens * width,
            transcendentals=tokens * hidden,
        ),
        name="mlp_part",
    )(order, normed, branch, *weights, *weights, down, down, *earlier)


def layer_kernel(group, base, tiles, tail, rows_d, shares, last, order_ref, *refs):
    normed_in = refs[:group]
    top_in = refs[group : 2 * group]
    at = 2 * group
    blocks = refs[at : at + group]
    at += group
    if last:
        tails = refs[at : at + group]
        at += group
        down_ref, down_tail_ref, act_old, acc_in = refs[at : at + 4]
        at += 4
    else:
        down_ref = refs[at]
        at += 1
    act_out, grad_out, back_out = refs[at : at + 3]
    normed, turned, branch, whole, acc, stage, act_stage, in_sems, out_sems, back_sem = refs[
        at + 3 : at + 13
    ]
    if last:
        whole_tail, down_wide, tail_stage, tail_act, tail_sems = refs[at + 13 :]
    bf16 = jnp.bfloat16
    f32 = jnp.float32
    step = pl.program_id(0)
    slot = lax.rem(step, 2)
    tokens = normed_in[0].shape[0]
    width = normed.shape[1]
    rows = rows_d // shares

    def arrivals():
        copies = []
        for j in range(group):
            copies.append(
                pltpu.make_async_copy(
                    normed_in[j], normed.at[pl.ds(j * tokens, tokens), :], in_sems.at[j]
                )
            )
            copies.append(
                pltpu.make_async_copy(
                    top_in[j], branch.at[pl.ds(j * tokens, tokens), :], in_sems.at[group + j]
                )
            )
        return copies

    @pl.when(step == 0)
    def _():
        copies = arrivals()
        for copy in copies:
            copy.start()
        if last:
            pltpu.make_async_copy(acc_in, acc, back_sem).start()
        else:
            acc[...] = jnp.zeros_like(acc)
        for j in range(group):
            at = pl.ds(j * tokens, tokens)
            copies[2 * j].wait()
            turned[:, j * tokens : (j + 1) * tokens] = normed[at, :].T
            copies[2 * j + 1].wait()
            branch[at, :] = (residual_scale * branch[at, :].astype(f32)).astype(bf16)
        if last:
            pltpu.make_async_copy(acc_in, acc, back_sem).wait()

    for j in range(group):
        start = pl.multiple_of(order_ref[j] * rows_d, 16)
        whole[pl.ds(start, rows_d), :] = blocks[j][...]

    def part(weights_ref, down, wide, act_to, grad_to):
        both = along(normed[...], weights_ref[...])
        gate = both[:, :wide]
        up = both[:, wide:]
        sigmoid = 1.0 / (1.0 + jnp.exp(-gate))
        silu = gate * sigmoid
        act_to[...] = (silu * up).astype(bf16)
        grad_act = across(branch[...], down)
        grad_gate = grad_act * up * sigmoid * (1.0 + gate * (1.0 - sigmoid))
        grad_up = grad_act * silu
        grad = jnp.concatenate([grad_gate.astype(bf16), grad_up.astype(bf16)], axis=1)
        cut = 512
        for c in range(width // cut):
            here = slice(c * cut, (c + 1) * cut)
            acc[:, here] += across(grad, weights_ref[here, :])
        for g in range(group):
            result = along(turned[g * rows_d : (g + 1) * rows_d, :], grad).astype(bf16)
            for r in range(shares):
                grad_to[r, g] = result[r * rows : (r + 1) * rows, :]

    def leaving(index, slot_index):
        first = pl.multiple_of((base + index) * TILE, TILE)
        return (
            pltpu.make_async_copy(
                act_stage.at[slot_index],
                act_out.at[:, pl.ds(first, TILE)],
                out_sems.at[0, slot_index],
            ),
            pltpu.make_async_copy(
                stage.at[slot_index],
                grad_out.at[:, :, :, pl.ds(pl.multiple_of(index * 2 * TILE, 2 * TILE), 2 * TILE)],
                out_sems.at[1, slot_index],
            ),
        )

    @pl.when(step >= 2)
    def _():
        for copy in leaving(step - 2, slot):
            copy.wait()

    part(whole, down_ref[...], TILE, act_stage.at[slot], stage.at[slot])
    for copy in leaving(step, slot):
        copy.start()

    @pl.when(step == tiles - 1)
    def _():
        if last:
            for j in range(group):
                start = pl.multiple_of(order_ref[j] * rows_d, 16)
                whole_tail[pl.ds(start, rows_d), :] = tails[j][...]
            down_wide[...] = jnp.zeros_like(down_wide)
            down_wide[:tail, :] = down_tail_ref[...]
            part(whole_tail, down_wide[...], TAIL, tail_act, tail_stage)
            final = [
                pltpu.make_async_copy(
                    tail_act, act_out.at[:, pl.ds((base + tiles) * TILE, TAIL)], tail_sems.at[0]
                ),
                pltpu.make_async_copy(
                    tail_stage,
                    grad_out.at[:, :, :, pl.ds(2 * tiles * TILE, 2 * TAIL)],
                    tail_sems.at[1],
                ),
            ]
            normed[...] = acc[...].astype(bf16)
            final.append(pltpu.make_async_copy(normed, back_out, back_sem))
        else:
            final = [pltpu.make_async_copy(acc, back_out, back_sem)]
        for copy in final:
            copy.start()
        for k in range(max(tiles - 2, 0), tiles):
            for copy in leaving(k, k % 2):
                copy.wait()
        for copy in final:
            copy.wait()


def layer_part(order, normed, top, own, gathered, down, earlier, tiles_from, tiles, group, shares):
    tokens, width = normed[0].shape
    hidden = down.shape[0]
    all_tiles = hidden // TILE
    tail = hidden - all_tiles * TILE
    rows_d = width // group
    rows = rows_d // shares
    bf16 = jnp.bfloat16
    f32 = jnp.float32
    last = earlier is not None
    total = group * tokens
    once = pl.Buffered(1)
    any_spec = pl.BlockSpec(memory_space=pl.ANY)
    weights = [own] + [gathered] * (group - 1)
    in_specs = [pl.BlockSpec(memory_space=pltpu.SMEM)] + [any_spec] * (2 * group)
    in_specs += [pl.BlockSpec((rows_d, 2 * TILE), lambda t: (0, tiles_from + t))]
    in_specs += [
        pl.BlockSpec((rows_d, 2 * TILE), lambda t, j=j: (0, j * all_tiles + tiles_from + t))
        for j in range(group - 1)
    ]
    inputs = [order] + normed + top + weights
    scratch = [
        pltpu.VMEM((total, width), bf16),
        pltpu.VMEM((width, total), bf16),
        pltpu.VMEM((total, width), bf16),
        pltpu.VMEM((width, 2 * TILE), bf16),
        pltpu.VMEM((total, width), f32),
        pltpu.VMEM((2, shares, group, rows, 2 * TILE), bf16),
        pltpu.VMEM((2, total, TILE), bf16),
        pltpu.SemaphoreType.DMA((2 * group,)),
        pltpu.SemaphoreType.DMA((2, 2)),
        pltpu.SemaphoreType.DMA,
    ]
    cols = 2 * tiles * TILE
    aliases = {}
    if last:
        first_tail = all_tiles * TILE // TAIL
        in_specs += [
            pl.BlockSpec((rows_d, 2 * TAIL), lambda t: (0, first_tail), pipeline_mode=once)
        ]
        in_specs += [
            pl.BlockSpec(
                (rows_d, 2 * TAIL),
                lambda t, j=j: (0, (group - 1) * first_tail + j),
                pipeline_mode=once,
            )
            for j in range(group - 1)
        ]
        inputs += weights
        cols += 2 * TAIL
    in_specs.append(pl.BlockSpec((TILE, width), lambda t: (tiles_from + t, 0)))
    inputs.append(down)
    if last:
        in_specs.append(
            pl.BlockSpec(
                (tail, width), lambda t: (all_tiles * TILE // tail, 0), pipeline_mode=once
            )
        )
        inputs.append(down)
        in_specs += [any_spec, any_spec]
        aliases = {len(inputs): 0}
        inputs += [earlier[0], earlier[2]]
        scratch += [
            pltpu.VMEM((width, 2 * TAIL), bf16),
            pltpu.VMEM((TAIL, width), bf16),
            pltpu.VMEM((shares, group, rows, 2 * TAIL), bf16),
            pltpu.VMEM((total, TAIL), bf16),
            pltpu.SemaphoreType.DMA((2,)),
        ]
    part_hidden = tiles * TILE + (tail if last else 0)
    return pl.pallas_call(
        functools.partial(
            layer_kernel, group, tiles_from, tiles, tail, rows_d, shares, last
        ),
        grid=(tiles,),
        in_specs=in_specs,
        out_specs=[any_spec] * 3,
        out_shape=[
            jax.ShapeDtypeStruct((total, all_tiles * TILE + TAIL), bf16),
            jax.ShapeDtypeStruct((shares, group, rows, cols), bf16),
            jax.ShapeDtypeStruct((total, width), bf16 if last else f32),
        ],
        scratch_shapes=scratch,
        input_output_aliases=aliases,
        compiler_params=pltpu.CompilerParams(vmem_limit_bytes=61 * 1024 * 1024),
        cost_estimate=pl.CostEstimate(
            flops=14 * total * width * part_hidden,
            bytes_accessed=12 * width * part_hidden + 16 * total * width,
            transcendentals=total * part_hidden,
        ),
        name="layer_part",
    )(*inputs)


def down_grad_kernel(group, tokens, act_ref, *refs):
    top = refs[:group]
    out_ref, whole = refs[group:]

    @pl.when(pl.program_id(0) == 0)
    def _():
        for j in range(group):
            whole[j * tokens : (j + 1) * tokens, :] = (
                residual_scale * top[j][...].astype(jnp.float32)
            ).astype(jnp.bfloat16)

    out_ref[...] = along(act_ref[...].T, whole[...]).astype(jnp.bfloat16)


def down_grad(act_all, top_parts, hidden, group):
    tokens, width = top_parts[0].shape
    tiles = (hidden + TILE - 1) // TILE
    return pl.pallas_call(
        functools.partial(down_grad_kernel, group, tokens),
        grid=(tiles,),
        in_specs=[pl.BlockSpec((group * tokens, TILE), lambda t: (0, t))]
        + [pl.BlockSpec((tokens, width), lambda t: (0, 0))] * group,
        out_specs=pl.BlockSpec((TILE, width), lambda t: (t, 0)),
        out_shape=jax.ShapeDtypeStruct((hidden, width), jnp.bfloat16),
        scratch_shapes=[pltpu.VMEM((group * tokens, width), jnp.bfloat16)],
        compiler_params=pltpu.CompilerParams(vmem_limit_bytes=VMEM_BYTES),
        cost_estimate=pl.CostEstimate(
            flops=2 * group * tokens * width * hidden,
            bytes_accessed=2 * width * hidden + 2 * group * tokens * (width + hidden),
            transcendentals=0,
        ),
        name="down_grad",
    )(act_all, *top_parts)


def lane_index(rows):
    return lax.broadcasted_iota(jnp.int32, (rows, LANES), 1)


def turn(values, table_ref, sign):
    ahead = pltpu.roll(values, LANES - RD // 2, 1)
    behind = pltpu.roll(values, RD // 2, 1)
    return values * table_ref[0] + sign * (ahead * table_ref[1] + behind * table_ref[2])


def seg_column(seg_ref):
    return seg_ref[...].T[:, :1]


def causal_mask(seg_ref):
    tokens = seg_ref.shape[1]
    row = lax.broadcasted_iota(jnp.int32, (tokens, tokens), 0)
    col = lax.broadcasted_iota(jnp.int32, (tokens, tokens), 1)
    return (seg_column(seg_ref) == seg_ref[:1, :]) & (col <= row)


def softmax_rows(query, key, allowed):
    scores = across(query, key) * score_scale
    masked = jnp.where(allowed, scores, -1e30)
    exponent = jnp.exp(masked - jnp.max(masked, axis=1, keepdims=True))
    return exponent * (1.0 / jnp.sum(exponent, axis=1, keepdims=True))


def key_lanes(keyval, latent_ref, lane):
    return jnp.where(lane < HD, keyval, latent_ref[:, QR + KR :])


def attend_kernel(
    heads,
    latent_ref,
    table_ref,
    seg_ref,
    query_w_ref,
    keyval_w_ref,
    out_w_ref,
    term_ref,
    query_ref,
    keyval_ref,
    mixed_ref,
):
    bf16 = jnp.bfloat16
    tokens = latent_ref.shape[0]
    lane = lane_index(tokens)
    allowed = causal_mask(seg_ref)
    query = along(latent_ref[:, :QR], query_w_ref[...])
    keyval_ref[...] = along(latent_ref[:, QR : QR + KR], keyval_w_ref[...]).astype(bf16)
    even = None
    for h in range(heads):
        at = slice(h * LANES, (h + 1) * LANES)
        query_h = turn(query[:, at], table_ref, 1.0).astype(bf16)
        query_ref[:, at] = query_h
        keyval_h = keyval_ref[:, at]
        probs = softmax_rows(query_h, key_lanes(keyval_h, latent_ref, lane), allowed).astype(bf16)
        mixed = along(probs, keyval_h)
        if h % 2 == 0:
            even = pltpu.roll(mixed, HD, 1)
            if h == heads - 1:
                mixed_ref[:, h * HD :] = even[:, :HD].astype(bf16)
        else:
            mixed_ref[:, (h - 1) * HD : (h + 1) * HD] = jnp.where(lane < HD, even, mixed).astype(
                bf16
            )
    term_ref[...] = along(mixed_ref[...], out_w_ref[...]).astype(bf16)


def nth(array, index):
    return pl.BlockSpec((None,) + array.shape[1:], lambda i: (index,) + (0,) * (array.ndim - 1))


def entire(array):
    return pl.BlockSpec(array.shape, lambda i: (0,) * array.ndim)


def attend(index, latent, table, seg, query_w, keyval_w, out_w):
    tokens = latent.shape[1]
    heads = query_w.shape[1] // LANES
    width = out_w.shape[1]
    bf16 = jnp.bfloat16
    return pl.pallas_call(
        functools.partial(attend_kernel, heads),
        grid=(1,),
        out_specs=[
            pl.BlockSpec((tokens, cols), lambda i: (0, 0))
            for cols in (width, heads * LANES, heads * LANES, heads * HD)
        ],
        in_specs=[nth(array, index) for array in (latent, table, seg)]
        + [entire(array) for array in (query_w, keyval_w, out_w)],
        out_shape=[
            jax.ShapeDtypeStruct((tokens, width), bf16),
            jax.ShapeDtypeStruct((tokens, heads * LANES), bf16),
            jax.ShapeDtypeStruct((tokens, heads * LANES), bf16),
            jax.ShapeDtypeStruct((tokens, heads * HD), bf16),
        ],
        compiler_params=pltpu.CompilerParams(vmem_limit_bytes=VMEM_BYTES),
        cost_estimate=pl.CostEstimate(
            flops=2 * tokens * (heads * LANES * (QR + KR + 2 * tokens) + heads * HD * width),
            bytes_accessed=2 * (heads * LANES * (QR + KR) + heads * HD * width + tokens * width),
            transcendentals=heads * tokens * tokens,
        ),
        name="attend",
    )(latent, table, seg, query_w, keyval_w, out_w)


def attend_back_kernel(
    heads,
    grad_ref,
    query_ref,
    keyval_ref,
    latent_ref,
    table_ref,
    seg_ref,
    query_w_ref,
    keyval_w_ref,
    out_w_ref,
    term_ref,
    grad_query_ref,
    grad_keyval_ref,
):
    bf16 = jnp.bfloat16
    f32 = jnp.float32
    tokens = latent_ref.shape[0]
    lane = lane_index(tokens)
    allowed = causal_mask(seg_ref)
    grad_mixed = across(grad_ref[...], out_w_ref[...])
    grad_rope = jnp.zeros((tokens, LANES), f32)
    for h in range(heads):
        at = slice(h * LANES, (h + 1) * LANES)
        query_h = query_ref[:, at]
        keyval_h = keyval_ref[:, at]
        key_h = key_lanes(keyval_h, latent_ref, lane)
        probs = softmax_rows(query_h, key_h, allowed)
        if h % 2 == 0:
            if h == heads - 1:
                one = jnp.concatenate([grad_mixed[:, h * HD :]] * 2, axis=1)
            else:
                pair = grad_mixed[:, h * HD : (h + 2) * HD]
                one = pltpu.roll(pair, HD, 1)
        else:
            one = pair
        value_grad = jnp.where(lane >= HD, one, 0.0).astype(bf16)
        turned = probs.astype(bf16).T
        grad_values = along(turned, value_grad)
        grad_probs = across(value_grad, keyval_h)
        delta = jnp.sum(probs * grad_probs, axis=1, keepdims=True)
        grad_scores = (probs * (grad_probs - delta)).astype(bf16)
        grad_q = along(grad_scores, key_h) * score_scale
        grad_k = along(grad_scores.T, query_h) * score_scale
        grad_query_ref[:, at] = turn(grad_q, table_ref, -1.0).astype(bf16)
        grad_keyval_ref[:, at] = jnp.where(lane < HD, grad_k, grad_values).astype(bf16)
        grad_rope = grad_rope + grad_k
    rope = jnp.where(lane >= HD, turn(grad_rope, table_ref, -1.0), 0.0)
    term_ref[:, :QR] = across(grad_query_ref[...], query_w_ref[...]).astype(bf16)
    term_ref[:, QR : QR + KR] = across(grad_keyval_ref[...], keyval_w_ref[...]).astype(bf16)
    term_ref[:, QR + KR :] = rope.astype(bf16)


def attend_back(
    index, grad, query, keyval, latent, table, seg, query_w, keyval_w, out_w
):
    tokens = latent.shape[1]
    heads = query_w.shape[1] // LANES
    width = out_w.shape[1]
    bf16 = jnp.bfloat16
    return pl.pallas_call(
        functools.partial(attend_back_kernel, heads),
        grid=(1,),
        out_specs=[
            pl.BlockSpec((tokens, cols), lambda i: (0, 0))
            for cols in (LATENT, heads * LANES, heads * LANES)
        ],
        in_specs=[entire(array) for array in (grad, query, keyval)]
        + [nth(array, index) for array in (latent, table, seg)]
        + [entire(array) for array in (query_w, keyval_w, out_w)],
        out_shape=[
            jax.ShapeDtypeStruct((tokens, LATENT), bf16),
            jax.ShapeDtypeStruct((tokens, heads * LANES), bf16),
            jax.ShapeDtypeStruct((tokens, heads * LANES), bf16),
        ],
        compiler_params=pltpu.CompilerParams(vmem_limit_bytes=VMEM_BYTES),
        cost_estimate=pl.CostEstimate(
            flops=2 * tokens * (heads * LANES * (QR + KR + 5 * tokens) + heads * HD * width),
            bytes_accessed=2 * (heads * LANES * (QR + KR) + heads * HD * width + tokens * width),
            transcendentals=heads * tokens * tokens,
        ),
        name="attend_back",
    )(grad, query, keyval, latent, table, seg, query_w, keyval_w, out_w)


def token_grad_kernel(count, *refs):
    left = refs[:count]
    right = refs[count : 2 * count]
    out_ref, turned, whole = refs[2 * count :]
    tokens = left[0].shape[0]
    for j in range(count):
        turned[:, j * tokens : (j + 1) * tokens] = left[j][...].T
        whole[j * tokens : (j + 1) * tokens, :] = right[j][...]
    out_ref[...] = along(turned[...], whole[...]).astype(jnp.bfloat16)


def token_grad(left, right, first, rows, name):
    count = len(right)
    tokens, cols = right[0].shape
    at = first // rows
    if isinstance(left, list):
        left_specs = [pl.BlockSpec((tokens, rows), lambda i: (0, at))] * count
    else:
        left_specs = [
            pl.BlockSpec((None, tokens, rows), lambda i, j=j: (j, 0, at)) for j in range(count)
        ]
        left = [left] * count
    return pl.pallas_call(
        functools.partial(token_grad_kernel, count),
        grid=(1,),
        in_specs=left_specs + [pl.BlockSpec((tokens, cols), lambda i: (0, 0))] * count,
        out_specs=pl.BlockSpec((rows, cols), lambda i: (0, 0)),
        out_shape=jax.ShapeDtypeStruct((rows, cols), jnp.bfloat16),
        scratch_shapes=[
            pltpu.VMEM((rows, count * tokens), jnp.bfloat16),
            pltpu.VMEM((count * tokens, cols), jnp.bfloat16),
        ],
        compiler_params=pltpu.CompilerParams(vmem_limit_bytes=VMEM_BYTES),
        cost_estimate=pl.CostEstimate(
            flops=2 * count * tokens * rows * cols,
            bytes_accessed=2 * (rows * cols + count * tokens * (rows + cols)),
            transcendentals=0,
        ),
        name=name,
    )(*left, *right)


MESH = pl.DeviceIdType.MESH


def partner(me, distance):
    bit = 1
    while bit <= distance:
        if distance & bit:
            me = me + bit - 2 * bit * lax.rem(lax.div(me, bit), 2)
        bit *= 2
    return me


def greet(peers, count):
    barrier = pltpu.get_barrier_semaphore()
    for peer in peers:
        pl.semaphore_signal(barrier, inc=1, device_id=peer, device_id_type=MESH)
    pl.semaphore_wait(barrier, count)


def send(src, dst, sems, index, peer):
    copy = pltpu.make_async_remote_copy(
        src_ref=src,
        dst_ref=dst,
        send_sem=sems.at[0, index],
        recv_sem=sems.at[1, index],
        device_id=peer,
        device_id_type=MESH,
    )
    copy.start()
    return copy


def tile_format(gate, up, store, tiles, tail):
    bf16 = jnp.bfloat16
    for t in range(tiles):
        store(2 * t * TILE, gate[:, t * TILE : (t + 1) * TILE].astype(bf16))
        store((2 * t + 1) * TILE, up[:, t * TILE : (t + 1) * TILE].astype(bf16))
    lane = lax.broadcasted_iota(jnp.int32, (gate.shape[0], TAIL), 1)
    for second, values in enumerate((gate, up)):
        last = values[:, tiles * TILE : tiles * TILE + TAIL]
        store(
            2 * tiles * TILE + second * TAIL, jnp.where(lane < tail, last, 0.0).astype(bf16)
        )


def head_table(seg_ref, rates_ref, table_ref):
    tokens = seg_ref.shape[1]
    row = lax.broadcasted_iota(jnp.int32, (tokens, tokens), 0)
    col = lax.broadcasted_iota(jnp.int32, (tokens, tokens), 1)
    before = (seg_column(seg_ref) == seg_ref[:1, :]) & (col < row)
    position = jnp.sum(jnp.where(before, 1.0, 0.0), axis=1, keepdims=True)
    angles = position * rates_ref[...]
    sine = jnp.sin(angles)
    lane = lane_index(tokens)
    middle = HD + RD // 2
    end = HD + RD
    table_ref[0] = jnp.where(lane < end, jnp.cos(angles), 0.0)
    table_ref[1] = jnp.where((lane >= HD) & (lane < middle), -sine, 0.0)
    table_ref[2] = jnp.where((lane >= middle) & (lane < end), sine, 0.0)


def share_small(group, me, peers, gains_ref, seg_ref, gains_all_ref, segs_ref, sems):
    mine = pl.ds(pl.multiple_of(me * 8, 8), 8)
    gains_all_ref[mine, :] = gains_ref[...]
    segs_ref[0] = seg_ref[...]
    copies = []
    for j in range(1, group):
        copies.append(send(gains_ref, gains_all_ref.at[mine, :], sems, 2 * (j - 1), peers[j - 1]))
        copies.append(send(seg_ref, segs_ref.at[j], sems, 2 * (j - 1) + 1, peers[j - 1]))
    return copies


def small_kernel(
    group, gains_ref, seg_ref, rates_ref, gains_all_ref, segs_ref, table_ref, small_sems
):
    me = lax.axis_index("shard")
    rep = lax.axis_index("rep")
    peers = [(partner(me, j), rep) for j in range(1, group)]
    greet(peers, group - 1)
    for copy in share_small(group, me, peers, gains_ref, seg_ref, gains_all_ref, segs_ref, small_sems):
        copy.wait()
    for j in range(group):
        head_table(segs_ref.at[j], rates_ref, table_ref.at[j])


def columns_kernel(
    group,
    replicas,
    hidden,
    slab,
    gate_up_ref,
    gains_ref,
    seg_ref,
    rates_ref,
    own_ref,
    pieces_ref,
    gains_all_ref,
    segs_ref,
    table_ref,
    own_slab,
    slabs,
    out_pieces,
    local_sems,
    sems,
    small_sems,
):
    me = lax.axis_index("shard")
    rep = lax.axis_index("rep")
    rows, share = own_slab.shape[1], slabs.shape[1]
    tiles = hidden // TILE
    tail = hidden - tiles * TILE
    main = 2 * tiles * TILE

    def begin(index, second):
        offset = index * hidden
        return pl.multiple_of(second * FF + offset - lax.rem(offset, LANES), LANES)

    loads = []
    for j in range(1, group):
        for second in range(2):
            at = 2 * (j - 1) + second
            copy = pltpu.make_async_copy(
                gate_up_ref.at[
                    pl.ds(pl.multiple_of(rep * share, 16), share), pl.ds(begin(partner(me, j), second), slab)
                ],
                slabs.at[at],
                local_sems.at[at],
            )
            copy.start()
            loads.append(copy)
    for second in range(2):
        at = 2 * (group - 1) + second
        copy = pltpu.make_async_copy(
            gate_up_ref.at[:, pl.ds(begin(me, second), slab)],
            own_slab.at[second],
            local_sems.at[at],
        )
        copy.start()
        loads.append(copy)
    peers = [(partner(me, j), rep) for j in range(1, group)]
    greet(peers, group - 1)
    small = share_small(group, me, peers, gains_ref, seg_ref, gains_all_ref, segs_ref, small_sems)

    def shifted(ref, index):
        amount = lax.rem(slab - lax.rem(index * hidden, LANES), slab)
        return pltpu.roll(ref[...].astype(jnp.float32), amount, 1)

    sent = []
    for j in range(1, group):
        for second in range(2):
            loads[2 * (j - 1) + second].wait()

        def store(first, values, j=j):
            out_pieces[j - 1, :, first : first + values.shape[1]] = values

        tile_format(
            shifted(slabs.at[2 * (j - 1)], partner(me, j)),
            shifted(slabs.at[2 * (j - 1) + 1], partner(me, j)),
            store,
            tiles,
            tail,
        )
        sent.append(
            send(
                out_pieces.at[j - 1, :, pl.ds(0, main)],
                pieces_ref.at[:, pl.ds((j - 1) * main, main)],
                sems,
                2 * (j - 1),
                peers[j - 1],
            )
        )
        sent.append(
            send(
                out_pieces.at[j - 1, :, pl.ds(main, 2 * TAIL)],
                pieces_ref.at[:, pl.ds((group - 1) * main + (j - 1) * 2 * TAIL, 2 * TAIL)],
                sems,
                2 * (j - 1) + 1,
                peers[j - 1],
            )
        )
    for second in range(2):
        loads[2 * (group - 1) + second].wait()

    def store_own(first, values):
        own_ref[:, first : first + values.shape[1]] = values

    tile_format(
        shifted(own_slab.at[0], me), shifted(own_slab.at[1], me), store_own, tiles, tail
    )
    for copy in small:
        copy.wait()
    for j in range(group):
        head_table(segs_ref.at[j], rates_ref, table_ref.at[j])
    for copy in sent:
        copy.wait()


def small_shapes(gains, seg, group):
    rows, tokens = seg.shape
    f32 = jnp.float32
    return [
        jax.ShapeDtypeStruct((group * rows, gains.shape[1]), f32),
        jax.ShapeDtypeStruct((group, rows, tokens), f32),
        jax.ShapeDtypeStruct((group, 3, tokens, LANES), f32),
    ]


def small_things(gains, seg, group):
    return pl.pallas_call(
        functools.partial(small_kernel, group),
        in_specs=[pl.BlockSpec(memory_space=pltpu.VMEM)] * 3,
        out_specs=[pl.BlockSpec(memory_space=pltpu.VMEM)] * 3,
        out_shape=small_shapes(gains, seg, group),
        scratch_shapes=[pltpu.SemaphoreType.DMA((2, 2 * (group - 1)))],
        compiler_params=pltpu.CompilerParams(
            collective_id=3, has_side_effects=True, vmem_limit_bytes=VMEM_BYTES
        ),
        name="small_things",
    )(gains, seg, rotation_rates())


def hidden_pieces(gate_up, gains, seg, group, replicas):
    rows = gate_up.shape[0]
    share = rows // replicas
    hidden = FF // group
    whole = 2 * (hidden // TILE * TILE + TAIL)
    slab = -(-(hidden + LANES - math.gcd(hidden, LANES)) // LANES) * LANES
    bf16 = jnp.bfloat16
    others = group - 1
    return pl.pallas_call(
        functools.partial(columns_kernel, group, replicas, hidden, slab),
        in_specs=[pl.BlockSpec(memory_space=pl.ANY)] + [pl.BlockSpec(memory_space=pltpu.VMEM)] * 3,
        out_specs=[pl.BlockSpec(memory_space=pltpu.VMEM)] * 5,
        out_shape=[
            jax.ShapeDtypeStruct((rows, whole), bf16),
            jax.ShapeDtypeStruct((share, others * whole), bf16),
        ]
        + small_shapes(gains, seg, group),
        scratch_shapes=[
            pltpu.VMEM((2, rows, slab), bf16),
            pltpu.VMEM((2 * others, share, slab), bf16),
            pltpu.VMEM((others, share, whole), bf16),
            pltpu.SemaphoreType.DMA((2 * group,)),
            pltpu.SemaphoreType.DMA((2, 2 * others)),
            pltpu.SemaphoreType.DMA((2, 2 * others)),
        ],
        compiler_params=pltpu.CompilerParams(
            collective_id=1, has_side_effects=True, vmem_limit_bytes=VMEM_BYTES
        ),
        cost_estimate=pl.CostEstimate(flops=0, bytes_accessed=100_000_000, transcendentals=0),
        name="hidden_pieces",
    )(gate_up, gains, seg, rotation_rates())


def latent_kernel(
    group,
    tokens_ref,
    gains_ref,
    latent_gains_ref,
    table_ref,
    latent_proj_ref,
    query_ref,
    keyval_ref,
    parts_ref,
    rows_ref,
    normed_ref,
    latent_w_ref,
    query_w_ref,
    keyval_w_ref,
    local_sems,
    fetch_sems,
    swap_sems,
    weight_sems,
    weight_swap_sems,
    part_sems,
):
    f32 = jnp.float32
    bf16 = jnp.bfloat16
    me = lax.axis_index("shard")
    rep = lax.axis_index("rep")
    core = lax.rem(rep, 2)
    tokens = tokens_ref.shape[0]
    rows_d = latent_proj_ref.shape[0]
    half = rows_d // 2
    query_rows = query_ref.shape[0]
    keyval_rows = keyval_ref.shape[0]
    width = query_w_ref.shape[1]
    others = range(1, group)
    peers = [None] + [(partner(me, j), rep) for j in others]
    sibling = (me, rep + 1 - 2 * core)
    greet(peers[1:] + [sibling], group)

    def block(index, which):
        return pl.ds(pl.multiple_of(index * rows_d + which * half, 16), half)

    fetched = [None] + [
        send(
            latent_proj_ref.at[pl.ds(pl.multiple_of(core * half, 16), half), :],
            latent_w_ref.at[block(me, core), :],
            fetch_sems,
            j - 1,
            peers[j],
        )
        for j in others
    ]
    own = pltpu.make_async_copy(
        latent_proj_ref,
        latent_w_ref.at[pl.ds(pl.multiple_of(me * rows_d, 16), rows_d), :],
        local_sems.at[0],
    )
    own.start()
    kinds = ((query_ref, query_w_ref, query_rows), (keyval_ref, keyval_w_ref, keyval_rows))

    def weight_rows(index, rows):
        return pl.ds(pl.multiple_of(index * rows + core * (rows // 2), 16), rows // 2)

    def fetch_weights():
        return [
            send(
                ref.at[
                    pl.ds(pl.multiple_of(core * (rows // 2), 16), rows // 2),
                    pl.ds(pl.multiple_of(partner(me, j) * width, LANES), width),
                ],
                out_ref.at[weight_rows(me, rows), :],
                weight_sems,
                kind * (group - 1) + j - 1,
                peers[j],
            )
            for kind, (ref, out_ref, rows) in enumerate(kinds)
            for j in others
        ]

    def swap_weights(copies):
        swaps = []
        for kind, (ref, out_ref, rows) in enumerate(kinds):
            for j in others:
                index = kind * (group - 1) + j - 1
                copies[index].wait_recv()
                where = weight_rows(partner(me, j), rows)
                swaps.append(
                    send(
                        out_ref.at[where, :],
                        out_ref.at[where, :],
                        weight_swap_sems,
                        index,
                        sibling,
                    )
                )
        return swaps

    mine = []
    for at, (ref, out_ref, rows) in enumerate(kinds):
        copy = pltpu.make_async_copy(
            ref.at[:, pl.ds(pl.multiple_of(me * width, LANES), width)],
            out_ref.at[pl.ds(pl.multiple_of(me * rows, 16), rows), :],
            local_sems.at[1 + at],
        )
        copy.start()
        mine.append(copy)

    rows_in = tokens_ref[...].astype(f32)
    scale = lax.rsqrt(jnp.mean(rows_in * rows_in, axis=1, keepdims=True) + norm_eps)
    normed_ref[...] = (rows_in * scale * gains_ref[...]).astype(bf16)

    swaps = []
    for j in others:
        fetched[j].wait_recv()
        where = block(partner(me, j), core)
        swaps.append(
            send(latent_w_ref.at[where, :], latent_w_ref.at[where, :], swap_sems, j - 1, sibling)
        )
    weights = fetch_weights()
    own.wait()
    for copy in swaps:
        copy.wait()
    for j in others:
        fetched[j].wait_send()
    latent = along(normed_ref[...], latent_w_ref[...])
    rows_ref[...] = latent

    def rms(values):
        return values * lax.rsqrt(jnp.mean(values * values, axis=1, keepdims=True) + norm_eps)

    query = rms(latent[:, :QR]) * latent_gains_ref[:, :QR]
    keyval = rms(latent[:, QR : QR + KR]) * latent_gains_ref[:, QR:]
    rope = latent[:, QR + KR :]
    wide = jnp.concatenate(
        [jnp.zeros((tokens, HD), f32), rope, jnp.zeros((tokens, LANES - HD - RD), f32)], axis=1
    )
    parts_ref[0, :, :QR] = query.astype(bf16)
    parts_ref[0, :, QR : QR + KR] = keyval.astype(bf16)
    parts_ref[0, :, QR + KR :] = turn(wide, table_ref, 1.0).astype(bf16)

    direct = (1, 2) if group == 4 else others
    near = [
        send(parts_ref.at[0], parts_ref.at[j], part_sems, j - 1, peers[j]) for j in direct
    ]
    swaps = swap_weights(weights)
    far = []
    if group == 4:
        part = tokens // 2
        top = pl.ds(0, part)
        low = pl.ds(part, part)
        near[0].wait_recv()
        far.append(send(parts_ref.at[1, top], parts_ref.at[3, top], part_sems, 2, peers[2]))
        near[1].wait_recv()
        far.append(send(parts_ref.at[2, low], parts_ref.at[3, low], part_sems, 3, peers[1]))
        for copy in near:
            copy.wait_send()
    else:
        for copy in near:
            copy.wait()
    for copy in far + swaps + mine:
        copy.wait()
    for copy in weights:
        copy.wait_send()


def latent_front(tokens, gain_in, latent_gains, table, latent_proj, query_pad, keyval, group):
    rows = tokens.shape[0]
    heads = query_pad.shape[1] // LANES // group
    bf16 = jnp.bfloat16
    others = group - 1
    dma = pltpu.SemaphoreType.DMA
    width = latent_proj.shape[1]
    return pl.pallas_call(
        functools.partial(latent_kernel, group),
        in_specs=[pl.BlockSpec(memory_space=pltpu.VMEM)] * 7,
        out_specs=[pl.BlockSpec(memory_space=pltpu.VMEM)] * 6,
        out_shape=[
            jax.ShapeDtypeStruct((group, rows, LATENT), bf16),
            jax.ShapeDtypeStruct((rows, width), jnp.float32),
            jax.ShapeDtypeStruct((rows, D), bf16),
            jax.ShapeDtypeStruct((D, width), bf16),
            jax.ShapeDtypeStruct((QR, heads * LANES), bf16),
            jax.ShapeDtypeStruct((KR, heads * LANES), bf16),
        ],
        scratch_shapes=[
            dma((3,)),
            dma((2, others)),
            dma((2, others)),
            dma((2, 2 * others)),
            dma((2, 2 * others)),
            dma((2, max(others, 4))),
        ],
        compiler_params=pltpu.CompilerParams(
            collective_id=2, has_side_effects=True, vmem_limit_bytes=VMEM_BYTES
        ),
        cost_estimate=pl.CostEstimate(
            flops=2 * rows * D * width, bytes_accessed=60_000_000, transcendentals=0
        ),
        name="latent_front",
    )(tokens, gain_in, latent_gains, table, latent_proj, query_pad, keyval)


def hop(array, group, distance):
    return lax.ppermute(array, "shard", [(i, i ^ distance) for i in range(group)])


def near_blocks(array, group):
    return [hop(array, group, j) for j in ((1, 2) if group == 4 else range(1, group))]


def all_blocks(array, near, group):
    if group != 4:
        return [array] + near
    half = array.shape[0] // 2
    far_top = hop(near[0][:half], group, 2)
    far_low = hop(near[1][half:], group, 1)
    return [array] + near + [jnp.concatenate([far_top, far_low], axis=0)]


def gather_blocks(array, group):
    return all_blocks(array, near_blocks(array, group), group)


def scatter_sum(parts, group):
    low = jnp.bfloat16
    f32 = jnp.float32
    total = parts[0].astype(f32)
    if group != 4:
        for j in range(1, group):
            total = total + hop(parts[j], group, j).astype(f32)
        return total
    half = parts[0].shape[0] // 2
    top = hop(parts[3][:half], group, 1)
    bottom = hop(parts[3][half:], group, 2)

    def add(left, right):
        return (left.astype(f32) + right.astype(f32)).astype(low)

    two = jnp.concatenate([add(parts[2][:half], top), parts[2][half:]], axis=0)
    one = jnp.concatenate([parts[1][:half], add(parts[1][half:], bottom)], axis=0)
    return total + hop(one, group, 1).astype(f32) + hop(two, group, 2).astype(f32)


def place(blocks, me):
    rows = blocks[0].shape[0]
    whole = jnp.zeros((rows * len(blocks),) + blocks[0].shape[1:], blocks[0].dtype)
    for j, block in enumerate(blocks):
        whole = lax.dynamic_update_slice_in_dim(whole, block, (me ^ j) * rows, 0)
    return whole


def pick(whole, me, group):
    rows = whole.shape[0] // group
    return [lax.dynamic_slice_in_dim(whole, (me ^ j) * rows, rows, 0) for j in range(group)]


def columns(array, index, width):
    return lax.dynamic_slice_in_dim(array, index * width, width, 1)


def per_device(
    group,
    replicas,
    tokens,
    segments,
    cotangent,
    latent_proj,
    query_up,
    keyval_up,
    out_proj,
    gate_up,
    down_proj,
    norm_gains,
    latent_mean,
    query_mean,
    keyval_mean,
    outproj_mean,
    gateup_mean,
    down_mean,
    gains_mean,
    latent_square,
    query_square,
    keyval_square,
    outproj_square,
    gateup_square,
    down_square,
    gains_square,
):
    f32 = jnp.float32
    bf16 = jnp.bfloat16
    me = lax.axis_index("shard")
    rep = lax.axis_index("rep")
    seq_len = tokens.shape[0]
    heads = H // group
    hidden_part = FF // group
    tiles = hidden_part // TILE
    tail = hidden_part - tiles * TILE
    rows_d = D // group
    others = range(1, group)
    order = jnp.stack([me ^ j for j in range(group)]).astype(jnp.int32)

    share = rows_d // replicas
    fast = group == 4 and share % 16 == 0
    gains_rows = jnp.broadcast_to(norm_gains.astype(f32), (8,) + norm_gains.shape)
    seg_rows = jnp.broadcast_to(segments.astype(f32), (8, seq_len))
    query_pad = jnp.pad(
        query_up.reshape(-1, H, HD + RD), ((0, 0), (0, 0), (0, LANES - HD - RD))
    ).reshape(-1, H * LANES)

    def hidden_columns(array, index):
        gate = columns(array, index, hidden_part)
        up = lax.dynamic_slice_in_dim(array, FF + index * hidden_part, hidden_part, 1)
        cut = []
        for t in range(tiles):
            cut += [gate[:, t * TILE : (t + 1) * TILE], up[:, t * TILE : (t + 1) * TILE]]
        for last in (gate, up):
            cut.append(jnp.pad(last[:, tiles * TILE :], ((0, 0), (0, TAIL - tail))))
        return jnp.concatenate(cut, axis=1)

    share = rows_d // replicas
    cot_near = near_blocks(cotangent, group)
    if share % 16 == 0:
        own_columns, pieces, gains_all, segs, tables = hidden_pieces(
            gate_up, gains_rows, seg_rows, group, replicas
        )
    else:
        gains_all, segs, tables = small_things(gains_rows, seg_rows, group)
        own_share = lax.dynamic_slice_in_dim(gate_up, rep * share, share, 0)
        own_columns = hidden_columns(gate_up, me)
        main = 2 * tiles * TILE
        pieces = [hop(hidden_columns(own_share, me ^ j), group, j) for j in others]
        pieces = jnp.concatenate(
            [piece[:, :main] for piece in pieces] + [piece[:, main:] for piece in pieces], axis=1
        )
    gathered_columns = lax.all_gather(pieces, "rep", axis=0, tiled=True)
    gains_f = gains_all.reshape(group, 8, -1)[:, 0, :].reshape(-1)
    gain_in = gains_f[:D]
    gain_query = gains_f[D : D + QR]
    gain_keyval = gains_f[D + QR : D + QR + KR]
    gain_mlp = gains_f[D + QR + KR :]

    latent_late, _ = lax.optimization_barrier((latent_proj, pieces))
    latent_parts, latent_all, normed_in, latent_w, query_w, keyval_w = latent_front(
        tokens,
        gain_in.reshape(1, D),
        gains_f[D : D + QR + KR].reshape(1, QR + KR),
        tables[0],
        latent_late,
        query_pad,
        keyval_up,
        group,
    )
    rows_in = tokens.astype(f32)
    inv_in = inverse_rms(rows_in)
    query_lat = latent_all[:, :QR]
    keyval_lat = latent_all[:, QR : QR + KR]
    inv_query = inverse_rms(query_lat)
    inv_keyval = inverse_rms(keyval_lat)

    attention = [None] * group
    latents_next = latent_parts
    for at, j in enumerate((*reversed(others), 0)):
        if at == 0:
            latents_next, cot_near = lax.optimization_barrier((latents_next, cot_near))
            cot_parts = all_blocks(cotangent, cot_near, group)
        if at == 1:
            latents_next, cot_parts = lax.optimization_barrier((latents_next, cot_parts))
        attention[j] = attend(j, latents_next, tables, segs, query_w, keyval_w, out_proj)
        latents_next, _ = lax.optimization_barrier((latent_parts, attention[j][0]))
    out_terms = [part[0] for part in attention]
    hidden = rows_in + residual_scale * scatter_sum(out_terms, group)
    inv_hidden = inverse_rms(hidden)
    normed_mlp = (hidden * inv_hidden * gain_mlp).astype(bf16)

    near = near_blocks(normed_mlp, group)
    half_tiles = tiles // 2
    if fast:
        mlp_parts = all_blocks(normed_mlp, near, group)

        def some_tiles(earlier, first, count):
            return layer_part(
                order,
                mlp_parts,
                cot_parts,
                own_columns,
                gathered_columns,
                down_proj,
                earlier,
                first,
                count,
                group,
                replicas,
            )

        early = some_tiles(None, 0, half_tiles)
        act_all, grad_late, back_all = some_tiles(early, half_tiles, tiles - half_tiles)
        cuts = [(0, half_tiles), (half_tiles, tiles)]
        grad_cuts = [early[1].reshape(D, -1), grad_late.reshape(D, -1)]
        hidden_terms = [back_all[j * seq_len : (j + 1) * seq_len] for j in range(group)]
    else:
        branch_parts = [(residual_scale * part.astype(f32)).astype(bf16) for part in cot_parts]

        def mlp_block(j, normed, earlier):
            return mlp_part(
                order,
                normed,
                branch_parts[j],
                own_columns,
                gathered_columns,
                down_proj,
                earlier,
                j,
                group,
            )

        first = mlp_block(0, normed_mlp, ())
        near, first = lax.optimization_barrier((near, first))
        mlp_parts = all_blocks(normed_mlp, near, group)
        terms = [first]
        for j in others:
            terms.append(mlp_block(j, mlp_parts[j], terms[-1][:2]))
        act_all, grad_all = terms[-1][:2]
        down_terms = [term[2] for term in terms]
        hidden_terms = [term[3] for term in terms]
        cuts = [(0, tiles)]
        grad_gateup = jnp.einsum(
            "td,tf->df", jnp.concatenate(mlp_parts), grad_all, preferred_element_type=f32
        )
        grad_cuts = [
            grad_gateup.astype(bf16)
            .reshape(group, replicas, share, -1)
            .transpose(1, 0, 2, 3)
            .reshape(D, -1)
        ]
    normed_late, _ = lax.optimization_barrier((normed_in, mlp_parts[1:]))
    normed_columns = [columns(normed_late, me, rows_d)] + [
        hop(columns(normed_late, me ^ j, rows_d), group, j) for j in others
    ]
    grad_normed_mlp = scatter_sum(hidden_terms, group)

    grad_down = down_grad(act_all, cot_parts, hidden_part, group)

    def to_owner_rows(block_rows):
        blocks = pick(block_rows, me, group)
        blocks = [blocks[0]] + [hop(blocks[j], group, j) for j in others]
        return place(blocks, me).reshape((group,) + blocks[0].shape)

    summed = [lax.psum_scatter(grad_cuts[0], "rep", scatter_dimension=0, tiled=True)]
    grad_normed_mlp, summed[0] = lax.optimization_barrier((grad_normed_mlp, summed[0]))
    for grad_cut in grad_cuts[1:]:
        grad_cut, _ = lax.optimization_barrier((grad_cut, summed[-1]))
        summed.append(lax.psum_scatter(grad_cut, "rep", scatter_dimension=0, tiled=True))
    grad_top = cotangent.astype(f32)
    grad_gain_mlp = jnp.sum(grad_normed_mlp * hidden * inv_hidden, axis=0)
    grad_hidden = grad_top + norm_back(grad_normed_mlp * gain_mlp, hidden, inv_hidden)
    grad_attn = (residual_scale * grad_hidden).astype(bf16)

    def back_block(j, grad):
        return attend_back(
            j,
            grad,
            attention[j][1],
            attention[j][2],
            latent_parts,
            tables,
            segs,
            query_w,
            keyval_w,
            out_proj,
        )

    near = near_blocks(grad_attn, group)
    back = [back_block(0, grad_attn)]
    near, back, grad_down = lax.optimization_barrier((near, back, grad_down))
    attn_parts = all_blocks(grad_attn, near, group)
    back += [back_block(j, attn_parts[j]) for j in others]
    owned = [to_owner_rows(rows) for rows in summed]

    def unpack(q, second):
        pieces = []
        for (start, stop), rows in zip(cuts, owned):
            for t in range(stop - start):
                first = (2 * t + second) * TILE
                pieces.append(rows[q, :, first : first + TILE])
        first = 2 * (cuts[-1][1] - cuts[-1][0]) * TILE + second * TAIL
        return pieces + [owned[-1][q, :, first : first + tail]]

    gateup_total = jnp.concatenate(
        [piece for second in (0, 1) for q in range(group) for piece in unpack(q, second)], axis=1
    )
    latent_terms = [part[0] for part in back]
    grad_latent_low = scatter_sum(latent_terms, group)
    if fast:
        act_late, _ = lax.optimization_barrier((act_all, latent_terms))
        down_all = jnp.dot(
            act_late[:, :hidden_part], down_proj, preferred_element_type=f32
        ).astype(bf16)
        down_terms = [down_all[j * seq_len : (j + 1) * seq_len] for j in range(group)]
    grad_latent_low, down_terms = lax.optimization_barrier((grad_latent_low, down_terms))
    grad_down, _ = lax.optimization_barrier((grad_down, (summed[-1], grad_latent_low)))
    down_total = lax.psum_scatter(grad_down, "rep", scatter_dimension=0, tiled=True)
    grad_normed_query = grad_latent_low[:, :QR]
    grad_normed_keyval = grad_latent_low[:, QR : QR + KR]
    grad_key_rope = grad_latent_low[:, QR + KR + HD : QR + KR + HD + RD]
    grad_gain_query = jnp.sum(grad_normed_query * query_lat * inv_query, axis=0)
    grad_gain_keyval = jnp.sum(grad_normed_keyval * keyval_lat * inv_keyval, axis=0)
    grad_latent_rows = jnp.concatenate(
        [
            norm_back(grad_normed_query * gain_query, query_lat, inv_query),
            norm_back(grad_normed_keyval * gain_keyval, keyval_lat, inv_keyval),
            grad_key_rope,
        ],
        axis=1,
    ).astype(bf16)
    grad_latent_parts = gather_blocks(grad_latent_rows, group)
    mixed_late, late_query, late_keyval, _ = lax.optimization_barrier(
        (
            [part[3] for part in attention],
            [part[1] for part in back],
            [part[2] for part in back],
            grad_latent_rows,
        )
    )
    grad_out = token_grad(mixed_late, attn_parts, 0, heads * HD, "out_grad")
    grad_query = token_grad(latent_parts, late_query, 0, QR, "query_grad")
    grad_keyval = token_grad(latent_parts, late_keyval, QR, KR, "keyval_grad")
    query_rows = QR // (group * replicas)
    keyval_rows = KR // (group * replicas)
    unit = heads * LANES
    pair_rows = group * (query_rows + keyval_rows)
    out_units = D // unit
    out_count = heads * HD // replicas
    pair = (
        jnp.concatenate(
            [
                grad_query.reshape(group, replicas, query_rows, unit),
                grad_keyval.reshape(group, replicas, keyval_rows, unit),
            ],
            axis=2,
        )
        .transpose(1, 0, 2, 3)
        .reshape(replicas, pair_rows, unit)
    )
    grad_out = grad_out.reshape(replicas, out_count, D)
    grad_out = [grad_out[:, :, k * unit : (k + 1) * unit] for k in range(out_units)]

    grad_normed_in = jnp.einsum(
        "tc,dc->td", grad_latent_rows, latent_w, preferred_element_type=f32
    )
    grad_gain_in = jnp.sum(grad_normed_in * rows_in * inv_in, axis=0)
    input_grad = grad_hidden + norm_back(grad_normed_in * gain_in, rows_in, inv_in)
    grad_gains = jnp.concatenate([grad_gain_in, grad_gain_query, grad_gain_keyval, grad_gain_mlp])
    gain_blocks = pick(grad_gains, me, group)
    gains_sum = gain_blocks[0]
    for j in others:
        gains_sum = gains_sum + hop(gain_blocks[j].astype(bf16), group, j).astype(f32)
    grad_latent = jnp.einsum(
        "td,tc->dc",
        jnp.concatenate(normed_columns, axis=0),
        jnp.concatenate(grad_latent_parts, axis=0),
        preferred_element_type=f32,
    ).astype(bf16)
    width = grad_latent.shape[1]
    latent_units = -(-width // unit)
    grad_latent = jnp.pad(
        grad_latent.reshape(replicas, share, width), ((0, 0), (0, 0), (0, latent_units * unit - width))
    )
    grad_latent = [grad_latent[:, :, k * unit : (k + 1) * unit] for k in range(latent_units)]
    gains_row = gains_sum.reshape(replicas, 1, -1).astype(bf16)
    gains_row = jnp.pad(gains_row, ((0, 0), (0, 15), (0, unit - gains_row.shape[2])))
    last = jnp.concatenate([pair] + grad_out + grad_latent + [gains_row], axis=1)
    last, down_terms = lax.optimization_barrier((last, down_terms))
    block_out = (hidden + residual_scale * scatter_sum(down_terms, group)).astype(bf16)
    last, _ = lax.optimization_barrier((last.reshape(-1, unit), down_total))
    last = lax.psum_scatter(last, "rep", scatter_dimension=0, tiled=True)
    pair_own = to_owner_rows(last[:pair_rows])
    query_total = (
        pair_own[:, :query_rows]
        .reshape(group, query_rows, heads, LANES)[..., : HD + RD]
        .transpose(1, 0, 2, 3)
        .reshape(query_rows, H * (HD + RD))
    )
    keyval_total = pair_own[:, query_rows:].transpose(1, 0, 2).reshape(keyval_rows, 2 * H * HD)

    def side_by_side(first, count, pieces):
        return jnp.concatenate(
            [last[first + k * count : first + (k + 1) * count] for k in range(pieces)], axis=1
        )

    outproj_total = side_by_side(pair_rows, out_count, out_units)
    latent_at = pair_rows + out_units * out_count
    latent_total = side_by_side(latent_at, share, latent_units)[:, :width]
    gains_total = last[latent_at + latent_units * share, : gains_mean.shape[0]]

    updates = [
        adam_step(latent_proj, latent_total, latent_mean, latent_square, D ** (-0.5), decay_rate),
        adam_step(query_up, query_total, query_mean, query_square, QR ** (-0.5), decay_rate),
        adam_step(keyval_up, keyval_total, keyval_mean, keyval_square, KR ** (-0.5), decay_rate),
        adam_step(
            out_proj,
            outproj_total,
            outproj_mean,
            outproj_square,
            max(H * HD // 512, 1) ** (-0.5),
            decay_rate,
        ),
        adam_step(gate_up, gateup_total, gateup_mean, gateup_square, D ** (-0.5), decay_rate),
        adam_step(
            down_proj, down_total, down_mean, down_square, max(FF // 32, 1) ** (-0.5), decay_rate
        ),
        adam_step(norm_gains, gains_total, gains_mean, gains_square, gain_rate, 0.0),
    ]
    return (block_out, input_grad) + tuple(value for update in updates for value in update)


def solution(mesh):
    return jax.shard_map(
        functools.partial(per_device, mesh.shape["shard"], mesh.shape["rep"]),
        mesh=mesh,
        in_specs=(
            P(("shard", "rep"), None),
            P(("shard", "rep"), None),
            P(("shard", "rep"), None),
            P("shard", None),
            P("shard", None),
            P("shard", None),
            P("shard", None),
            P("shard", None),
            P("shard", None),
            P("shard"),
            P(("shard", "rep"), None),
            P(("shard", "rep"), None),
            P(("shard", "rep"), None),
            P(("shard", "rep"), None),
            P(("shard", "rep"), None),
            P(("shard", "rep"), None),
            P(("shard", "rep")),
            P(("shard", "rep"), None),
            P(("shard", "rep"), None),
            P(("shard", "rep"), None),
            P(("shard", "rep"), None),
            P(("shard", "rep"), None),
            P(("shard", "rep"), None),
            P(("shard", "rep")),
        ),
        out_specs=(
            P(("shard", "rep"), None),
            P(("shard", "rep"), None),
            P(("shard", "rep"), None),
            P(("shard", "rep"), None),
            P(("shard", "rep"), None),
            P(("shard", "rep"), None),
            P(("shard", "rep"), None),
            P(("shard", "rep"), None),
            P(("shard", "rep"), None),
            P(("shard", "rep"), None),
            P(("shard", "rep"), None),
            P(("shard", "rep"), None),
            P(("shard", "rep"), None),
            P(("shard", "rep"), None),
            P(("shard", "rep"), None),
            P(("shard", "rep"), None),
            P(("shard", "rep"), None),
            P(("shard", "rep"), None),
            P(("shard", "rep"), None),
            P(("shard", "rep"), None),
            P(("shard", "rep")),
            P(("shard", "rep")),
            P(("shard", "rep")),
        ),
        check_vma=False,
    )
```

```python
import functools
import math

import jax
import jax.numpy as jnp
from jax import lax
from jax.experimental import pallas as pl
from jax.experimental.pallas import tpu as pltpu
from jax.sharding import PartitionSpec as P

D = 2560
H = 40
HD = 64
RD = 32
QR = 768
KR = 256
FF = 6400
STEP = 10


norm_eps = 1e-05
residual_scale = 1.4 / math.sqrt(62.0)
beta_one = 0.9
beta_two = 0.95
adam_eps = 1e-08
decay_rate = 0.1
gain_rate = 0.8


def inverse_rms(values):
    return lax.rsqrt(jnp.mean(values * values, axis=-1, keepdims=True) + norm_eps)


def norm_back(incoming, operand, inv_scale):
    return inv_scale * (
        incoming
        - operand * inv_scale * inv_scale * jnp.mean(incoming * operand, axis=-1, keepdims=True)
    )


def rotation_rates():
    rates = [0.0] * LANES
    for i in range(RD // 2):
        rates[HD + i] = rates[HD + RD // 2 + i] = 10000.0 ** (-2.0 * i / RD)
    return jnp.array([rates], jnp.float32)


def own_rows(weight, gradient):
    count = gradient.shape[0]
    start = lax.axis_index("rep") * count
    return lax.dynamic_slice_in_dim(weight, start, count, 0)


def adam_step(weight, gradient, mean_old, square_old, step_rate, decay_factor):
    weight_f = own_rows(weight, gradient).astype(jnp.float32)
    gradient = gradient.astype(jnp.float32)
    mean_new = beta_one * mean_old.astype(jnp.float32) + (1.0 - beta_one) * gradient
    square_new = beta_two * square_old.astype(jnp.float32) + (1.0 - beta_two) * gradient * gradient
    ratio = (
        mean_new
        / (1.0 - beta_one**STEP)
        / (jnp.sqrt(square_new / (1.0 - beta_two**STEP)) + adam_eps)
    )
    updated = weight_f - step_rate * (ratio + decay_factor * weight_f)
    return (updated, mean_new, square_new)


TILE = 256
TAIL = 128
LANES = 128
LATENT = QR + KR + LANES
score_scale = (HD + RD) ** (-0.5)
VMEM_BYTES = 48 * 1024 * 1024


def across(a, b):
    return lax.dot_general(a, b, (((1,), (1,)), ((), ())), preferred_element_type=jnp.float32)


def along(a, b):
    return lax.dot_general(a, b, (((1,), (0,)), ((), ())), preferred_element_type=jnp.float32)


def mlp_kernel(group, tiles, tail, rows_d, order_ref, normed_ref, branch_ref, *refs):
    blocks = refs[:group]
    tails = refs[group : 2 * group]
    down_ref, down_tail_ref = refs[2 * group : 2 * group + 2]
    out_refs = refs[-9:]
    act_ref, grad_ref, sum_ref, back_ref, whole, whole_tail, down_wide, sum_acc, back_acc = out_refs
    step = pl.program_id(0)
    bf16 = jnp.bfloat16

    for j in range(group):
        start = pl.multiple_of(order_ref[j] * rows_d, 16)
        whole[pl.ds(start, rows_d), :] = blocks[j][...]

    def part(weights, down, width):
        both = along(normed_ref[...], weights)
        gate = both[:, :width]
        up = both[:, width:]
        sigmoid = 1.0 / (1.0 + jnp.exp(-gate))
        silu = gate * sigmoid
        act = (silu * up).astype(bf16)
        grad_act = across(branch_ref[...], down)
        grad_gate = grad_act * up * sigmoid * (1.0 + gate * (1.0 - sigmoid))
        grad_up = grad_act * silu
        grad = jnp.concatenate([grad_gate.astype(bf16), grad_up.astype(bf16)], axis=1)
        return act, grad, along(act, down), across(grad, weights)

    act, grad, term, back = part(whole[...], down_ref[...], TILE)
    first = pl.multiple_of(step * TILE, TILE)
    act_ref[:, pl.ds(first, TILE)] = act
    grad_ref[:, pl.ds(pl.multiple_of(2 * first, 2 * TILE), 2 * TILE)] = grad

    @pl.when(step == 0)
    def _():
        sum_acc[...] = term
        back_acc[...] = back

    @pl.when(step > 0)
    def _():
        sum_acc[...] += term
        back_acc[...] += back

    @pl.when(step == tiles - 1)
    def _():
        for j in range(group):
            start = pl.multiple_of(order_ref[j] * rows_d, 16)
            whole_tail[pl.ds(start, rows_d), :] = tails[j][...]
        down_wide[...] = jnp.zeros_like(down_wide)
        down_wide[:tail, :] = down_tail_ref[...]
        act, grad, term, back = part(whole_tail[...], down_wide[...], TAIL)
        act_ref[:, tiles * TILE :] = act
        grad_ref[:, 2 * tiles * TILE :] = grad
        sum_ref[...] = (sum_acc[...] + term).astype(bf16)
        back_ref[...] = (back_acc[...] + back).astype(bf16)


def mlp_part(order, normed, branch, own, gathered, down, earlier, index, group):
    tokens, width = normed.shape
    hidden = down.shape[0]
    tiles = hidden // TILE
    tail = hidden - tiles * TILE
    rows_d = width // group
    bf16 = jnp.bfloat16
    f32 = jnp.float32
    fixed = lambda t: (0, 0)
    weights = [own] + [gathered] * (group - 1)
    return pl.pallas_call(
        functools.partial(mlp_kernel, group, tiles, tail, rows_d),
        grid=(tiles,),
        in_specs=[
            pl.BlockSpec(memory_space=pltpu.SMEM),
            pl.BlockSpec((tokens, width), fixed),
            pl.BlockSpec((tokens, width), fixed),
        ]
        + [pl.BlockSpec((rows_d, 2 * TILE), lambda t: (0, t))]
        + [
            pl.BlockSpec((rows_d, 2 * TILE), lambda t, j=j: (0, j * tiles + t))
            for j in range(group - 1)
        ]
        + [pl.BlockSpec((rows_d, 2 * TAIL), lambda t: (0, tiles * TILE // TAIL))]
        + [
            pl.BlockSpec(
                (rows_d, 2 * TAIL), lambda t, j=j: (0, (group - 1) * tiles * TILE // TAIL + j)
            )
            for j in range(group - 1)
        ]
        + [
            pl.BlockSpec((TILE, width), lambda t: (t, 0)),
            pl.BlockSpec((tail, width), lambda t: (tiles * TILE // tail, 0)),
        ]
        + [pl.BlockSpec(memory_space=pl.ANY)] * len(earlier),
        out_specs=[
            pl.BlockSpec((tokens, tiles * TILE + TAIL), lambda t: (index, 0)),
            pl.BlockSpec((tokens, 2 * (tiles * TILE + TAIL)), lambda t: (index, 0)),
            pl.BlockSpec((tokens, width), fixed),
            pl.BlockSpec((tokens, width), fixed),
        ],
        out_shape=[
            jax.ShapeDtypeStruct((group * tokens, tiles * TILE + TAIL), bf16),
            jax.ShapeDtypeStruct((group * tokens, 2 * (tiles * TILE + TAIL)), bf16),
            jax.ShapeDtypeStruct((tokens, width), bf16),
            jax.ShapeDtypeStruct((tokens, width), bf16),
        ],
        scratch_shapes=[
            pltpu.VMEM((width, 2 * TILE), bf16),
            pltpu.VMEM((width, 2 * TAIL), bf16),
            pltpu.VMEM((TAIL, width), bf16),
            pltpu.VMEM((tokens, width), f32),
            pltpu.VMEM((tokens, width), f32),
        ],
        input_output_aliases={5 + 2 * group + i: i for i in range(len(earlier))},
        compiler_params=pltpu.CompilerParams(vmem_limit_bytes=VMEM_BYTES),
        cost_estimate=pl.CostEstimate(
            flops=12 * tokens * width * hidden,
            bytes_accessed=6 * width * hidden + 8 * tokens * width,
            transcendentals=tokens * hidden,
        ),
        name="mlp_part",
    )(order, normed, branch, *weights, *weights, down, down, *earlier)


def layer_kernel(group, base, tiles, tail, rows_d, shares, last, order_ref, *refs):
    normed_in = refs[:group]
    top_in = refs[group : 2 * group]
    at = 2 * group
    blocks = refs[at : at + group]
    at += group
    if last:
        tails = refs[at : at + group]
        at += group
        down_ref, down_tail_ref, act_old, acc_in = refs[at : at + 4]
        at += 4
    else:
        down_ref = refs[at]
        at += 1
    act_out, grad_out, back_out = refs[at : at + 3]
    normed, turned, branch, whole, acc, stage, act_stage, in_sems, out_sems, back_sem = refs[
        at + 3 : at + 13
    ]
    if last:
        whole_tail, down_wide, tail_stage, tail_act, tail_sems = refs[at + 13 :]
    bf16 = jnp.bfloat16
    f32 = jnp.float32
    step = pl.program_id(0)
    slot = lax.rem(step, 2)
    tokens = normed_in[0].shape[0]
    width = normed.shape[1]
    rows = rows_d // shares

    def arrivals():
        copies = []
        for j in range(group):
            copies.append(
                pltpu.make_async_copy(
                    normed_in[j], normed.at[pl.ds(j * tokens, tokens), :], in_sems.at[j]
                )
            )
            copies.append(
                pltpu.make_async_copy(
                    top_in[j], branch.at[pl.ds(j * tokens, tokens), :], in_sems.at[group + j]
                )
            )
        return copies

    @pl.when(step == 0)
    def _():
        copies = arrivals()
        for copy in copies:
            copy.start()
        if last:
            pltpu.make_async_copy(acc_in, acc, back_sem).start()
        else:
            acc[...] = jnp.zeros_like(acc)
        for j in range(group):
            at = pl.ds(j * tokens, tokens)
            copies[2 * j].wait()
            turned[:, j * tokens : (j + 1) * tokens] = normed[at, :].T
            copies[2 * j + 1].wait()
            branch[at, :] = (residual_scale * branch[at, :].astype(f32)).astype(bf16)
        if last:
            pltpu.make_async_copy(acc_in, acc, back_sem).wait()

    for j in range(group):
        start = pl.multiple_of(order_ref[j] * rows_d, 16)
        whole[pl.ds(start, rows_d), :] = blocks[j][...]

    def part(weights_ref, down, wide, act_to, grad_to):
        both = along(normed[...], weights_ref[...])
        gate = both[:, :wide]
        up = both[:, wide:]
        sigmoid = 1.0 / (1.0 + jnp.exp(-gate))
        silu = gate * sigmoid
        act_to[...] = (silu * up).astype(bf16)
        grad_act = across(branch[...], down)
        grad_gate = grad_act * up * sigmoid * (1.0 + gate * (1.0 - sigmoid))
        grad_up = grad_act * silu
        grad = jnp.concatenate([grad_gate.astype(bf16), grad_up.astype(bf16)], axis=1)
        cut = 512
        for c in range(width // cut):
            here = slice(c * cut, (c + 1) * cut)
            acc[:, here] += across(grad, weights_ref[here, :])
        for g in range(group):
            result = along(turned[g * rows_d : (g + 1) * rows_d, :], grad).astype(bf16)
            for r in range(shares):
                grad_to[r, g] = result[r * rows : (r + 1) * rows, :]

    def leaving(index, slot_index):
        first = pl.multiple_of((base + index) * TILE, TILE)
        return (
            pltpu.make_async_copy(
                act_stage.at[slot_index],
                act_out.at[:, pl.ds(first, TILE)],
                out_sems.at[0, slot_index],
            ),
            pltpu.make_async_copy(
                stage.at[slot_index],
                grad_out.at[:, :, :, pl.ds(pl.multiple_of(index * 2 * TILE, 2 * TILE), 2 * TILE)],
                out_sems.at[1, slot_index],
            ),
        )

    @pl.when(step >= 2)
    def _():
        for copy in leaving(step - 2, slot):
            copy.wait()

    part(whole, down_ref[...], TILE, act_stage.at[slot], stage.at[slot])
    for copy in leaving(step, slot):
        copy.start()

    @pl.when(step == tiles - 1)
    def _():
        if last:
            for j in range(group):
                start = pl.multiple_of(order_ref[j] * rows_d, 16)
                whole_tail[pl.ds(start, rows_d), :] = tails[j][...]
            down_wide[...] = jnp.zeros_like(down_wide)
            down_wide[:tail, :] = down_tail_ref[...]
            part(whole_tail, down_wide[...], TAIL, tail_act, tail_stage)
            final = [
                pltpu.make_async_copy(
                    tail_act, act_out.at[:, pl.ds((base + tiles) * TILE, TAIL)], tail_sems.at[0]
                ),
                pltpu.make_async_copy(
                    tail_stage,
                    grad_out.at[:, :, :, pl.ds(2 * tiles * TILE, 2 * TAIL)],
                    tail_sems.at[1],
                ),
            ]
            normed[...] = acc[...].astype(bf16)
            final.append(pltpu.make_async_copy(normed, back_out, back_sem))
        else:
            final = [pltpu.make_async_copy(acc, back_out, back_sem)]
        for copy in final:
            copy.start()
        for k in range(max(tiles - 2, 0), tiles):
            for copy in leaving(k, k % 2):
                copy.wait()
        for copy in final:
            copy.wait()


def layer_part(order, normed, top, own, gathered, down, earlier, tiles_from, tiles, group, shares):
    tokens, width = normed[0].shape
    hidden = down.shape[0]
    all_tiles = hidden // TILE
    tail = hidden - all_tiles * TILE
    rows_d = width // group
    rows = rows_d // shares
    bf16 = jnp.bfloat16
    f32 = jnp.float32
    last = earlier is not None
    total = group * tokens
    once = pl.Buffered(1)
    any_spec = pl.BlockSpec(memory_space=pl.ANY)
    weights = [own] + [gathered] * (group - 1)
    in_specs = [pl.BlockSpec(memory_space=pltpu.SMEM)] + [any_spec] * (2 * group)
    in_specs += [pl.BlockSpec((rows_d, 2 * TILE), lambda t: (0, tiles_from + t))]
    in_specs += [
        pl.BlockSpec((rows_d, 2 * TILE), lambda t, j=j: (0, j * all_tiles + tiles_from + t))
        for j in range(group - 1)
    ]
    inputs = [order] + normed + top + weights
    scratch = [
        pltpu.VMEM((total, width), bf16),
        pltpu.VMEM((width, total), bf16),
        pltpu.VMEM((total, width), bf16),
        pltpu.VMEM((width, 2 * TILE), bf16),
        pltpu.VMEM((total, width), f32),
        pltpu.VMEM((2, shares, group, rows, 2 * TILE), bf16),
        pltpu.VMEM((2, total, TILE), bf16),
        pltpu.SemaphoreType.DMA((2 * group,)),
        pltpu.SemaphoreType.DMA((2, 2)),
        pltpu.SemaphoreType.DMA,
    ]
    cols = 2 * tiles * TILE
    aliases = {}
    if last:
        first_tail = all_tiles * TILE // TAIL
        in_specs += [
            pl.BlockSpec((rows_d, 2 * TAIL), lambda t: (0, first_tail), pipeline_mode=once)
        ]
        in_specs += [
            pl.BlockSpec(
                (rows_d, 2 * TAIL),
                lambda t, j=j: (0, (group - 1) * first_tail + j),
                pipeline_mode=once,
            )
            for j in range(group - 1)
        ]
        inputs += weights
        cols += 2 * TAIL
    in_specs.append(pl.BlockSpec((TILE, width), lambda t: (tiles_from + t, 0)))
    inputs.append(down)
    if last:
        in_specs.append(
            pl.BlockSpec(
                (tail, width), lambda t: (all_tiles * TILE // tail, 0), pipeline_mode=once
            )
        )
        inputs.append(down)
        in_specs += [any_spec, any_spec]
        aliases = {len(inputs): 0}
        inputs += [earlier[0], earlier[2]]
        scratch += [
            pltpu.VMEM((width, 2 * TAIL), bf16),
            pltpu.VMEM((TAIL, width), bf16),
            pltpu.VMEM((shares, group, rows, 2 * TAIL), bf16),
            pltpu.VMEM((total, TAIL), bf16),
            pltpu.SemaphoreType.DMA((2,)),
        ]
    part_hidden = tiles * TILE + (tail if last else 0)
    return pl.pallas_call(
        functools.partial(
            layer_kernel, group, tiles_from, tiles, tail, rows_d, shares, last
        ),
        grid=(tiles,),
        in_specs=in_specs,
        out_specs=[any_spec] * 3,
        out_shape=[
            jax.ShapeDtypeStruct((total, all_tiles * TILE + TAIL), bf16),
            jax.ShapeDtypeStruct((shares, group, rows, cols), bf16),
            jax.ShapeDtypeStruct((total, width), bf16 if last else f32),
        ],
        scratch_shapes=scratch,
        input_output_aliases=aliases,
        compiler_params=pltpu.CompilerParams(vmem_limit_bytes=61 * 1024 * 1024),
        cost_estimate=pl.CostEstimate(
            flops=14 * total * width * part_hidden,
            bytes_accessed=12 * width * part_hidden + 16 * total * width,
            transcendentals=total * part_hidden,
        ),
        name="layer_part",
    )(*inputs)


def down_grad_kernel(group, tokens, act_ref, *refs):
    top = refs[:group]
    out_ref, whole = refs[group:]

    @pl.when(pl.program_id(0) == 0)
    def _():
        for j in range(group):
            whole[j * tokens : (j + 1) * tokens, :] = (
                residual_scale * top[j][...].astype(jnp.float32)
            ).astype(jnp.bfloat16)

    out_ref[...] = along(act_ref[...].T, whole[...]).astype(jnp.bfloat16)


def down_grad(act_all, top_parts, hidden, group):
    tokens, width = top_parts[0].shape
    tiles = (hidden + TILE - 1) // TILE
    return pl.pallas_call(
        functools.partial(down_grad_kernel, group, tokens),
        grid=(tiles,),
        in_specs=[pl.BlockSpec((group * tokens, TILE), lambda t: (0, t))]
        + [pl.BlockSpec((tokens, width), lambda t: (0, 0))] * group,
        out_specs=pl.BlockSpec((TILE, width), lambda t: (t, 0)),
        out_shape=jax.ShapeDtypeStruct((hidden, width), jnp.bfloat16),
        scratch_shapes=[pltpu.VMEM((group * tokens, width), jnp.bfloat16)],
        compiler_params=pltpu.CompilerParams(vmem_limit_bytes=VMEM_BYTES),
        cost_estimate=pl.CostEstimate(
            flops=2 * group * tokens * width * hidden,
            bytes_accessed=2 * width * hidden + 2 * group * tokens * (width + hidden),
            transcendentals=0,
        ),
        name="down_grad",
    )(act_all, *top_parts)


def lane_index(rows):
    return lax.broadcasted_iota(jnp.int32, (rows, LANES), 1)


def turn(values, table_ref, sign):
    ahead = pltpu.roll(values, LANES - RD // 2, 1)
    behind = pltpu.roll(values, RD // 2, 1)
    return values * table_ref[0] + sign * (ahead * table_ref[1] + behind * table_ref[2])


def seg_column(seg_ref):
    return seg_ref[...].T[:, :1]


def causal_mask(seg_ref):
    tokens = seg_ref.shape[1]
    row = lax.broadcasted_iota(jnp.int32, (tokens, tokens), 0)
    col = lax.broadcasted_iota(jnp.int32, (tokens, tokens), 1)
    return (seg_column(seg_ref) == seg_ref[:1, :]) & (col <= row)


def softmax_rows(query, key, allowed):
    scores = across(query, key) * score_scale
    masked = jnp.where(allowed, scores, -1e30)
    exponent = jnp.exp(masked - jnp.max(masked, axis=1, keepdims=True))
    return exponent * (1.0 / jnp.sum(exponent, axis=1, keepdims=True))


def key_lanes(keyval, latent_ref, lane):
    return jnp.where(lane < HD, keyval, latent_ref[:, QR + KR :])


def attend_kernel(
    heads,
    latent_ref,
    table_ref,
    seg_ref,
    query_w_ref,
    keyval_w_ref,
    out_w_ref,
    term_ref,
    query_ref,
    keyval_ref,
    mixed_ref,
):
    bf16 = jnp.bfloat16
    tokens = latent_ref.shape[0]
    lane = lane_index(tokens)
    allowed = causal_mask(seg_ref)
    query = along(latent_ref[:, :QR], query_w_ref[...])
    keyval_ref[...] = along(latent_ref[:, QR : QR + KR], keyval_w_ref[...]).astype(bf16)
    even = None
    for h in range(heads):
        at = slice(h * LANES, (h + 1) * LANES)
        query_h = turn(query[:, at], table_ref, 1.0).astype(bf16)
        query_ref[:, at] = query_h
        keyval_h = keyval_ref[:, at]
        probs = softmax_rows(query_h, key_lanes(keyval_h, latent_ref, lane), allowed).astype(bf16)
        mixed = along(probs, keyval_h)
        if h % 2 == 0:
            even = pltpu.roll(mixed, HD, 1)
            if h == heads - 1:
                mixed_ref[:, h * HD :] = even[:, :HD].astype(bf16)
        else:
            mixed_ref[:, (h - 1) * HD : (h + 1) * HD] = jnp.where(lane < HD, even, mixed).astype(
                bf16
            )
    term_ref[...] = along(mixed_ref[...], out_w_ref[...]).astype(bf16)


def nth(array, index):
    return pl.BlockSpec((None,) + array.shape[1:], lambda i: (index,) + (0,) * (array.ndim - 1))


def entire(array):
    return pl.BlockSpec(array.shape, lambda i: (0,) * array.ndim)


def attend(index, latent, table, seg, query_w, keyval_w, out_w):
    tokens = latent.shape[1]
    heads = query_w.shape[1] // LANES
    width = out_w.shape[1]
    bf16 = jnp.bfloat16
    return pl.pallas_call(
        functools.partial(attend_kernel, heads),
        grid=(1,),
        out_specs=[
            pl.BlockSpec((tokens, cols), lambda i: (0, 0))
            for cols in (width, heads * LANES, heads * LANES, heads * HD)
        ],
        in_specs=[nth(array, index) for array in (latent, table, seg)]
        + [entire(array) for array in (query_w, keyval_w, out_w)],
        out_shape=[
            jax.ShapeDtypeStruct((tokens, width), bf16),
            jax.ShapeDtypeStruct((tokens, heads * LANES), bf16),
            jax.ShapeDtypeStruct((tokens, heads * LANES), bf16),
            jax.ShapeDtypeStruct((tokens, heads * HD), bf16),
        ],
        compiler_params=pltpu.CompilerParams(vmem_limit_bytes=VMEM_BYTES),
        cost_estimate=pl.CostEstimate(
            flops=2 * tokens * (heads * LANES * (QR + KR + 2 * tokens) + heads * HD * width),
            bytes_accessed=2 * (heads * LANES * (QR + KR) + heads * HD * width + tokens * width),
            transcendentals=heads * tokens * tokens,
        ),
        name="attend",
    )(latent, table, seg, query_w, keyval_w, out_w)


def attend_back_kernel(
    heads,
    grad_ref,
    query_ref,
    keyval_ref,
    latent_ref,
    table_ref,
    seg_ref,
    query_w_ref,
    keyval_w_ref,
    out_w_ref,
    term_ref,
    grad_query_ref,
    grad_keyval_ref,
):
    bf16 = jnp.bfloat16
    f32 = jnp.float32
    tokens = latent_ref.shape[0]
    lane = lane_index(tokens)
    allowed = causal_mask(seg_ref)
    grad_mixed = across(grad_ref[...], out_w_ref[...])
    grad_rope = jnp.zeros((tokens, LANES), f32)
    for h in range(heads):
        at = slice(h * LANES, (h + 1) * LANES)
        query_h = query_ref[:, at]
        keyval_h = keyval_ref[:, at]
        key_h = key_lanes(keyval_h, latent_ref, lane)
        probs = softmax_rows(query_h, key_h, allowed)
        if h % 2 == 0:
            if h == heads - 1:
                one = jnp.concatenate([grad_mixed[:, h * HD :]] * 2, axis=1)
            else:
                pair = grad_mixed[:, h * HD : (h + 2) * HD]
                one = pltpu.roll(pair, HD, 1)
        else:
            one = pair
        value_grad = jnp.where(lane >= HD, one, 0.0).astype(bf16)
        turned = probs.astype(bf16).T
        grad_values = along(turned, value_grad)
        grad_probs = across(value_grad, keyval_h)
        delta = jnp.sum(probs * grad_probs, axis=1, keepdims=True)
        grad_scores = (probs * (grad_probs - delta)).astype(bf16)
        grad_q = along(grad_scores, key_h) * score_scale
        grad_k = along(grad_scores.T, query_h) * score_scale
        grad_query_ref[:, at] = turn(grad_q, table_ref, -1.0).astype(bf16)
        grad_keyval_ref[:, at] = jnp.where(lane < HD, grad_k, grad_values).astype(bf16)
        grad_rope = grad_rope + grad_k
    rope = jnp.where(lane >= HD, turn(grad_rope, table_ref, -1.0), 0.0)
    term_ref[:, :QR] = across(grad_query_ref[...], query_w_ref[...]).astype(bf16)
    term_ref[:, QR : QR + KR] = across(grad_keyval_ref[...], keyval_w_ref[...]).astype(bf16)
    term_ref[:, QR + KR :] = rope.astype(bf16)


def attend_back(
    index, grad, query, keyval, latent, table, seg, query_w, keyval_w, out_w
):
    tokens = latent.shape[1]
    heads = query_w.shape[1] // LANES
    width = out_w.shape[1]
    bf16 = jnp.bfloat16
    return pl.pallas_call(
        functools.partial(attend_back_kernel, heads),
        grid=(1,),
        out_specs=[
            pl.BlockSpec((tokens, cols), lambda i: (0, 0))
            for cols in (LATENT, heads * LANES, heads * LANES)
        ],
        in_specs=[entire(array) for array in (grad, query, keyval)]
        + [nth(array, index) for array in (latent, table, seg)]
        + [entire(array) for array in (query_w, keyval_w, out_w)],
        out_shape=[
            jax.ShapeDtypeStruct((tokens, LATENT), bf16),
            jax.ShapeDtypeStruct((tokens, heads * LANES), bf16),
            jax.ShapeDtypeStruct((tokens, heads * LANES), bf16),
        ],
        compiler_params=pltpu.CompilerParams(vmem_limit_bytes=VMEM_BYTES),
        cost_estimate=pl.CostEstimate(
            flops=2 * tokens * (heads * LANES * (QR + KR + 5 * tokens) + heads * HD * width),
            bytes_accessed=2 * (heads * LANES * (QR + KR) + heads * HD * width + tokens * width),
            transcendentals=heads * tokens * tokens,
        ),
        name="attend_back",
    )(grad, query, keyval, latent, table, seg, query_w, keyval_w, out_w)


def token_grad_kernel(count, *refs):
    left = refs[:count]
    right = refs[count : 2 * count]
    out_ref, turned, whole = refs[2 * count :]
    tokens = left[0].shape[0]
    for j in range(count):
        turned[:, j * tokens : (j + 1) * tokens] = left[j][...].T
        whole[j * tokens : (j + 1) * tokens, :] = right[j][...]
    out_ref[...] = along(turned[...], whole[...]).astype(jnp.bfloat16)


def token_grad(left, right, first, rows, name):
    count = len(right)
    tokens, cols = right[0].shape
    at = first // rows
    if isinstance(left, list):
        left_specs = [pl.BlockSpec((tokens, rows), lambda i: (0, at))] * count
    else:
        left_specs = [
            pl.BlockSpec((None, tokens, rows), lambda i, j=j: (j, 0, at)) for j in range(count)
        ]
        left = [left] * count
    return pl.pallas_call(
        functools.partial(token_grad_kernel, count),
        grid=(1,),
        in_specs=left_specs + [pl.BlockSpec((tokens, cols), lambda i: (0, 0))] * count,
        out_specs=pl.BlockSpec((rows, cols), lambda i: (0, 0)),
        out_shape=jax.ShapeDtypeStruct((rows, cols), jnp.bfloat16),
        scratch_shapes=[
            pltpu.VMEM((rows, count * tokens), jnp.bfloat16),
            pltpu.VMEM((count * tokens, cols), jnp.bfloat16),
        ],
        compiler_params=pltpu.CompilerParams(vmem_limit_bytes=VMEM_BYTES),
        cost_estimate=pl.CostEstimate(
            flops=2 * count * tokens * rows * cols,
            bytes_accessed=2 * (rows * cols + count * tokens * (rows + cols)),
            transcendentals=0,
        ),
        name=name,
    )(*left, *right)


MESH = pl.DeviceIdType.MESH


def partner(me, distance):
    bit = 1
    while bit <= distance:
        if distance & bit:
            me = me + bit - 2 * bit * lax.rem(lax.div(me, bit), 2)
        bit *= 2
    return me


def greet(peers, count):
    barrier = pltpu.get_barrier_semaphore()
    for peer in peers:
        pl.semaphore_signal(barrier, inc=1, device_id=peer, device_id_type=MESH)
    pl.semaphore_wait(barrier, count)


def send(src, dst, sems, index, peer):
    copy = pltpu.make_async_remote_copy(
        src_ref=src,
        dst_ref=dst,
        send_sem=sems.at[0, index],
        recv_sem=sems.at[1, index],
        device_id=peer,
        device_id_type=MESH,
    )
    copy.start()
    return copy


def tile_format(gate, up, store, tiles, tail):
    bf16 = jnp.bfloat16
    for t in range(tiles):
        store(2 * t * TILE, gate[:, t * TILE : (t + 1) * TILE].astype(bf16))
        store((2 * t + 1) * TILE, up[:, t * TILE : (t + 1) * TILE].astype(bf16))
    lane = lax.broadcasted_iota(jnp.int32, (gate.shape[0], TAIL), 1)
    for second, values in enumerate((gate, up)):
        last = values[:, tiles * TILE : tiles * TILE + TAIL]
        store(
            2 * tiles * TILE + second * TAIL, jnp.where(lane < tail, last, 0.0).astype(bf16)
        )


def head_table(seg_ref, rates_ref, table_ref):
    tokens = seg_ref.shape[1]
    row = lax.broadcasted_iota(jnp.int32, (tokens, tokens), 0)
    col = lax.broadcasted_iota(jnp.int32, (tokens, tokens), 1)
    before = (seg_column(seg_ref) == seg_ref[:1, :]) & (col < row)
    position = jnp.sum(jnp.where(before, 1.0, 0.0), axis=1, keepdims=True)
    angles = position * rates_ref[...]
    sine = jnp.sin(angles)
    lane = lane_index(tokens)
    middle = HD + RD // 2
    end = HD + RD
    table_ref[0] = jnp.where(lane < end, jnp.cos(angles), 0.0)
    table_ref[1] = jnp.where((lane >= HD) & (lane < middle), -sine, 0.0)
    table_ref[2] = jnp.where((lane >= middle) & (lane < end), sine, 0.0)


def share_small(group, me, peers, gains_ref, seg_ref, gains_all_ref, segs_ref, sems):
    mine = pl.ds(pl.multiple_of(me * 8, 8), 8)
    gains_all_ref[mine, :] = gains_ref[...]
    segs_ref[0] = seg_ref[...]
    copies = []
    for j in range(1, group):
        copies.append(send(gains_ref, gains_all_ref.at[mine, :], sems, 2 * (j - 1), peers[j - 1]))
        copies.append(send(seg_ref, segs_ref.at[j], sems, 2 * (j - 1) + 1, peers[j - 1]))
    return copies


def small_kernel(
    group, gains_ref, seg_ref, rates_ref, gains_all_ref, segs_ref, table_ref, small_sems
):
    me = lax.axis_index("shard")
    rep = lax.axis_index("rep")
    peers = [(partner(me, j), rep) for j in range(1, group)]
    greet(peers, group - 1)
    for copy in share_small(group, me, peers, gains_ref, seg_ref, gains_all_ref, segs_ref, small_sems):
        copy.wait()
    for j in range(group):
        head_table(segs_ref.at[j], rates_ref, table_ref.at[j])


def columns_kernel(
    group,
    replicas,
    hidden,
    slab,
    gate_up_ref,
    gains_ref,
    seg_ref,
    rates_ref,
    own_ref,
    pieces_ref,
    gains_all_ref,
    segs_ref,
    table_ref,
    own_slab,
    slabs,
    out_pieces,
    local_sems,
    sems,
    small_sems,
):
    me = lax.axis_index("shard")
    rep = lax.axis_index("rep")
    rows, share = own_slab.shape[1], slabs.shape[1]
    tiles = hidden // TILE
    tail = hidden - tiles * TILE
    main = 2 * tiles * TILE

    def begin(index, second):
        offset = index * hidden
        return pl.multiple_of(second * FF + offset - lax.rem(offset, LANES), LANES)

    loads = []
    for j in range(1, group):
        for second in range(2):
            at = 2 * (j - 1) + second
            copy = pltpu.make_async_copy(
                gate_up_ref.at[
                    pl.ds(pl.multiple_of(rep * share, 16), share), pl.ds(begin(partner(me, j), second), slab)
                ],
                slabs.at[at],
                local_sems.at[at],
            )
            copy.start()
            loads.append(copy)
    for second in range(2):
        at = 2 * (group - 1) + second
        copy = pltpu.make_async_copy(
            gate_up_ref.at[:, pl.ds(begin(me, second), slab)],
            own_slab.at[second],
            local_sems.at[at],
        )
        copy.start()
        loads.append(copy)
    peers = [(partner(me, j), rep) for j in range(1, group)]
    greet(peers, group - 1)
    small = share_small(group, me, peers, gains_ref, seg_ref, gains_all_ref, segs_ref, small_sems)

    def shifted(ref, index):
        amount = lax.rem(slab - lax.rem(index * hidden, LANES), slab)
        return pltpu.roll(ref[...].astype(jnp.float32), amount, 1)

    sent = []
    for j in range(1, group):
        for second in range(2):
            loads[2 * (j - 1) + second].wait()

        def store(first, values, j=j):
            out_pieces[j - 1, :, first : first + values.shape[1]] = values

        tile_format(
            shifted(slabs.at[2 * (j - 1)], partner(me, j)),
            shifted(slabs.at[2 * (j - 1) + 1], partner(me, j)),
            store,
            tiles,
            tail,
        )
        sent.append(
            send(
                out_pieces.at[j - 1, :, pl.ds(0, main)],
                pieces_ref.at[:, pl.ds((j - 1) * main, main)],
                sems,
                2 * (j - 1),
                peers[j - 1],
            )
        )
        sent.append(
            send(
                out_pieces.at[j - 1, :, pl.ds(main, 2 * TAIL)],
                pieces_ref.at[:, pl.ds((group - 1) * main + (j - 1) * 2 * TAIL, 2 * TAIL)],
                sems,
                2 * (j - 1) + 1,
                peers[j - 1],
            )
        )
    for second in range(2):
        loads[2 * (group - 1) + second].wait()

    def store_own(first, values):
        own_ref[:, first : first + values.shape[1]] = values

    tile_format(
        shifted(own_slab.at[0], me), shifted(own_slab.at[1], me), store_own, tiles, tail
    )
    for copy in small:
        copy.wait()
    for j in range(group):
        head_table(segs_ref.at[j], rates_ref, table_ref.at[j])
    for copy in sent:
        copy.wait()


def small_shapes(gains, seg, group):
    rows, tokens = seg.shape
    f32 = jnp.float32
    return [
        jax.ShapeDtypeStruct((group * rows, gains.shape[1]), f32),
        jax.ShapeDtypeStruct((group, rows, tokens), f32),
        jax.ShapeDtypeStruct((group, 3, tokens, LANES), f32),
    ]


def small_things(gains, seg, group):
    return pl.pallas_call(
        functools.partial(small_kernel, group),
        in_specs=[pl.BlockSpec(memory_space=pltpu.VMEM)] * 3,
        out_specs=[pl.BlockSpec(memory_space=pltpu.VMEM)] * 3,
        out_shape=small_shapes(gains, seg, group),
        scratch_shapes=[pltpu.SemaphoreType.DMA((2, 2 * (group - 1)))],
        compiler_params=pltpu.CompilerParams(
            collective_id=3, has_side_effects=True, vmem_limit_bytes=VMEM_BYTES
        ),
        name="small_things",
    )(gains, seg, rotation_rates())


def hidden_pieces(gate_up, gains, seg, group, replicas):
    rows = gate_up.shape[0]
    share = rows // replicas
    hidden = FF // group
    whole = 2 * (hidden // TILE * TILE + TAIL)
    slab = -(-(hidden + LANES - math.gcd(hidden, LANES)) // LANES) * LANES
    bf16 = jnp.bfloat16
    others = group - 1
    return pl.pallas_call(
        functools.partial(columns_kernel, group, replicas, hidden, slab),
        in_specs=[pl.BlockSpec(memory_space=pl.ANY)] + [pl.BlockSpec(memory_space=pltpu.VMEM)] * 3,
        out_specs=[pl.BlockSpec(memory_space=pltpu.VMEM)] * 5,
        out_shape=[
            jax.ShapeDtypeStruct((rows, whole), bf16),
            jax.ShapeDtypeStruct((share, others * whole), bf16),
        ]
        + small_shapes(gains, seg, group),
        scratch_shapes=[
            pltpu.VMEM((2, rows, slab), bf16),
            pltpu.VMEM((2 * others, share, slab), bf16),
            pltpu.VMEM((others, share, whole), bf16),
            pltpu.SemaphoreType.DMA((2 * group,)),
            pltpu.SemaphoreType.DMA((2, 2 * others)),
            pltpu.SemaphoreType.DMA((2, 2 * others)),
        ],
        compiler_params=pltpu.CompilerParams(
            collective_id=1, has_side_effects=True, vmem_limit_bytes=VMEM_BYTES
        ),
        cost_estimate=pl.CostEstimate(flops=0, bytes_accessed=100_000_000, transcendentals=0),
        name="hidden_pieces",
    )(gate_up, gains, seg, rotation_rates())


def latent_kernel(
    group,
    tokens_ref,
    gains_ref,
    latent_gains_ref,
    table_ref,
    latent_proj_ref,
    query_ref,
    keyval_ref,
    parts_ref,
    rows_ref,
    normed_ref,
    latent_w_ref,
    query_w_ref,
    keyval_w_ref,
    local_sems,
    fetch_sems,
    swap_sems,
    weight_sems,
    weight_swap_sems,
    part_sems,
):
    f32 = jnp.float32
    bf16 = jnp.bfloat16
    me = lax.axis_index("shard")
    rep = lax.axis_index("rep")
    core = lax.rem(rep, 2)
    tokens = tokens_ref.shape[0]
    rows_d = latent_proj_ref.shape[0]
    half = rows_d // 2
    query_rows = query_ref.shape[0]
    keyval_rows = keyval_ref.shape[0]
    width = query_w_ref.shape[1]
    others = range(1, group)
    peers = [None] + [(partner(me, j), rep) for j in others]
    sibling = (me, rep + 1 - 2 * core)
    greet(peers[1:] + [sibling], group)

    def block(index, which):
        return pl.ds(pl.multiple_of(index * rows_d + which * half, 16), half)

    fetched = [None] + [
        send(
            latent_proj_ref.at[pl.ds(pl.multiple_of(core * half, 16), half), :],
            latent_w_ref.at[block(me, core), :],
            fetch_sems,
            j - 1,
            peers[j],
        )
        for j in others
    ]
    own = pltpu.make_async_copy(
        latent_proj_ref,
        latent_w_ref.at[pl.ds(pl.multiple_of(me * rows_d, 16), rows_d), :],
        local_sems.at[0],
    )
    own.start()
    kinds = ((query_ref, query_w_ref, query_rows), (keyval_ref, keyval_w_ref, keyval_rows))

    def weight_rows(index, rows):
        return pl.ds(pl.multiple_of(index * rows + core * (rows // 2), 16), rows // 2)

    def fetch_weights():
        return [
            send(
                ref.at[
                    pl.ds(pl.multiple_of(core * (rows // 2), 16), rows // 2),
                    pl.ds(pl.multiple_of(partner(me, j) * width, LANES), width),
                ],
                out_ref.at[weight_rows(me, rows), :],
                weight_sems,
                kind * (group - 1) + j - 1,
                peers[j],
            )
            for kind, (ref, out_ref, rows) in enumerate(kinds)
            for j in others
        ]

    def swap_weights(copies):
        swaps = []
        for kind, (ref, out_ref, rows) in enumerate(kinds):
            for j in others:
                index = kind * (group - 1) + j - 1
                copies[index].wait_recv()
                where = weight_rows(partner(me, j), rows)
                swaps.append(
                    send(
                        out_ref.at[where, :],
                        out_ref.at[where, :],
                        weight_swap_sems,
                        index,
                        sibling,
                    )
                )
        return swaps

    mine = []
    for at, (ref, out_ref, rows) in enumerate(kinds):
        copy = pltpu.make_async_copy(
            ref.at[:, pl.ds(pl.multiple_of(me * width, LANES), width)],
            out_ref.at[pl.ds(pl.multiple_of(me * rows, 16), rows), :],
            local_sems.at[1 + at],
        )
        copy.start()
        mine.append(copy)

    rows_in = tokens_ref[...].astype(f32)
    scale = lax.rsqrt(jnp.mean(rows_in * rows_in, axis=1, keepdims=True) + norm_eps)
    normed_ref[...] = (rows_in * scale * gains_ref[...]).astype(bf16)

    swaps = []
    for j in others:
        fetched[j].wait_recv()
        where = block(partner(me, j), core)
        swaps.append(
            send(latent_w_ref.at[where, :], latent_w_ref.at[where, :], swap_sems, j - 1, sibling)
        )
    weights = fetch_weights()
    own.wait()
    for copy in swaps:
        copy.wait()
    for j in others:
        fetched[j].wait_send()
    latent = along(normed_ref[...], latent_w_ref[...])
    rows_ref[...] = latent

    def rms(values):
        return values * lax.rsqrt(jnp.mean(values * values, axis=1, keepdims=True) + norm_eps)

    query = rms(latent[:, :QR]) * latent_gains_ref[:, :QR]
    keyval = rms(latent[:, QR : QR + KR]) * latent_gains_ref[:, QR:]
    rope = latent[:, QR + KR :]
    wide = jnp.concatenate(
        [jnp.zeros((tokens, HD), f32), rope, jnp.zeros((tokens, LANES - HD - RD), f32)], axis=1
    )
    parts_ref[0, :, :QR] = query.astype(bf16)
    parts_ref[0, :, QR : QR + KR] = keyval.astype(bf16)
    parts_ref[0, :, QR + KR :] = turn(wide, table_ref, 1.0).astype(bf16)

    direct = (1, 2) if group == 4 else others
    near = [
        send(parts_ref.at[0], parts_ref.at[j], part_sems, j - 1, peers[j]) for j in direct
    ]
    swaps = swap_weights(weights)
    far = []
    if group == 4:
        part = tokens // 2
        top = pl.ds(0, part)
        low = pl.ds(part, part)
        near[0].wait_recv()
        far.append(send(parts_ref.at[1, top], parts_ref.at[3, top], part_sems, 2, peers[2]))
        near[1].wait_recv()
        far.append(send(parts_ref.at[2, low], parts_ref.at[3, low], part_sems, 3, peers[1]))
        for copy in near:
            copy.wait_send()
    else:
        for copy in near:
            copy.wait()
    for copy in far + swaps + mine:
        copy.wait()
    for copy in weights:
        copy.wait_send()


def latent_front(tokens, gain_in, latent_gains, table, latent_proj, query_pad, keyval, group):
    rows = tokens.shape[0]
    heads = query_pad.shape[1] // LANES // group
    bf16 = jnp.bfloat16
    others = group - 1
    dma = pltpu.SemaphoreType.DMA
    width = latent_proj.shape[1]
    return pl.pallas_call(
        functools.partial(latent_kernel, group),
        in_specs=[pl.BlockSpec(memory_space=pltpu.VMEM)] * 7,
        out_specs=[pl.BlockSpec(memory_space=pltpu.VMEM)] * 6,
        out_shape=[
            jax.ShapeDtypeStruct((group, rows, LATENT), bf16),
            jax.ShapeDtypeStruct((rows, width), jnp.float32),
            jax.ShapeDtypeStruct((rows, D), bf16),
            jax.ShapeDtypeStruct((D, width), bf16),
            jax.ShapeDtypeStruct((QR, heads * LANES), bf16),
            jax.ShapeDtypeStruct((KR, heads * LANES), bf16),
        ],
        scratch_shapes=[
            dma((3,)),
            dma((2, others)),
            dma((2, others)),
            dma((2, 2 * others)),
            dma((2, 2 * others)),
            dma((2, max(others, 4))),
        ],
        compiler_params=pltpu.CompilerParams(
            collective_id=2, has_side_effects=True, vmem_limit_bytes=VMEM_BYTES
        ),
        cost_estimate=pl.CostEstimate(
            flops=2 * rows * D * width, bytes_accessed=60_000_000, transcendentals=0
        ),
        name="latent_front",
    )(tokens, gain_in, latent_gains, table, latent_proj, query_pad, keyval)


def hop(array, group, distance):
    return lax.ppermute(array, "shard", [(i, i ^ distance) for i in range(group)])


def near_blocks(array, group):
    return [hop(array, group, j) for j in ((1, 2) if group == 4 else range(1, group))]


def all_blocks(array, near, group):
    if group != 4:
        return [array] + near
    half = array.shape[0] // 2
    far_top = hop(near[0][:half], group, 2)
    far_low = hop(near[1][half:], group, 1)
    return [array] + near + [jnp.concatenate([far_top, far_low], axis=0)]


def gather_blocks(array, group):
    return all_blocks(array, near_blocks(array, group), group)


def scatter_sum(parts, group):
    low = jnp.bfloat16
    f32 = jnp.float32
    total = parts[0].astype(f32)
    if group != 4:
        for j in range(1, group):
            total = total + hop(parts[j], group, j).astype(f32)
        return total
    half = parts[0].shape[0] // 2
    top = hop(parts[3][:half], group, 1)
    bottom = hop(parts[3][half:], group, 2)

    def add(left, right):
        return (left.astype(f32) + right.astype(f32)).astype(low)

    two = jnp.concatenate([add(parts[2][:half], top), parts[2][half:]], axis=0)
    one = jnp.concatenate([parts[1][:half], add(parts[1][half:], bottom)], axis=0)
    return total + hop(one, group, 1).astype(f32) + hop(two, group, 2).astype(f32)


def place(blocks, me):
    rows = blocks[0].shape[0]
    whole = jnp.zeros((rows * len(blocks),) + blocks[0].shape[1:], blocks[0].dtype)
    for j, block in enumerate(blocks):
        whole = lax.dynamic_update_slice_in_dim(whole, block, (me ^ j) * rows, 0)
    return whole


def pick(whole, me, group):
    rows = whole.shape[0] // group
    return [lax.dynamic_slice_in_dim(whole, (me ^ j) * rows, rows, 0) for j in range(group)]


def columns(array, index, width):
    return lax.dynamic_slice_in_dim(array, index * width, width, 1)


def per_device(
    group,
    replicas,
    tokens,
    segments,
    cotangent,
    latent_proj,
    query_up,
    keyval_up,
    out_proj,
    gate_up,
    down_proj,
    norm_gains,
    latent_mean,
    query_mean,
    keyval_mean,
    outproj_mean,
    gateup_mean,
    down_mean,
    gains_mean,
    latent_square,
    query_square,
    keyval_square,
    outproj_square,
    gateup_square,
    down_square,
    gains_square,
):
    f32 = jnp.float32
    bf16 = jnp.bfloat16
    me = lax.axis_index("shard")
    rep = lax.axis_index("rep")
    seq_len = tokens.shape[0]
    heads = H // group
    hidden_part = FF // group
    tiles = hidden_part // TILE
    tail = hidden_part - tiles * TILE
    rows_d = D // group
    others = range(1, group)
    order = jnp.stack([me ^ j for j in range(group)]).astype(jnp.int32)

    share = rows_d // replicas
    fast = group == 4 and share % 16 == 0
    gains_rows = jnp.broadcast_to(norm_gains.astype(f32), (8,) + norm_gains.shape)
    seg_rows = jnp.broadcast_to(segments.astype(f32), (8, seq_len))
    query_pad = jnp.pad(
        query_up.reshape(-1, H, HD + RD), ((0, 0), (0, 0), (0, LANES - HD - RD))
    ).reshape(-1, H * LANES)

    def hidden_columns(array, index):
        gate = columns(array, index, hidden_part)
        up = lax.dynamic_slice_in_dim(array, FF + index * hidden_part, hidden_part, 1)
        cut = []
        for t in range(tiles):
            cut += [gate[:, t * TILE : (t + 1) * TILE], up[:, t * TILE : (t + 1) * TILE]]
        for last in (gate, up):
            cut.append(jnp.pad(last[:, tiles * TILE :], ((0, 0), (0, TAIL - tail))))
        return jnp.concatenate(cut, axis=1)

    share = rows_d // replicas
    cot_near = near_blocks(cotangent, group)
    if share % 16 == 0:
        own_columns, pieces, gains_all, segs, tables = hidden_pieces(
            gate_up, gains_rows, seg_rows, group, replicas
        )
    else:
        gains_all, segs, tables = small_things(gains_rows, seg_rows, group)
        own_share = lax.dynamic_slice_in_dim(gate_up, rep * share, share, 0)
        own_columns = hidden_columns(gate_up, me)
        main = 2 * tiles * TILE
        pieces = [hop(hidden_columns(own_share, me ^ j), group, j) for j in others]
        pieces = jnp.concatenate(
            [piece[:, :main] for piece in pieces] + [piece[:, main:] for piece in pieces], axis=1
        )
    gathered_columns = lax.all_gather(pieces, "rep", axis=0, tiled=True)
    gains_f = gains_all.reshape(group, 8, -1)[:, 0, :].reshape(-1)
    gain_in = gains_f[:D]
    gain_query = gains_f[D : D + QR]
    gain_keyval = gains_f[D + QR : D + QR + KR]
    gain_mlp = gains_f[D + QR + KR :]

    latent_late, _ = lax.optimization_barrier((latent_proj, pieces))
    latent_parts, latent_all, normed_in, latent_w, query_w, keyval_w = latent_front(
        tokens,
        gain_in.reshape(1, D),
        gains_f[D : D + QR + KR].reshape(1, QR + KR),
        tables[0],
        latent_late,
        query_pad,
        keyval_up,
        group,
    )
    rows_in = tokens.astype(f32)
    inv_in = inverse_rms(rows_in)
    query_lat = latent_all[:, :QR]
    keyval_lat = latent_all[:, QR : QR + KR]
    inv_query = inverse_rms(query_lat)
    inv_keyval = inverse_rms(keyval_lat)

    attention = [None] * group
    latents_next = latent_parts
    for at, j in enumerate((*reversed(others), 0)):
        if at == 0:
            latents_next, cot_near = lax.optimization_barrier((latents_next, cot_near))
            cot_parts = all_blocks(cotangent, cot_near, group)
        if at == 1:
            latents_next, cot_parts = lax.optimization_barrier((latents_next, cot_parts))
        attention[j] = attend(j, latents_next, tables, segs, query_w, keyval_w, out_proj)
        latents_next, _ = lax.optimization_barrier((latent_parts, attention[j][0]))
    out_terms = [part[0] for part in attention]
    hidden = rows_in + residual_scale * scatter_sum(out_terms, group)
    inv_hidden = inverse_rms(hidden)
    normed_mlp = (hidden * inv_hidden * gain_mlp).astype(bf16)

    near = near_blocks(normed_mlp, group)
    half_tiles = tiles // 2
    if fast:
        mlp_parts = all_blocks(normed_mlp, near, group)

        def some_tiles(earlier, first, count):
            return layer_part(
                order,
                mlp_parts,
                cot_parts,
                own_columns,
                gathered_columns,
                down_proj,
                earlier,
                first,
                count,
                group,
                replicas,
            )

        early = some_tiles(None, 0, half_tiles)
        act_all, grad_late, back_all = some_tiles(early, half_tiles, tiles - half_tiles)
        cuts = [(0, half_tiles), (half_tiles, tiles)]
        grad_cuts = [early[1].reshape(D, -1), grad_late.reshape(D, -1)]
        hidden_terms = [back_all[j * seq_len : (j + 1) * seq_len] for j in range(group)]
    else:
        branch_parts = [(residual_scale * part.astype(f32)).astype(bf16) for part in cot_parts]

        def mlp_block(j, normed, earlier):
            return mlp_part(
                order,
                normed,
                branch_parts[j],
                own_columns,
                gathered_columns,
                down_proj,
                earlier,
                j,
                group,
            )

        first = mlp_block(0, normed_mlp, ())
        near, first = lax.optimization_barrier((near, first))
        mlp_parts = all_blocks(normed_mlp, near, group)
        terms = [first]
        for j in others:
            terms.append(mlp_block(j, mlp_parts[j], terms[-1][:2]))
        act_all, grad_all = terms[-1][:2]
        down_terms = [term[2] for term in terms]
        hidden_terms = [term[3] for term in terms]
        cuts = [(0, tiles)]
        grad_gateup = jnp.einsum(
            "td,tf->df", jnp.concatenate(mlp_parts), grad_all, preferred_element_type=f32
        )
        grad_cuts = [
            grad_gateup.astype(bf16)
            .reshape(group, replicas, share, -1)
            .transpose(1, 0, 2, 3)
            .reshape(D, -1)
        ]
    normed_late, _ = lax.optimization_barrier((normed_in, mlp_parts[1:]))
    normed_columns = [columns(normed_late, me, rows_d)] + [
        hop(columns(normed_late, me ^ j, rows_d), group, j) for j in others
    ]
    grad_normed_mlp = scatter_sum(hidden_terms, group)

    grad_down = down_grad(act_all, cot_parts, hidden_part, group)

    def to_owner_rows(block_rows):
        blocks = pick(block_rows, me, group)
        blocks = [blocks[0]] + [hop(blocks[j], group, j) for j in others]
        return place(blocks, me).reshape((group,) + blocks[0].shape)

    summed = [lax.psum_scatter(grad_cuts[0], "rep", scatter_dimension=0, tiled=True)]
    grad_normed_mlp, summed[0] = lax.optimization_barrier((grad_normed_mlp, summed[0]))
    for grad_cut in grad_cuts[1:]:
        grad_cut, _ = lax.optimization_barrier((grad_cut, summed[-1]))
        summed.append(lax.psum_scatter(grad_cut, "rep", scatter_dimension=0, tiled=True))
    grad_top = cotangent.astype(f32)
    grad_gain_mlp = jnp.sum(grad_normed_mlp * hidden * inv_hidden, axis=0)
    grad_hidden = grad_top + norm_back(grad_normed_mlp * gain_mlp, hidden, inv_hidden)
    grad_attn = (residual_scale * grad_hidden).astype(bf16)

    def back_block(j, grad):
        return attend_back(
            j,
            grad,
            attention[j][1],
            attention[j][2],
            latent_parts,
            tables,
            segs,
            query_w,
            keyval_w,
            out_proj,
        )

    near = near_blocks(grad_attn, group)
    back = [back_block(0, grad_attn)]
    near, back, grad_down = lax.optimization_barrier((near, back, grad_down))
    attn_parts = all_blocks(grad_attn, near, group)
    back += [back_block(j, attn_parts[j]) for j in others]

    def unpack(owned, q, second):
        pieces = []
        for (start, stop), rows in zip(cuts, owned):
            for t in range(stop - start):
                first = (2 * t + second) * TILE
                pieces.append(rows[q, :, first : first + TILE])
        first = 2 * (cuts[-1][1] - cuts[-1][0]) * TILE + second * TAIL
        return pieces + [owned[-1][q, :, first : first + tail]]

    def unpacked(owned):
        return jnp.concatenate(
            [piece for second in (0, 1) for q in range(group) for piece in unpack(owned, q, second)],
            axis=1,
        )

    latent_terms = [part[0] for part in back]
    grad_latent_low = scatter_sum(latent_terms, group)
    if fast:
        act_late, _ = lax.optimization_barrier((act_all, latent_terms))
        down_all = jnp.dot(
            act_late[:, :hidden_part], down_proj, preferred_element_type=f32
        ).astype(bf16)
        down_terms = [down_all[j * seq_len : (j + 1) * seq_len] for j in range(group)]
    grad_latent_low, down_terms = lax.optimization_barrier((grad_latent_low, down_terms))
    grad_down, _ = lax.optimization_barrier((grad_down, (summed[-1], grad_latent_low)))
    down_total = lax.psum_scatter(grad_down, "rep", scatter_dimension=0, tiled=True)
    grad_normed_query = grad_latent_low[:, :QR]
    grad_normed_keyval = grad_latent_low[:, QR : QR + KR]
    grad_key_rope = grad_latent_low[:, QR + KR + HD : QR + KR + HD + RD]
    grad_gain_query = jnp.sum(grad_normed_query * query_lat * inv_query, axis=0)
    grad_gain_keyval = jnp.sum(grad_normed_keyval * keyval_lat * inv_keyval, axis=0)
    grad_latent_rows = jnp.concatenate(
        [
            norm_back(grad_normed_query * gain_query, query_lat, inv_query),
            norm_back(grad_normed_keyval * gain_keyval, keyval_lat, inv_keyval),
            grad_key_rope,
        ],
        axis=1,
    ).astype(bf16)
    grad_latent_parts = gather_blocks(grad_latent_rows, group)
    first_rows, _ = lax.optimization_barrier((summed[0], grad_latent_low))
    owned = [to_owner_rows(rows) for rows in [first_rows] + summed[1:]]
    grad_latent_parts, owned = lax.optimization_barrier((grad_latent_parts, owned))
    gateup_total = unpacked(owned)
    mixed_late, late_query, late_keyval, _ = lax.optimization_barrier(
        (
            [part[3] for part in attention],
            [part[1] for part in back],
            [part[2] for part in back],
            grad_latent_rows,
        )
    )
    grad_out = token_grad(mixed_late, attn_parts, 0, heads * HD, "out_grad")
    grad_query = token_grad(latent_parts, late_query, 0, QR, "query_grad")
    grad_keyval = token_grad(latent_parts, late_keyval, QR, KR, "keyval_grad")
    query_rows = QR // (group * replicas)
    keyval_rows = KR // (group * replicas)
    unit = heads * LANES
    pair_rows = group * (query_rows + keyval_rows)
    out_units = D // unit
    out_count = heads * HD // replicas
    pair = (
        jnp.concatenate(
            [
                grad_query.reshape(group, replicas, query_rows, unit),
                grad_keyval.reshape(group, replicas, keyval_rows, unit),
            ],
            axis=2,
        )
        .transpose(1, 0, 2, 3)
        .reshape(replicas, pair_rows, unit)
    )
    grad_out = grad_out.reshape(replicas, out_count, D)
    grad_out = [grad_out[:, :, k * unit : (k + 1) * unit] for k in range(out_units)]

    grad_normed_in = jnp.einsum(
        "tc,dc->td", grad_latent_rows, latent_w, preferred_element_type=f32
    )
    grad_gain_in = jnp.sum(grad_normed_in * rows_in * inv_in, axis=0)
    input_grad = grad_hidden + norm_back(grad_normed_in * gain_in, rows_in, inv_in)
    grad_gains = jnp.concatenate([grad_gain_in, grad_gain_query, grad_gain_keyval, grad_gain_mlp])
    gain_blocks = pick(grad_gains, me, group)
    gains_sum = gain_blocks[0]
    for j in others:
        gains_sum = gains_sum + hop(gain_blocks[j].astype(bf16), group, j).astype(f32)
    grad_latent = jnp.einsum(
        "td,tc->dc",
        jnp.concatenate(normed_columns, axis=0),
        jnp.concatenate(grad_latent_parts, axis=0),
        preferred_element_type=f32,
    ).astype(bf16)
    width = grad_latent.shape[1]
    latent_units = -(-width // unit)
    grad_latent = jnp.pad(
        grad_latent.reshape(replicas, share, width), ((0, 0), (0, 0), (0, latent_units * unit - width))
    )
    grad_latent = [grad_latent[:, :, k * unit : (k + 1) * unit] for k in range(latent_units)]
    gains_row = gains_sum.reshape(replicas, 1, -1).astype(bf16)
    gains_row = jnp.pad(gains_row, ((0, 0), (0, 15), (0, unit - gains_row.shape[2])))
    last = jnp.concatenate([pair] + grad_out + grad_latent + [gains_row], axis=1)
    last, down_terms = lax.optimization_barrier((last, down_terms))
    block_out = (hidden + residual_scale * scatter_sum(down_terms, group)).astype(bf16)
    last, _ = lax.optimization_barrier((last.reshape(-1, unit), down_total))
    last = lax.psum_scatter(last, "rep", scatter_dimension=0, tiled=True)
    pair_own = to_owner_rows(last[:pair_rows])
    query_total = (
        pair_own[:, :query_rows]
        .reshape(group, query_rows, heads, LANES)[..., : HD + RD]
        .transpose(1, 0, 2, 3)
        .reshape(query_rows, H * (HD + RD))
    )
    keyval_total = pair_own[:, query_rows:].transpose(1, 0, 2).reshape(keyval_rows, 2 * H * HD)

    def side_by_side(first, count, pieces):
        return jnp.concatenate(
            [last[first + k * count : first + (k + 1) * count] for k in range(pieces)], axis=1
        )

    outproj_total = side_by_side(pair_rows, out_count, out_units)
    latent_at = pair_rows + out_units * out_count
    latent_total = side_by_side(latent_at, share, latent_units)[:, :width]
    gains_total = last[latent_at + latent_units * share, : gains_mean.shape[0]]

    updates = [
        adam_step(latent_proj, latent_total, latent_mean, latent_square, D ** (-0.5), decay_rate),
        adam_step(query_up, query_total, query_mean, query_square, QR ** (-0.5), decay_rate),
        adam_step(keyval_up, keyval_total, keyval_mean, keyval_square, KR ** (-0.5), decay_rate),
        adam_step(
            out_proj,
            outproj_total,
            outproj_mean,
            outproj_square,
            max(H * HD // 512, 1) ** (-0.5),
            decay_rate,
        ),
        adam_step(gate_up, gateup_total, gateup_mean, gateup_square, D ** (-0.5), decay_rate),
        adam_step(
            down_proj, down_total, down_mean, down_square, max(FF // 32, 1) ** (-0.5), decay_rate
        ),
        adam_step(norm_gains, gains_total, gains_mean, gains_square, gain_rate, 0.0),
    ]
    return (block_out, input_grad) + tuple(value for update in updates for value in update)


def solution(mesh):
    return jax.shard_map(
        functools.partial(per_device, mesh.shape["shard"], mesh.shape["rep"]),
        mesh=mesh,
        in_specs=(
            P(("shard", "rep"), None),
            P(("shard", "rep"), None),
            P(("shard", "rep"), None),
            P("shard", None),
            P("shard", None),
            P("shard", None),
            P("shard", None),
            P("shard", None),
            P("shard", None),
            P("shard"),
            P(("shard", "rep"), None),
            P(("shard", "rep"), None),
            P(("shard", "rep"), None),
            P(("shard", "rep"), None),
            P(("shard", "rep"), None),
            P(("shard", "rep"), None),
            P(("shard", "rep")),
            P(("shard", "rep"), None),
            P(("shard", "rep"), None),
            P(("shard", "rep"), None),
            P(("shard", "rep"), None),
            P(("shard", "rep"), None),
            P(("shard", "rep"), None),
            P(("shard", "rep")),
        ),
        out_specs=(
            P(("shard", "rep"), None),
            P(("shard", "rep"), None),
            P(("shard", "rep"), None),
            P(("shard", "rep"), None),
            P(("shard", "rep"), None),
            P(("shard", "rep"), None),
            P(("shard", "rep"), None),
            P(("shard", "rep"), None),
            P(("shard", "rep"), None),
            P(("shard", "rep"), None),
            P(("shard", "rep"), None),
            P(("shard", "rep"), None),
            P(("shard", "rep"), None),
            P(("shard", "rep"), None),
            P(("shard", "rep"), None),
            P(("shard", "rep"), None),
            P(("shard", "rep"), None),
            P(("shard", "rep"), None),
            P(("shard", "rep"), None),
            P(("shard", "rep"), None),
            P(("shard", "rep")),
            P(("shard", "rep")),
            P(("shard", "rep")),
        ),
        check_vma=False,
    )
```
